32 devices in a mesh: parts: 2 (over y), space: 16 (over z, x, core).
Axes of the slice: x: 2, y: 2, z: 4, core: 2. Of those that a mesh axis runs over, the one named last changes fastest.
Arguments:
- counts: int32 [32], P(('parts', 'space')), parts along dimension 0, may hold values from 1 to 12, as said below
- points: float32 [384, 3, 256], P(('parts', 'space')), parts along dimension 0
- weights: float32 [384, 256], P(('parts', 'space')), parts along dimension 0, may hold values from 0.001953125 to 0.0078125
- block_lists: int32 [384, 8], P(('parts', 'space')), parts along dimension 0, may hold values from 0 to 127, as said below
- pattern: int32 [256, 4], P(('parts', 'space')), parts along dimension 0, may hold values from 0 to 127, as said below
- basis_table: bfloat16 [256, 4, 128], P(('parts', 'space')), parts along dimension 0
- density: bfloat16 [256, 4, 128, 128], P(('parts', 'space')), parts along dimension 0
Outputs:
- xc_matrix: float32 [256, 4, 128, 128], P(('parts', 'space')), parts along dimension 0
The draws below stay inside these ranges and needn't reach their ends.
There are 2 independent parts, one for each index of `parts`. The reference program is written for one: setup_inputs(seed, part) draws one part's arguments, and reference() takes and returns one part's arrays. A program takes and returns all parts, laid end to end along the dimension named above; each array names one. Nothing has to cross between parts.
Inputs may be any that keep to these rules, and one draw needn't show every extreme that they name: `block_lists`: each batch's list holds 8 distinct block rows, all owned by the batch's own device along space or its two neighbours. `pattern`: entry 0 of each row is the row itself; the others are distinct rows within 3 of it. `counts`: slots 0 to count - 1 of a device are its live batches; some device has all 12 live.
All inputs are finite; a program needn't handle non-finite values.
Results may differ from the reference program's by a relative error of at most 0.0004.
Values may be sent and summed in bfloat16 or wider, within the bound.
No kernel may reach another device: no remote copies, remote signals or barrier semaphores. Data moves between devices by JAX's collectives and lax.ppermute only.
A program may use at most 64 MiB of HBM per device.

```python
import math
import jax
import jax.numpy as jnp
from jax import lax

B = 128
LB = 8
K = 4
PTS = 256
NBLK_DEV = 8
BATCH_DEV = 12
NBLK = 128
NBATCH = 192


def home_blocks(key):
    inner = jax.random.randint(jax.random.fold_in(key, 101), (NBATCH,), 0, NBLK_DEV)
    order = jnp.arange(NBATCH, dtype=jnp.int32)
    inner = jnp.where(order % BATCH_DEV == 0, NBLK_DEV - 1, inner)
    return order // BATCH_DEV * NBLK_DEV + inner


def draw_counts(key, part):
    key = jax.random.fold_in(key, 4)
    devices = NBATCH // BATCH_DEV
    first_key, second_key, third_key = jax.random.split(key, 3)
    first_draw = jax.random.randint(first_key, (devices,), 1, BATCH_DEV + 1)
    second_draw = jax.random.randint(second_key, (devices,), 1, BATCH_DEV + 1)
    loads = jnp.minimum(first_draw, second_draw)
    forced = jax.random.randint(third_key, (), 0, devices)
    return jnp.where(jnp.arange(devices) == forced, BATCH_DEV, loads).astype(jnp.int32)


def draw_points(key, part):
    home = home_blocks(key)
    key = jax.random.fold_in(key, 3)
    values = jax.random.uniform(key, (NBATCH, 3, PTS), jnp.float32)
    along = values[:, 0, :]
    first_axis = home[:, None].astype(jnp.float32) + along
    return jnp.stack([first_axis, 2.0 * values[:, 1, :], 2.0 * values[:, 2, :]], axis=1)


def draw_block_lists(key, part):
    home = home_blocks(key)
    key = jax.random.fold_in(key, 2)
    span = 2 * NBLK_DEV
    begin = jnp.clip(home - NBLK_DEV, 0, NBLK - span)
    scores = jax.random.randint(key, (NBATCH, span), 0, 2 ** 20) * span + jnp.arange(span, dtype=jnp.int32)[None, :]
    row_index = jnp.arange(NBATCH, dtype=jnp.int32)[:, None]
    column_index = jnp.arange(span, dtype=jnp.int32)[None, :]
    forced_top = (row_index == NBATCH - 1) & (column_index == span - 1)
    forced_bottom = (row_index == 0) & (column_index == 0)
    target = home[:, None] + 1 - begin[:, None]
    forced_reach = (row_index % BATCH_DEV == 0) & (column_index == target)
    scores = scores - jnp.where(forced_top | forced_bottom | forced_reach, 2 ** 28, 0)
    chosen = jnp.argsort(scores, axis=1, stable=True)[:, :LB]
    return (begin[:, None] + chosen).astype(jnp.int32)


def draw_pattern(key, part):
    key = jax.random.fold_in(key, 5)
    offsets = jnp.array([-3, -2, -1, 1, 2, 3], dtype=jnp.int32)
    rows = jnp.arange(NBLK, dtype=jnp.int32)
    candidates = rows[:, None] + offsets[None, :]
    valid = (candidates >= 0) & (candidates < NBLK)
    scores = jax.random.randint(key, (NBLK, 6), 0, 2 ** 20) * 8 + jnp.arange(6, dtype=jnp.int32)[None, :]
    scores = scores + jnp.where(valid, 0, 2 ** 26)
    chosen = jnp.argsort(scores, axis=1, stable=True)[:, :K - 1]
    others = jnp.take_along_axis(candidates, chosen, axis=1)
    return jnp.concatenate([rows[:, None], others], axis=1).astype(jnp.int32)


def draw_basis_table(key, part):
    key = jax.random.fold_in(key, 6)
    values = jax.random.uniform(key, (NBLK, 4, B), jnp.float32)
    rate = values[:, 3, :]
    exponent = jnp.exp(jnp.log(0.05) + rate * (jnp.log(0.5) - jnp.log(0.05)))
    table = jnp.stack([values[:, 0, :], 2.0 * values[:, 1, :], 2.0 * values[:, 2, :], exponent], axis=1)
    return table.astype(jnp.bfloat16)


def draw_density(key, part):
    key = jax.random.fold_in(key, 7)
    first_key, second_key, third_key = jax.random.split(key, 3)
    raw = jax.random.uniform(first_key, (NBLK, B, B), jnp.float32, -1.0, 1.0)
    diagonal = jax.random.uniform(second_key, (NBLK, B), jnp.float32)
    spread = jax.random.uniform(third_key, (NBLK, K, B, B), jnp.float32)
    factor = raw * (3.0 / B) ** 0.5
    product = jnp.einsum('nij,nkj->nik', factor, factor, precision=lax.Precision.HIGHEST)
    identity = (jnp.arange(B)[:, None] == jnp.arange(B)[None, :]).astype(jnp.float32)
    lead = (1.0 + diagonal)[:, :, None] * identity[None, :, :] + product
    positive = 1.5 / B * spread
    blocks = positive.at[:, 0].add(lead)
    return blocks.astype(jnp.bfloat16)


def level_of(stream_key, extent, shards, smallest, top_value):
    loudness = 1.0
    for dim, parts in shards:
        draws = jax.random.uniform(jax.random.fold_in(jax.random.fold_in(stream_key, 6), dim), (parts,), jnp.float32, smallest / len(shards), top_value / len(shards))
        loudness = loudness * jnp.repeat(jnp.exp(draws), extent[dim] // parts).reshape((-1,) + (1,) * (len(extent) - 1 - dim))
    return loudness


def setup_inputs(seed: int = 0, part: int = 0) -> dict:
    splits = jax.random.split(jax.random.key(seed), 8)
    own_keys = jax.random.split(jax.random.fold_in(splits[7], part), 8)
    counts = draw_counts(jax.random.fold_in(jax.random.fold_in(splits[7], part), 71), part)
    points = draw_points(jax.random.fold_in(jax.random.fold_in(splits[7], part), 71), part)
    weights = jnp.clip(jnp.exp(math.log(0.0078125) - 1.3862944 * jax.random.uniform(own_keys[2], (NBATCH, PTS), jnp.float32) ** level_of(own_keys[2], (NBATCH, PTS), ((0, 16),), -0.2, 0.2)), 0.001953125, 0.0078125)
    block_lists = draw_block_lists(jax.random.fold_in(jax.random.fold_in(splits[7], part), 71), part)
    pattern = draw_pattern(jax.random.fold_in(jax.random.fold_in(splits[7], part), 71), part)
    basis_table = draw_basis_table(jax.random.fold_in(jax.random.fold_in(splits[7], part), 71), part)
    density = draw_density(jax.random.fold_in(jax.random.fold_in(splits[7], part), 71), part)
    return dict(counts=counts, points=points, weights=weights, block_lists=block_lists, pattern=pattern, basis_table=basis_table, density=density)


exchange_coef = (3.0 / math.pi) ** (1.0 / 3.0)


def batch_terms(points_one, weights_one, block_list, window_start, window_density, window_pattern, window_basis):
    window_rows = (block_list - window_start).astype(jnp.int32)
    parameters = window_basis[window_rows].astype(jnp.float32)
    centre_first = parameters[:, 0, :] + block_list[:, None].astype(jnp.float32)
    distance = (points_one[0][None, :, None] - centre_first[:, None, :]) ** 2
    distance = distance + (points_one[1][None, :, None] - parameters[:, 1, :][:, None, :]) ** 2
    distance = distance + (points_one[2][None, :, None] - parameters[:, 2, :][:, None, :]) ** 2
    orbitals = jnp.exp(-parameters[:, 3, :][:, None, :] * distance).astype(jnp.bfloat16)
    orbital_wide = orbitals.astype(jnp.float32)
    matches = (window_pattern[window_rows][:, :, None] == block_list[None, None, :]).astype(jnp.float32)
    partners = jnp.einsum("akb,brj->akrj", matches, orbital_wide).astype(jnp.bfloat16)
    partner_wide = partners.astype(jnp.float32)
    stored = window_density[window_rows].astype(jnp.float32)
    folded = jnp.einsum("akrj,akij->ari", partner_wide, stored)
    density_values = jnp.sum(orbital_wide * folded, axis=(0, 2))
    potential = -exchange_coef * jnp.cbrt(density_values) * weights_one
    weighted = (orbital_wide * potential[None, :, None]).astype(jnp.bfloat16)
    contrib = jnp.einsum("ari,akrj->akij", weighted.astype(jnp.float32), partner_wide)
    return window_rows, contrib


def reference(counts, points, weights, block_lists, pattern, basis_table, density):
    batches = points.shape[0]
    batch_order = jnp.arange(batches, dtype=jnp.int32)
    living_mask = (batch_order % BATCH_DEV) < counts[batch_order // BATCH_DEV]

    def visit(totals, scanned):
        points_one, weights_one, block_list, living = scanned

        def include(held):
            window_rows, contrib = batch_terms(points_one, weights_one, block_list, 0, density, pattern, basis_table)
            return held.at[window_rows].add(contrib)

        return lax.cond(living, include, lambda held: held, totals), None

    totals, unused = lax.scan(visit, jnp.zeros(density.shape, jnp.float32), (points, weights, block_lists, living_mask))
    return totals
```

```python
import functools
import math

import jax
import jax.numpy as jnp
from jax import lax
from jax.experimental import pallas as pl
from jax.experimental.pallas import tpu as pltpu
from jax.sharding import PartitionSpec as P

exchange_coef = (3.0 / math.pi) ** (1.0 / 3.0)
VMEM = pltpu.VMEM
SMEM = pltpu.SMEM
LIMIT = 28 << 20
REACH = 3
UNROLL = 4


class Layout:
    def __init__(self, batches, listed, points, rows, partners, orbitals):
        self.batches, self.listed, self.points = batches, listed, points
        self.rows, self.partners, self.orbitals = rows, partners, orbitals
        self.weights = -(-3 * batches // 8) * 8
        self.basis = self.weights + -(-batches // 8) * 8
        self.lists = 0
        self.pattern = -(-batches // 8) * 8
        self.meta = self.pattern + rows
        self.scalar_rows = -(-max(4 * rows, self.meta + 1) // 8) * 8
        self.height = self.basis + self.scalar_rows
        self.slots = 3 * batches * listed
        self.blank = self.slots
        self.work_kept = partners * (self.slots + 1)
        self.work_row = self.work_kept
        self.work_first = self.work_row + self.slots + 1
        self.work_second = self.work_first + self.slots + UNROLL
        self.work_counts = self.work_second + self.slots + UNROLL
        self.work = -(-(self.work_counts + 2) // 128) * 128


def pack_kernel(lay, me, counts, points, weights, lists, pattern, basis, out):
    out[...] = jnp.zeros_like(out)
    for t in range(lay.batches):
        out[3 * t : 3 * t + 3, :] = points[t]
    out[lay.weights : lay.weights + lay.batches, :] = weights[...]
    for w in range(lay.rows):
        out[lay.basis + 4 * w : lay.basis + 4 * w + 4, :128] = basis[w].astype(jnp.float32)
    begin = lay.basis + lay.lists
    out[begin : begin + lay.batches, 128 : 128 + lay.listed] = lists[...].astype(jnp.float32)
    begin = lay.basis + lay.pattern
    out[begin : begin + lay.rows, 128 : 128 + lay.partners] = pattern[...].astype(jnp.float32)
    begin = lay.basis + lay.meta
    lane = lax.broadcasted_iota(jnp.int32, (1, 128), 1)
    meta = jnp.where(lane == 0, counts[0], jnp.where(lane == 1, me[0], 0))
    out[begin : begin + 1, 128:256] = meta.astype(jnp.float32)


def first_kernel(
    lay,
    pack_own,
    pack_pair,
    pack_far,
    density_own,
    density_pair,
    part,
    orb,
    work,
    columns,
    density,
    rho,
    scalars,
    window_pattern,
    place,
    needed,
    scalar_sems,
    density_sems,
):
    packs = (pack_own, pack_pair, pack_far)
    rows, listed = lay.rows, lay.listed
    scalar_copies = [
        pltpu.make_async_copy(
            packs[g].at[pl.ds(lay.basis, lay.scalar_rows), pl.ds(128, 128)],
            scalars.at[g],
            scalar_sems.at[g],
        )
        for g in range(3)
    ]
    for copy in scalar_copies:
        copy.start()
    density_copies = [
        pltpu.make_async_copy(
            source, density.at[pl.ds(g * rows, rows)], density_sems.at[g]
        )
        for g, source in enumerate((density_own, density_pair))
    ]
    for copy in density_copies:
        copy.start()
    orb[lay.blank] = jnp.zeros(orb.shape[1:], orb.dtype)
    rho[...] = jnp.zeros_like(rho)
    for copy in scalar_copies:
        copy.wait()

    def whole(g, row, lane):
        return scalars[g, row, lane].astype(jnp.int32)

    ids = [whole(g, lay.meta, 1) for g in range(3)]
    own_start = ids[0] * rows

    for g in range(3):
        table = packs[g][lay.basis : lay.basis + 4 * rows, :128].T
        start = (ids[g] * rows).astype(jnp.float32)
        for w in range(rows):
            for c in range(4):
                column = table[:, 4 * w + c : 4 * w + c + 1]
                if c == 0:
                    column = column + (start + float(w))
                if c == 3:
                    column = -column
                columns[g * rows + w, c] = jnp.broadcast_to(column, (lay.orbitals, 128))

    def window(row):
        owner = row // rows
        inner = row - owner * rows
        outside = jnp.where(owner == ids[2], 2 * rows + inner, 3 * rows)
        return jnp.where(
            owner == ids[0], inner, jnp.where(owner == ids[1], rows + inner, outside)
        )

    for g in range(2):
        for w in range(rows):
            for k in range(lay.partners):
                window_pattern[(g * rows + w) * lay.partners + k] = window(
                    whole(g, lay.pattern + w, k)
                )
    for w in range(3 * rows + 1):
        place[w] = -1
    for k in range(lay.partners):
        work[lay.blank * lay.partners + k] = lay.blank
    work[lay.work_row + lay.blank] = 0

    def batch(g, t, totals):
        first_total, second_total = totals
        number = g * lay.batches + t
        base = number * listed
        total = jnp.int32(0)
        places = []
        for b in range(listed):
            row = whole(g, lay.lists + t, b)
            w = window(row)
            place[w] = base + b
            near = (row >= own_start - REACH) & (row < own_start + rows + REACH)
            wanted = (near | (w < 2 * rows)) if g == 0 else near
            needed[total] = w * listed + b
            total = total + jnp.where(wanted, 1, 0)
            places.append(w)
        place[3 * rows] = -1
        for b in range(listed):
            w = places[b]
            slot = base + b
            safe = jnp.minimum(w, 2 * rows - 1)
            for k in range(lay.partners):
                held = place[window_pattern[safe * lay.partners + k]]
                work[slot * lay.partners + k] = jnp.where(held >= base, held, lay.blank)
            work[lay.work_row + slot] = w
            if g != 1:
                work[lay.work_first + first_total] = slot
                limit = 2 * rows if g == 0 else rows
                first_total = first_total + jnp.where(w < limit, 1, 0)
            work[lay.work_second + second_total] = slot
            second_total = second_total + jnp.where(w < rows, 1, 0)

        at = [packs[g][pl.ds(3 * t + c, 1), :] for c in range(3)]

        def orbital(index, carry):
            coded = needed[index]
            w = coded // listed
            slot = base + coded - w * listed
            for begin in range(0, lay.orbitals, 32):
                some = pl.ds(begin, 32)
                centre = [columns[w, c, some, :] for c in range(4)]
                for half in range(0, lay.points, 128):
                    distance = (at[0][:, half : half + 128] - centre[0]) ** 2
                    distance = distance + (at[1][:, half : half + 128] - centre[1]) ** 2
                    distance = distance + (at[2][:, half : half + 128] - centre[2]) ** 2
                    value = jnp.exp(centre[3] * distance)
                    orb[slot, some, half : half + 128] = value.astype(jnp.bfloat16)
            return carry

        lax.fori_loop(0, total, orbital, 0)
        return (first_total, second_total)

    totals = (jnp.int32(0), jnp.int32(0))
    for g in range(3):
        live = jnp.minimum(whole(g, lay.meta, 0), lay.batches)
        totals = lax.fori_loop(0, live, functools.partial(batch, g), totals)
    first_total, second_total = totals
    for u in range(UNROLL):
        work[lay.work_first + first_total + u] = lay.blank
        work[lay.work_second + second_total + u] = lay.blank
    work[lay.work_counts] = first_total
    work[lay.work_counts + 1] = second_total
    for copy in density_copies:
        copy.wait()

    def fold(step, carry):
        sums = []
        for u in range(UNROLL):
            slot = work[lay.work_first + step * UNROLL + u]
            row = work[lay.work_row + slot]
            others = jnp.concatenate(
                [orb[work[slot * lay.partners + k]] for k in range(lay.partners)], axis=0
            )
            stored = jnp.concatenate([density[row, k] for k in range(lay.partners)], axis=1)
            folded = jnp.dot(stored, others, preferred_element_type=jnp.float32)
            product = orb[slot].astype(jnp.float32) * folded
            total = product[0:8]
            for begin in range(8, lay.orbitals, 8):
                total = total + product[begin : begin + 8]
            sums.append((slot // listed, total))
        for number, total in sums:
            rho[number] = rho[number] + total
        return carry

    lax.fori_loop(0, (first_total + UNROLL - 1) // UNROLL, fold, 0)
    part[: lay.batches, :] = jnp.sum(rho[: lay.batches], axis=1)
    part[lay.batches :, :] = jnp.sum(rho[2 * lay.batches : 3 * lay.batches], axis=1)


def cube_root(x):
    size = jnp.abs(x)
    safe = jnp.where(size > 0.0, size, 1.0)
    root = jnp.exp2(jnp.log2(safe) * (1.0 / 3.0))
    root = root - (root - safe / (root * root)) * (1.0 / 3.0)
    root = jnp.where(size > 0.0, root, 0.0)
    return jnp.where(x < 0.0, -root, root)


def second_kernel(lay, pack_own, pack_pair, pack_far, part, arrived, pair_rho, orb, work, out, potential):
    packs = (pack_own, pack_pair, pack_far)
    n = lay.batches
    density_values = (part[:n] + arrived[n:], pair_rho[...], part[n:] + arrived[:n])
    potential[...] = jnp.zeros_like(potential)
    for g in range(3):
        weights = packs[g][lay.weights : lay.weights + n, :]
        potential[g * n : (g + 1) * n, :] = -exchange_coef * cube_root(density_values[g]) * weights
    out[...] = jnp.zeros_like(out)

    def contribute(step, carry):
        for u in range(UNROLL):
            slot = work[lay.work_second + step * UNROLL + u]
            row = work[lay.work_row + slot]
            others = jnp.concatenate(
                [orb[work[slot * lay.partners + k]] for k in range(lay.partners)], axis=0
            )
            scale = potential[pl.ds(slot // lay.listed, 1), :]
            weighted = (orb[slot].astype(jnp.float32) * scale).astype(jnp.bfloat16)
            contrib = lax.dot_general(
                weighted, others, (((1,), (1,)), ((), ())), preferred_element_type=jnp.float32
            )
            for k in range(lay.partners):
                begin = k * lay.orbitals
                out[row, k] += contrib[:, begin : begin + lay.orbitals]
        return carry

    total = work[lay.work_counts + 1]
    lax.fori_loop(0, (total + UNROLL - 1) // UNROLL, contribute, 0)


def on_device(counts, points, weights, block_lists, pattern, basis_table, density):
    batches, listed = block_lists.shape
    rows, partners = pattern.shape
    orbitals = basis_table.shape[2]
    lay = Layout(batches, listed, points.shape[2], rows, partners, orbitals)
    devices = lax.axis_size("space")
    me = lax.axis_index("space").astype(jnp.int32).reshape(1)
    in_vmem = pl.BlockSpec(memory_space=VMEM)
    in_smem = pl.BlockSpec(memory_space=SMEM)
    anywhere = pl.BlockSpec(memory_space=pl.ANY)
    params = pltpu.CompilerParams(vmem_limit_bytes=LIMIT)
    pair_route = [(i, i ^ 1) for i in range(devices)]
    far_route = [
        (i, i + 1 if i % 2 else i - 1)
        for i in range(devices)
        if 0 <= (i + 1 if i % 2 else i - 1) < devices
    ]

    pack = pl.pallas_call(
        functools.partial(pack_kernel, lay),
        out_shape=jax.ShapeDtypeStruct((lay.height, lay.points), jnp.float32),
        in_specs=[in_smem, in_smem] + [in_vmem] * 5,
        out_specs=in_vmem,
        compiler_params=params,
        name="pack",
    )(me, counts, points, weights, block_lists, pattern, basis_table)
    pack_far = lax.ppermute(pack, "space", far_route)
    pack_pair = lax.ppermute(pack, "space", pair_route)
    density_pair = lax.ppermute(density, "space", pair_route)

    part, orb, work = pl.pallas_call(
        functools.partial(first_kernel, lay),
        out_shape=(
            jax.ShapeDtypeStruct((2 * batches, lay.points), jnp.float32),
            jax.ShapeDtypeStruct((lay.slots + 1, orbitals, lay.points), jnp.bfloat16),
            jax.ShapeDtypeStruct((lay.work,), jnp.int32),
        ),
        in_specs=[in_vmem] * 3 + [anywhere] * 2,
        out_specs=(in_vmem, in_vmem, in_smem),
        scratch_shapes=[
            VMEM((3 * rows, 4, orbitals, 128), jnp.float32),
            VMEM((2 * rows, partners, orbitals, orbitals), jnp.bfloat16),
            VMEM((3 * batches + 1, 8, lay.points), jnp.float32),
            SMEM((3, lay.scalar_rows, 128), jnp.float32),
            SMEM((2 * rows * partners,), jnp.int32),
            SMEM((3 * rows + 1,), jnp.int32),
            SMEM((listed + 1,), jnp.int32),
            pltpu.SemaphoreType.DMA((3,)),
            pltpu.SemaphoreType.DMA((2,)),
        ],
        compiler_params=params,
        name="first",
    )(pack, pack_pair, pack_far, density, density_pair)

    arrived = lax.ppermute(part, "space", far_route)
    own_rho = part[:batches] + arrived[batches:]
    pair_rho = lax.ppermute(own_rho, "space", pair_route)

    return pl.pallas_call(
        functools.partial(second_kernel, lay),
        out_shape=jax.ShapeDtypeStruct(density.shape, jnp.float32),
        in_specs=[in_vmem] * 7 + [in_smem],
        out_specs=in_vmem,
        scratch_shapes=[VMEM((-(-(3 * batches + 1) // 8) * 8, lay.points), jnp.float32)],
        compiler_params=params,
        name="second",
    )(pack, pack_pair, pack_far, part, arrived, pair_rho, orb, work)


def solution(mesh):
    in_specs = (
        P(("parts", "space")),
        P(("parts", "space"), None, None),
        P(("parts", "space"), None),
        P(("parts", "space"), None),
        P(("parts", "space"), None),
        P(("parts", "space"), None, None),
        P(("parts", "space"), None, None, None),
    )
    out_specs = P(("parts", "space"), None, None, None)
    return jax.shard_map(
        on_device, mesh=mesh, in_specs=in_specs, out_specs=out_specs, check_vma=False
    )
```

```python
import functools
import math

import jax
import jax.numpy as jnp
from jax import lax
from jax.experimental import pallas as pl
from jax.experimental.pallas import tpu as pltpu
from jax.sharding import PartitionSpec as P

exchange_coef = (3.0 / math.pi) ** (1.0 / 3.0)
VMEM = pltpu.VMEM
SMEM = pltpu.SMEM
LIMIT = 12 << 20
REACH = 3
UNROLL = 4


class Layout:
    def __init__(self, batches, listed, points, rows, partners, orbitals):
        self.batches, self.listed, self.points = batches, listed, points
        self.rows, self.partners, self.orbitals = rows, partners, orbitals
        self.weights = -(-3 * batches // 8) * 8
        self.basis = self.weights + -(-batches // 8) * 8
        self.lists = 0
        self.pattern = -(-batches // 8) * 8
        self.meta = self.pattern + rows
        self.scalar_rows = -(-max(4 * rows, self.meta + 1) // 8) * 8
        self.height = self.basis + self.scalar_rows
        self.slots = 3 * batches * listed
        self.blank = self.slots
        self.work_kept = partners * (self.slots + 1)
        self.work_row = self.work_kept
        self.work_first = self.work_row + self.slots + 1
        self.work_second = self.work_first + self.slots + UNROLL
        self.work_counts = self.work_second + self.slots + UNROLL
        self.work = -(-(self.work_counts + 2) // 128) * 128


def pack_kernel(lay, me, counts, points, weights, lists, pattern, basis, out):
    out[...] = jnp.zeros_like(out)
    for t in range(lay.batches):
        out[3 * t : 3 * t + 3, :] = points[t]
    out[lay.weights : lay.weights + lay.batches, :] = weights[...]
    for w in range(lay.rows):
        out[lay.basis + 4 * w : lay.basis + 4 * w + 4, :128] = basis[w].astype(jnp.float32)
    begin = lay.basis + lay.lists
    out[begin : begin + lay.batches, 128 : 128 + lay.listed] = lists[...].astype(jnp.float32)
    begin = lay.basis + lay.pattern
    out[begin : begin + lay.rows, 128 : 128 + lay.partners] = pattern[...].astype(jnp.float32)
    begin = lay.basis + lay.meta
    lane = lax.broadcasted_iota(jnp.int32, (1, 128), 1)
    meta = jnp.where(lane == 0, counts[0], jnp.where(lane == 1, me[0], 0))
    out[begin : begin + 1, 128:256] = meta.astype(jnp.float32)


def first_kernel(
    lay,
    pack_own,
    pack_pair,
    pack_far,
    density_own,
    density_pair,
    part,
    orb,
    work,
    columns,
    density,
    rho,
    scalars,
    window_pattern,
    place,
    needed,
    scalar_sems,
    density_sems,
):
    packs = (pack_own, pack_pair, pack_far)
    rows, listed = lay.rows, lay.listed
    scalar_copies = [
        pltpu.make_async_copy(
            packs[g].at[pl.ds(lay.basis, lay.scalar_rows), pl.ds(128, 128)],
            scalars.at[g],
            scalar_sems.at[g],
        )
        for g in range(3)
    ]
    for copy in scalar_copies:
        copy.start()
    density_copies = [
        pltpu.make_async_copy(
            source, density.at[pl.ds(g * rows, rows)], density_sems.at[g]
        )
        for g, source in enumerate((density_own, density_pair))
    ]
    for copy in density_copies:
        copy.start()
    orb[lay.blank] = jnp.zeros(orb.shape[1:], orb.dtype)
    rho[...] = jnp.zeros_like(rho)
    for copy in scalar_copies:
        copy.wait()

    def whole(g, row, lane):
        return scalars[g, row, lane].astype(jnp.int32)

    ids = [whole(g, lay.meta, 1) for g in range(3)]
    own_start = ids[0] * rows

    for g in range(3):
        table = packs[g][lay.basis : lay.basis + 4 * rows, :128].T
        start = (ids[g] * rows).astype(jnp.float32)
        for w in range(rows):
            for c in range(4):
                column = table[:, 4 * w + c : 4 * w + c + 1]
                if c == 0:
                    column = column + (start + float(w))
                if c == 3:
                    column = -column
                columns[g * rows + w, c] = jnp.broadcast_to(column, (lay.orbitals, 128))

    def window(row):
        owner = row // rows
        inner = row - owner * rows
        outside = jnp.where(owner == ids[2], 2 * rows + inner, 3 * rows)
        return jnp.where(
            owner == ids[0], inner, jnp.where(owner == ids[1], rows + inner, outside)
        )

    for g in range(2):
        for w in range(rows):
            for k in range(lay.partners):
                window_pattern[(g * rows + w) * lay.partners + k] = window(
                    whole(g, lay.pattern + w, k)
                )
    for w in range(3 * rows + 1):
        place[w] = -1
    for k in range(lay.partners):
        work[lay.blank * lay.partners + k] = lay.blank
    work[lay.work_row + lay.blank] = 0

    def batch(g, t, totals):
        first_total, second_total = totals
        number = g * lay.batches + t
        base = number * listed
        total = jnp.int32(0)
        places = []
        for b in range(listed):
            row = whole(g, lay.lists + t, b)
            w = window(row)
            place[w] = base + b
            near = (row >= own_start - REACH) & (row < own_start + rows + REACH)
            wanted = (near | (w < 2 * rows)) if g == 0 else near
            needed[total] = w * listed + b
            total = total + jnp.where(wanted, 1, 0)
            places.append(w)
        place[3 * rows] = -1
        for b in range(listed):
            w = places[b]
            slot = base + b
            safe = jnp.minimum(w, 2 * rows - 1)
            for k in range(lay.partners):
                held = place[window_pattern[safe * lay.partners + k]]
                work[slot * lay.partners + k] = jnp.where(held >= base, held, lay.blank)
            work[lay.work_row + slot] = w
            if g != 1:
                work[lay.work_first + first_total] = slot
                limit = 2 * rows if g == 0 else rows
                first_total = first_total + jnp.where(w < limit, 1, 0)
            work[lay.work_second + second_total] = slot
            second_total = second_total + jnp.where(w < rows, 1, 0)

        at = [packs[g][pl.ds(3 * t + c, 1), :] for c in range(3)]

        def orbital(index, carry):
            coded = needed[index]
            w = coded // listed
            slot = base + coded - w * listed
            for begin in range(0, lay.orbitals, 32):
                some = pl.ds(begin, 32)
                centre = [columns[w, c, some, :] for c in range(4)]
                for half in range(0, lay.points, 128):
                    distance = (at[0][:, half : half + 128] - centre[0]) ** 2
                    distance = distance + (at[1][:, half : half + 128] - centre[1]) ** 2
                    distance = distance + (at[2][:, half : half + 128] - centre[2]) ** 2
                    value = jnp.exp(centre[3] * distance)
                    orb[slot, some, half : half + 128] = value.astype(jnp.bfloat16)
            return carry

        lax.fori_loop(0, total, orbital, 0)
        return (first_total, second_total)

    totals = (jnp.int32(0), jnp.int32(0))
    for g in range(3):
        live = jnp.minimum(whole(g, lay.meta, 0), lay.batches)
        totals = lax.fori_loop(0, live, functools.partial(batch, g), totals)
    first_total, second_total = totals
    for u in range(UNROLL):
        work[lay.work_first + first_total + u] = lay.blank
        work[lay.work_second + second_total + u] = lay.blank
    work[lay.work_counts] = first_total
    work[lay.work_counts + 1] = second_total
    for copy in density_copies:
        copy.wait()

    def fold(step, carry):
        sums = []
        for u in range(UNROLL):
            slot = work[lay.work_first + step * UNROLL + u]
            row = work[lay.work_row + slot]
            others = jnp.concatenate(
                [orb[work[slot * lay.partners + k]] for k in range(lay.partners)], axis=0
            )
            stored = jnp.concatenate([density[row, k] for k in range(lay.partners)], axis=1)
            folded = jnp.dot(stored, others, preferred_element_type=jnp.float32)
            product = orb[slot].astype(jnp.float32) * folded
            total = product[0:8]
            for begin in range(8, lay.orbitals, 8):
                total = total + product[begin : begin + 8]
            sums.append((slot // listed, total))
        for number, total in sums:
            rho[number] = rho[number] + total
        return carry

    lax.fori_loop(0, (first_total + UNROLL - 1) // UNROLL, fold, 0)
    part[: lay.batches, :] = jnp.sum(rho[: lay.batches], axis=1)
    part[lay.batches :, :] = jnp.sum(rho[2 * lay.batches : 3 * lay.batches], axis=1)


def cube_root(x):
    size = jnp.abs(x)
    safe = jnp.where(size > 0.0, size, 1.0)
    root = jnp.exp2(jnp.log2(safe) * (1.0 / 3.0))
    root = root - (root - safe / (root * root)) * (1.0 / 3.0)
    root = jnp.where(size > 0.0, root, 0.0)
    return jnp.where(x < 0.0, -root, root)


def second_kernel(lay, pack_own, pack_pair, pack_far, part, arrived, pair_rho, orb, work, out, potential):
    packs = (pack_own, pack_pair, pack_far)
    n = lay.batches
    density_values = (part[:n] + arrived[n:], pair_rho[...], part[n:] + arrived[:n])
    potential[...] = jnp.zeros_like(potential)
    for g in range(3):
        weights = packs[g][lay.weights : lay.weights + n, :]
        potential[g * n : (g + 1) * n, :] = -exchange_coef * cube_root(density_values[g]) * weights
    out[...] = jnp.zeros_like(out)

    def contribute(step, carry):
        for u in range(UNROLL):
            slot = work[lay.work_second + step * UNROLL + u]
            row = work[lay.work_row + slot]
            others = jnp.concatenate(
                [orb[work[slot * lay.partners + k]] for k in range(lay.partners)], axis=0
            )
            scale = potential[pl.ds(slot // lay.listed, 1), :]
            weighted = (orb[slot].astype(jnp.float32) * scale).astype(jnp.bfloat16)
            contrib = lax.dot_general(
                weighted, others, (((1,), (1,)), ((), ())), preferred_element_type=jnp.float32
            )
            for k in range(lay.partners):
                begin = k * lay.orbitals
                out[row, k] += contrib[:, begin : begin + lay.orbitals]
        return carry

    total = work[lay.work_counts + 1]
    lax.fori_loop(0, (total + UNROLL - 1) // UNROLL, contribute, 0)


def on_device(counts, points, weights, block_lists, pattern, basis_table, density):
    batches, listed = block_lists.shape
    rows, partners = pattern.shape
    orbitals = basis_table.shape[2]
    lay = Layout(batches, listed, points.shape[2], rows, partners, orbitals)
    devices = lax.axis_size("space")
    me = lax.axis_index("space").astype(jnp.int32).reshape(1)
    in_vmem = pl.BlockSpec(memory_space=VMEM)
    in_smem = pl.BlockSpec(memory_space=SMEM)
    anywhere = pl.BlockSpec(memory_space=pl.ANY)
    params = pltpu.CompilerParams(vmem_limit_bytes=LIMIT)
    pair_route = [(i, i ^ 1) for i in range(devices)]
    far_route = [
        (i, i + 1 if i % 2 else i - 1)
        for i in range(devices)
        if 0 <= (i + 1 if i % 2 else i - 1) < devices
    ]

    pack = pl.pallas_call(
        functools.partial(pack_kernel, lay),
        out_shape=jax.ShapeDtypeStruct((lay.height, lay.points), jnp.float32),
        in_specs=[in_smem, in_smem] + [in_vmem] * 5,
        out_specs=in_vmem,
        compiler_params=params,
        name="pack",
    )(me, counts, points, weights, block_lists, pattern, basis_table)
    pack_far = lax.ppermute(pack, "space", far_route)
    pack_pair = lax.ppermute(pack, "space", pair_route)
    density_pair = lax.ppermute(density, "space", pair_route)

    part, orb, work = pl.pallas_call(
        functools.partial(first_kernel, lay),
        out_shape=(
            jax.ShapeDtypeStruct((2 * batches, lay.points), jnp.float32),
            jax.ShapeDtypeStruct((lay.slots + 1, orbitals, lay.points), jnp.bfloat16),
            jax.ShapeDtypeStruct((lay.work,), jnp.int32),
        ),
        in_specs=[in_vmem] * 3 + [anywhere] * 2,
        out_specs=(in_vmem, in_vmem, in_smem),
        scratch_shapes=[
            VMEM((3 * rows, 4, orbitals, 128), jnp.float32),
            VMEM((2 * rows, partners, orbitals, orbitals), jnp.bfloat16),
            VMEM((3 * batches + 1, 8, lay.points), jnp.float32),
            SMEM((3, lay.scalar_rows, 128), jnp.float32),
            SMEM((2 * rows * partners,), jnp.int32),
            SMEM((3 * rows + 1,), jnp.int32),
            SMEM((listed + 1,), jnp.int32),
            pltpu.SemaphoreType.DMA((3,)),
            pltpu.SemaphoreType.DMA((2,)),
        ],
        compiler_params=params,
        name="first",
    )(pack, pack_pair, pack_far, density, density_pair)

    arrived = lax.ppermute(part, "space", far_route)
    own_rho = part[:batches] + arrived[batches:]
    pair_rho = lax.ppermute(own_rho, "space", pair_route)

    return pl.pallas_call(
        functools.partial(second_kernel, lay),
        out_shape=jax.ShapeDtypeStruct(density.shape, jnp.float32),
        in_specs=[in_vmem] * 7 + [in_smem],
        out_specs=in_vmem,
        scratch_shapes=[VMEM((-(-(3 * batches + 1) // 8) * 8, lay.points), jnp.float32)],
        compiler_params=params,
        name="second",
    )(pack, pack_pair, pack_far, part, arrived, pair_rho, orb, work)


def solution(mesh):
    in_specs = (
        P(("parts", "space")),
        P(("parts", "space"), None, None),
        P(("parts", "space"), None),
        P(("parts", "space"), None),
        P(("parts", "space"), None),
        P(("parts", "space"), None, None),
        P(("parts", "space"), None, None, None),
    )
    out_specs = P(("parts", "space"), None, None, None)
    return jax.shard_map(
        on_device, mesh=mesh, in_specs=in_specs, out_specs=out_specs, check_vma=False
    )
```

```python
import functools
import math

import jax
import jax.numpy as jnp
from jax import lax
from jax.experimental import pallas as pl
from jax.experimental.pallas import tpu as pltpu
from jax.sharding import PartitionSpec as P

exchange_coef = (3.0 / math.pi) ** (1.0 / 3.0)
VMEM = pltpu.VMEM
SMEM = pltpu.SMEM
HBM = pltpu.HBM
LIMIT = 12 << 20
WHOLE = 63 << 20
REACH = 3
UNROLL = 8
NEAR, PAIR = 32, 64


def split(value, size):
    if size & (size - 1):
        quotient = value // size
        return quotient, value - quotient * size
    return lax.shift_right_logical(value, size.bit_length() - 1), value & (size - 1)


class Layout:
    def __init__(self, batches, listed, points, rows, partners, orbitals):
        self.batches, self.listed, self.points = batches, listed, points
        self.rows, self.partners, self.orbitals = rows, partners, orbitals
        self.weights = -(-3 * batches // 8) * 8
        self.basis = self.weights + -(-batches // 8) * 8
        self.lists = 0
        self.pattern = -(-listed // 8) * 8
        self.meta = self.pattern + -(-partners // 8) * 8
        self.scalar_rows = -(-max(4 * rows, self.meta + 1) // 8) * 8
        self.height = self.basis + self.scalar_rows
        self.slots = 3 * batches * listed
        self.blank = self.slots
        self.code = 4 * (self.slots + 1 + -(self.slots + 1) % 512)
        self.outside = 3 * rows
        self.columns = 2 * rows + REACH
        self.units = 2 * self.slots


def pack_kernel(lay, counts, points, weights, lists, pattern, basis, out, held, sems):
    copies = [
        pltpu.make_async_copy(source, target, sems.at[number])
        for number, (source, target) in enumerate(
            zip((counts, points, weights, lists, pattern, basis), held)
        )
    ]
    for copy in copies:
        copy.start()
    out[...] = jnp.zeros_like(out)
    me = lax.axis_index("space")
    for copy in copies:
        copy.wait()
    counts, points, weights, lists, pattern, basis = held
    for t in range(lay.batches):
        out[3 * t : 3 * t + 3, :] = points[t]
    out[lay.weights : lay.weights + lay.batches, :] = weights[...]
    for w in range(lay.rows):
        out[lay.basis + 4 * w : lay.basis + 4 * w + 4, :128] = basis[w].astype(jnp.float32)
    begin = lay.basis + lay.lists
    out[begin : begin + lay.listed, 128 : 128 + lay.batches] = lists[...].astype(jnp.float32)
    begin = lay.basis + lay.pattern
    out[begin : begin + lay.partners, 128 : 128 + lay.rows] = pattern[...].astype(jnp.float32)
    begin = lay.basis + lay.meta
    lane = lax.broadcasted_iota(jnp.int32, (1, 128), 1)
    meta = jnp.where(lane == 0, counts[0], jnp.where(lane == 1, me, 0))
    out[begin : begin + 1, 128:256] = meta.astype(jnp.float32)


def first_kernel(
    lay,
    pack_own,
    pack_pair,
    pack_far,
    density_own,
    density_pair,
    part,
    orb,
    units,
    ends,
    columns,
    density,
    rho,
    coded,
    scalars,
    place,
    needed,
    scalar_sems,
    density_sems,
):
    packs = (pack_own, pack_pair, pack_far)
    rows, listed, partners = lay.rows, lay.listed, lay.partners
    density_copies = [
        pltpu.make_async_copy(source, density.at[pl.ds(g * rows, rows)], density_sems.at[g])
        for g, source in enumerate((density_own, density_pair))
    ]
    for copy in density_copies:
        copy.start()
    me = lax.axis_index("space")
    own, pair = me, me ^ 1
    far = jnp.where(me % 2 == 0, me - 1, me + 1)
    start = own * rows
    far_first = jnp.where(me % 2 == 0, rows - REACH, 0)

    for g in range(3):
        raw = packs[g][lay.basis : lay.basis + lay.scalar_rows, 128:256].astype(jnp.int32)
        owner, inner = split(raw, rows)
        place_far = jnp.where(owner == far, 2 * rows + inner, lay.outside)
        window = jnp.where(
            owner == own, inner, jnp.where(owner == pair, rows + inner, place_far)
        )
        near = (raw >= start - REACH) & (raw < start + rows + REACH)
        code = window + jnp.where(near, NEAR, 0) + jnp.where(owner == pair, PAIR, 0)
        line = lax.broadcasted_iota(jnp.int32, raw.shape, 0)
        code = jnp.where(line < lay.pattern, code, window)
        coded[g] = jnp.where(line < lay.meta, code, raw)
    scalar_copies = [
        pltpu.make_async_copy(coded.at[g], scalars.at[g], scalar_sems.at[g]) for g in range(3)
    ]
    for copy in scalar_copies:
        copy.start()

    orb[lay.blank] = jnp.zeros(orb.shape[1:], orb.dtype)
    rho[...] = jnp.zeros_like(rho)

    for g in range(3):
        count = REACH if g == 2 else rows
        first = far_first if g == 2 else 0
        owner = (own, pair, far)[g]
        table = packs[g][lay.basis : lay.basis + 4 * rows, :128]
        if g == 2:
            table = jnp.where(me % 2 == 0, table[4 * (rows - count) :], table[: 4 * count])
        table = table.T
        for w in range(count):
            for c in range(4):
                column = table[:, 4 * w + c : 4 * w + c + 1]
                if c == 0:
                    column = column + (owner * rows + first + w).astype(jnp.float32)
                if c == 3:
                    column = -column
                columns[g * rows + w, c] = jnp.broadcast_to(column, (lay.orbitals, 128))

    for w in range(lay.outside + 1):
        place[w] = -1
    units[0, lay.units] = lay.blank * 16
    units[1, lay.units] = lay.blank * lay.code + lay.blank
    for copy in scalar_copies:
        copy.wait()

    def visit(g, mask, value, limit, t, end):
        base = (g * lay.batches + t) * listed
        total = jnp.int32(0)
        for b in range(listed):
            code = scalars[g, lay.lists + b, t]
            w = code & 31
            place[w] = base + b
            needed[total] = w * listed + b
            if value == "own":
                keep = w < rows
            elif value == "rest":
                keep = (w >= rows) & (code >= NEAR)
            else:
                keep = (code & NEAR) != 0
            total = total + jnp.where(keep, 1, 0)
        place[lay.outside] = -1
        at = [packs[g][pl.ds(3 * t + c, 1), :] for c in range(3)]

        def entry(index, end):
            word = needed[index]
            w, inner = split(word, listed)
            slot = base + inner
            column = jnp.where(w < 2 * rows, w, w - far_first)
            for begin in range(0, lay.orbitals, 32):
                some = pl.ds(begin, 32)
                centre = [columns[column, c, some, :] for c in range(4)]
                for half in range(0, lay.points, 128):
                    distance = (at[0][:, half : half + 128] - centre[0]) ** 2
                    distance = distance + (at[1][:, half : half + 128] - centre[1]) ** 2
                    distance = distance + (at[2][:, half : half + 128] - centre[2]) ** 2
                    result = jnp.exp(centre[3] * distance)
                    orb[slot, some, half : half + 128] = result.astype(jnp.bfloat16)
            group = jnp.where(w < rows, 0, 1)
            inner = jnp.minimum(w - group * rows, rows - 1)
            codes, held = [], []
            for k in range(1, partners):
                other = place[scalars[group, lay.pattern + k, inner]]
                codes.append(k * (lay.code // 4) + other)
                held.append((other >= base) & (other < base + listed))
            one, two, three = held
            blank = jnp.int32(lay.blank)
            first = jnp.where(
                one, codes[0], jnp.where(two, codes[1], jnp.where(three, codes[2], blank))
            )
            second = jnp.where(
                one & two, codes[1], jnp.where((one | two) & three, codes[2], blank)
            )
            third = jnp.where(one & two & three, codes[2], blank)
            more = (one & two) | ((one | two) & three)
            valid = jnp.where(w < limit, 1, 0)
            units[0, end] = slot * 16 + w
            units[1, end] = slot * lay.code + first
            end = end + valid
            units[0, end] = slot * 16 + w
            units[1, end] = second * lay.code + third
            return end + jnp.where(more, valid, 0)

        return lax.fori_loop(0, total, entry, end)

    def live(g):
        return jnp.minimum(scalars[g, lay.meta, 0], lay.batches)

    end = jnp.int32(0)
    end = lax.fori_loop(0, live(0), functools.partial(visit, 0, 0, "own", rows), end)
    end = lax.fori_loop(0, live(2), functools.partial(visit, 2, 0, "near", rows), end)
    ends[0] = end
    end = lax.fori_loop(0, live(0), functools.partial(visit, 0, 0, "rest", 2 * rows), end)
    ends[1] = end
    last = lax.fori_loop(0, live(1), functools.partial(visit, 1, 0, "near", rows), end)
    ends[2] = last
    for copy in density_copies:
        copy.wait()

    def fold(step, carry):
        sums = []
        for u in range(UNROLL):
            index = step * UNROLL + u
            index = jnp.where(index < end, index, lay.units)
            slot, row, (k1, o1), (k2, o2) = decode(lay, units, index)
            others = jnp.concatenate([orb[o1], orb[o2]], axis=0)
            stored = jnp.concatenate([density[row, k1], density[row, k2]], axis=1)
            folded = jnp.dot(stored, others, preferred_element_type=jnp.float32)
            product = orb[slot].astype(jnp.float32) * folded
            total = product[0:8]
            for begin in range(8, lay.orbitals, 8):
                total = total + product[begin : begin + 8]
            sums.append((split(slot, listed)[0], total))
        for number, total in sums:
            rho[number] = rho[number] + total
        return carry

    lax.fori_loop(0, (end + UNROLL - 1) // UNROLL, fold, 0)
    part[: lay.batches, :] = jnp.sum(rho[: lay.batches], axis=1)
    part[lay.batches :, :] = jnp.sum(rho[2 * lay.batches : 3 * lay.batches], axis=1)


def decode(lay, units, index):
    word = units[0, index]
    both = units[1, index]
    each = [split(code, lay.code // 4) for code in split(both, lay.code)]
    return *split(word, 16), *each


def cube_root(x):
    size = jnp.abs(x)
    safe = jnp.where(size > 0.0, size, 1.0)
    root = jnp.exp2(jnp.log2(safe) * (1.0 / 3.0))
    root = root - (root - safe / (root * root)) * (1.0 / 3.0)
    root = jnp.where(size > 0.0, root, 0.0)
    return jnp.where(x < 0.0, -root, root)


def second_kernel(
    lay, pack_own, pack_pair, pack_far, part, arrived, pair_rho, orb, units, ends, out, potential
):
    packs = (pack_own, pack_pair, pack_far)
    n = lay.batches
    density_values = (part[:n] + arrived[n:], pair_rho[...], part[n:] + arrived[:n])
    potential[...] = jnp.zeros_like(potential)
    for g in range(3):
        weights = packs[g][lay.weights : lay.weights + n, :]
        potential[g * n : (g + 1) * n, :] = -exchange_coef * cube_root(density_values[g]) * weights
    out[...] = jnp.zeros_like(out)
    shared = ends[0]
    skipped = ends[1] - shared
    total = ends[2] - skipped

    def contribute(step, carry):
        for u in range(UNROLL):
            index = step * UNROLL + u
            index = jnp.where(
                index < shared, index, jnp.where(index < total, index + skipped, lay.units)
            )
            slot, row, (k1, o1), (k2, o2) = decode(lay, units, index)
            others = jnp.concatenate([orb[o1], orb[o2]], axis=0)
            scale = potential[pl.ds(split(slot, lay.listed)[0], 1), :]
            weighted = (orb[slot].astype(jnp.float32) * scale).astype(jnp.bfloat16)
            contrib = lax.dot_general(
                weighted, others, (((1,), (1,)), ((), ())), preferred_element_type=jnp.float32
            )
            out[row, k1] += contrib[:, : lay.orbitals]
            out[row, k2] += contrib[:, lay.orbitals :]
        return carry

    lax.fori_loop(0, (total + UNROLL - 1) // UNROLL, contribute, 0)


def on_device(counts, points, weights, block_lists, pattern, basis_table, density):
    batches, listed = block_lists.shape
    rows, partners = pattern.shape
    orbitals = basis_table.shape[2]
    lay = Layout(batches, listed, points.shape[2], rows, partners, orbitals)
    devices = lax.axis_size("space")
    in_vmem = pl.BlockSpec(memory_space=VMEM)
    in_smem = pl.BlockSpec(memory_space=SMEM)
    in_hbm = pl.BlockSpec(memory_space=HBM)
    params = pltpu.CompilerParams(vmem_limit_bytes=LIMIT)
    pair_route = [(i, i ^ 1) for i in range(devices)]
    far_route = [
        (i, i + 1 if i % 2 else i - 1)
        for i in range(devices)
        if 0 <= (i + 1 if i % 2 else i - 1) < devices
    ]

    density_pair = lax.ppermute(density, "space", pair_route)
    lists, pattern = block_lists.T, pattern.T
    inputs = (counts, points, weights, lists, pattern, basis_table)
    pack = pl.pallas_call(
        functools.partial(pack_kernel, lay),
        out_shape=jax.ShapeDtypeStruct((lay.height, lay.points), jnp.float32),
        in_specs=[in_hbm] * 6,
        out_specs=in_vmem,
        scratch_shapes=[
            [SMEM(counts.shape, counts.dtype)] + [VMEM(x.shape, x.dtype) for x in inputs[1:]],
            pltpu.SemaphoreType.DMA((6,)),
        ],
        compiler_params=pltpu.CompilerParams(vmem_limit_bytes=WHOLE),
        name="pack",
    )(*inputs)
    pack_far = lax.ppermute(pack, "space", far_route)
    pack_pair = lax.ppermute(pack, "space", pair_route)

    part, orb, units, ends = pl.pallas_call(
        functools.partial(first_kernel, lay),
        out_shape=(
            jax.ShapeDtypeStruct((2 * batches, lay.points), jnp.float32),
            jax.ShapeDtypeStruct((lay.slots + 1, orbitals, lay.points), jnp.bfloat16),
            jax.ShapeDtypeStruct((2, lay.units + 1), jnp.int32),
            jax.ShapeDtypeStruct((3,), jnp.int32),
        ),
        in_specs=[in_vmem] * 3 + [in_hbm, in_vmem],
        out_specs=(in_vmem, in_vmem, in_smem, in_smem),
        scratch_shapes=[
            VMEM((lay.columns, 4, orbitals, 128), jnp.float32),
            VMEM((2 * rows, partners, orbitals, orbitals), jnp.bfloat16),
            VMEM((3 * batches + 1, 8, lay.points), jnp.float32),
            VMEM((3, lay.scalar_rows, 128), jnp.int32),
            SMEM((3, lay.scalar_rows, 128), jnp.int32),
            SMEM((lay.outside + 1,), jnp.int32),
            SMEM((listed + 1,), jnp.int32),
            pltpu.SemaphoreType.DMA((3,)),
            pltpu.SemaphoreType.DMA((2,)),
        ],
        compiler_params=params,
        name="first",
    )(pack, pack_pair, pack_far, density, density_pair)

    arrived = lax.ppermute(part, "space", far_route)
    own_rho = part[:batches] + arrived[batches:]
    pair_rho = lax.ppermute(own_rho, "space", pair_route)

    return pl.pallas_call(
        functools.partial(second_kernel, lay),
        out_shape=jax.ShapeDtypeStruct(density.shape, jnp.float32),
        in_specs=[in_vmem] * 7 + [in_smem] * 2,
        out_specs=in_vmem,
        scratch_shapes=[VMEM((-(-(3 * batches + 1) // 8) * 8, lay.points), jnp.float32)],
        compiler_params=params,
        name="second",
    )(pack, pack_pair, pack_far, part, arrived, pair_rho, orb, units, ends)


def solution(mesh):
    in_specs = (
        P(("parts", "space")),
        P(("parts", "space"), None, None),
        P(("parts", "space"), None),
        P(("parts", "space"), None),
        P(("parts", "space"), None),
        P(("parts", "space"), None, None),
        P(("parts", "space"), None, None, None),
    )
    out_specs = P(("parts", "space"), None, None, None)
    return jax.shard_map(
        on_device, mesh=mesh, in_specs=in_specs, out_specs=out_specs, check_vma=False
    )
```

```python
import functools
import math

import jax
import jax.numpy as jnp
from jax import lax
from jax.experimental import pallas as pl
from jax.experimental.pallas import tpu as pltpu
from jax.sharding import PartitionSpec as P

exchange_coef = (3.0 / math.pi) ** (1.0 / 3.0)
VMEM = pltpu.VMEM
SMEM = pltpu.SMEM
HBM = pltpu.HBM
LIMIT = 12 << 20
WHOLE = 63 << 20
BUSY = 12 << 20
REACH = 3
UNROLL = 8
PAIRED = 2
LANES = 16
NOWHERE, ELSEWHERE = 31, 30
NONE = 15


def split(value, size):
    if size & (size - 1):
        quotient = value // size
        return quotient, value - quotient * size
    return lax.shift_right_logical(value, size.bit_length() - 1), value & (size - 1)


class Layout:
    def __init__(self, batches, listed, points, rows, partners, orbitals):
        self.batches, self.listed, self.points = batches, listed, points
        self.rows, self.partners, self.orbitals = rows, partners, orbitals
        self.weights = -(-3 * batches // 8) * 8
        self.basis = self.weights + -(-batches // 8) * 8
        self.lists = 0
        self.pattern = -(-listed // 8) * 8
        self.meta = self.pattern + -(-partners // 8) * 8
        self.scalar_rows = -(-max(4 * rows, self.meta + 1) // 8) * 8
        self.height = self.basis + self.scalar_rows
        self.slots = 3 * batches * listed
        self.blank, self.trash = self.slots, self.slots + 1
        self.columns = 2 * rows + REACH
        self.units = 2 * batches * listed
        self.empty = (self.blank * 16) << 12 | NONE << 6 | NONE


def pack_kernel(lay, counts, points, weights, lists, pattern, basis, out, held, sems):
    copies = [
        pltpu.make_async_copy(source, target, sems.at[number])
        for number, (source, target) in enumerate(
            zip((counts, points, weights, lists, pattern, basis), held)
        )
    ]
    for copy in copies:
        copy.start()
    out[...] = jnp.zeros_like(out)
    me = lax.axis_index("space")
    for copy in copies:
        copy.wait()
    counts, points, weights, lists, pattern, basis = held
    for t in range(lay.batches):
        out[3 * t : 3 * t + 3, :] = points[t]
    out[lay.weights : lay.weights + lay.batches, :] = weights[...]
    for w in range(lay.rows):
        out[lay.basis + 4 * w : lay.basis + 4 * w + 4, :128] = basis[w].astype(jnp.float32)
    begin = lay.basis + lay.lists
    out[begin : begin + lay.listed, 128 : 128 + lay.batches] = lists[...].astype(jnp.float32)
    begin = lay.basis + lay.pattern
    out[begin : begin + lay.partners, 128 : 128 + lay.rows] = pattern[...].astype(jnp.float32)
    begin = lay.basis + lay.meta
    lane = lax.broadcasted_iota(jnp.int32, (1, 128), 1)
    meta = jnp.where(lane == 0, counts[0], jnp.where(lane == 1, me, 0))
    out[begin : begin + 1, 128:256] = meta.astype(jnp.float32)


class Place:
    def __init__(self, lay):
        self.lay = lay
        self.own = lax.axis_index("space")
        self.pair = self.own ^ 1
        even = self.own % 2 == 0
        self.even = even
        self.far = jnp.where(even, self.own - 1, self.own + 1)
        self.far_first = jnp.where(even, lay.rows - REACH, 0)

    def window(self, raw, outside):
        rows = self.lay.rows
        owner, inner = split(raw, rows)
        far = jnp.where(owner == self.far, 2 * rows + inner, outside)
        return jnp.where(owner == self.own, inner, jnp.where(owner == self.pair, rows + inner, far))


def block_of(lay, pack):
    return pack[lay.basis : lay.basis + lay.scalar_rows, 128:256]


def partner_choice(lay, place, block):
    raw = block[lay.pattern : lay.pattern + 8].astype(jnp.int32)
    turned = place.window(raw, ELSEWHERE).astype(jnp.float32).T
    lane = lax.broadcasted_iota(jnp.int32, (lay.rows, 32), 1).astype(jnp.float32)
    return jnp.concatenate(
        [
            jnp.where(turned[: lay.rows, k : k + 1] == lane, 1.0, 0.0)
            for k in range(1, lay.partners)
        ],
        axis=0,
    ).astype(jnp.bfloat16)


def code_batches(lay, place, g, block, choice, first_row, wanted):
    listed, rows = lay.listed, lay.rows
    raw = block.astype(jnp.int32)
    lists = raw[lay.lists : lay.lists + listed]
    window = place.window(lists, NOWHERE)
    lane = lax.broadcasted_iota(jnp.int32, (listed, 128), 1)
    position = lax.broadcasted_iota(jnp.int32, (listed, 128), 0)
    base = (g * lay.batches + lane) * listed
    column = jnp.where(window < 2 * rows, window, window - place.far_first)
    start = place.own * rows
    near = (lists >= start - REACH) & (lists < start + rows + REACH)
    entry = (base + position) * 32 + column
    result = jnp.where(wanted(window, near), entry, -1)

    line = lax.broadcasted_iota(jnp.int32, (32, 128), 0)
    held = jnp.zeros((32, 128), jnp.int32)
    for b in range(listed):
        held = jnp.where(line == window[b : b + 1], b + 1, held)
    others = jnp.dot(
        choice, held.astype(jnp.float32).astype(jnp.bfloat16), preferred_element_type=jnp.float32
    ).astype(jnp.int32)
    codes = [
        (k * 16 - 1) + others[(k - 1) * rows : k * rows] for k in range(1, lay.partners)
    ]
    one, two, three = [others[(k - 1) * rows : k * rows] > 0 for k in range(1, lay.partners)]
    itself = held[first_row : first_row + rows] - 1
    item_row = first_row + lax.broadcasted_iota(jnp.int32, (rows, 128), 0)
    item_base = (g * lay.batches + lax.broadcasted_iota(jnp.int32, (rows, 128), 1)) * listed
    common = ((item_base + itself) * 16 + item_row) << 12
    first = jnp.where(one, codes[0], jnp.where(two, codes[1], jnp.where(three, codes[2], NONE)))
    more = (one & two) | ((one | two) & three)
    second = jnp.where(one & two, codes[1], codes[2])
    third = jnp.where(one & two & three, codes[2], NONE)
    exists = itself >= 0
    units = (
        jnp.where(exists, common + (itself << 6) + first, -1),
        jnp.where(exists & more, common + (second << 6) + third, -1),
    )
    for number, unit in enumerate(units):
        found = jnp.full((listed, 128), -1, jnp.int32)
        for w in range(rows):
            found = jnp.where(window == first_row + w, unit[w : w + 1], found)
        begin = LANES * (number + 1)
        result = jnp.where(lane < begin, result, pltpu.roll(found, begin, 1))
    begin = LANES * 3
    return jnp.where(lane < begin, result, pltpu.roll(raw[lay.meta : lay.meta + 8], begin, 1))


def list_batches(lay, scalars, begin, entries, units, totals):
    def visit(t, totals):
        entry_total, unit_total = totals
        for b in range(lay.listed):
            entry = scalars[b, begin + t]
            entries[entry_total] = entry
            entry_total = entry_total + jnp.where(entry >= 0, 1, 0)
            for lane in (LANES, 2 * LANES):
                unit = scalars[b, begin + lane + t]
                units[unit_total] = unit
                unit_total = unit_total + jnp.where(unit >= 0, 1, 0)
        return (entry_total, unit_total)

    live = jnp.minimum(scalars[0, begin + 3 * LANES], lay.batches)
    return lax.fori_loop(0, live, visit, totals)


def spread_columns(lay, place, g, pack, columns):
    rows = lay.rows
    table = pack[lay.basis : lay.basis + 4 * rows, :128]
    count, first, owner = rows, 0, (place.own, place.pair, place.far)[g]
    if g == 2:
        count, first = REACH, place.far_first
        table = jnp.where(place.even, table[4 * (rows - count) :], table[: 4 * count])
    table = table.T
    for w in range(count):
        for c in range(4):
            column = table[:, 4 * w + c : 4 * w + c + 1]
            if c == 0:
                column = column + (owner * rows + first + w).astype(jnp.float32)
            if c == 3:
                column = -column
            columns[g * rows + w, c] = jnp.broadcast_to(column, (lay.orbitals, 128))


def spread_points(lay, g, pack, points):
    for t in range(lay.batches):
        points[g * lay.batches + t, 0:3, :] = pack[3 * t : 3 * t + 3, :]


def work_out(lay, entries, total, points, columns, orb):
    for u in range(PAIRED - 1):
        entries[total + u] = lay.trash * 32

    def some(step, carry):
        for u in range(PAIRED):
            slot, column = split(entries[step * PAIRED + u], 32)
            batch = jnp.minimum(split(slot, lay.listed)[0], 3 * lay.batches - 1)
            at = [points[batch, c : c + 1, :] for c in range(3)]
            for begin in range(0, lay.orbitals, 16):
                lines = pl.ds(begin, 16)
                centre = [columns[column, c, lines, :] for c in range(4)]
                for half in range(0, lay.points, 128):
                    distance = (at[0][:, half : half + 128] - centre[0]) ** 2
                    distance = distance + (at[1][:, half : half + 128] - centre[1]) ** 2
                    distance = distance + (at[2][:, half : half + 128] - centre[2]) ** 2
                    result = jnp.exp(centre[3] * distance)
                    orb[slot, lines, half : half + 128] = result.astype(jnp.bfloat16)
        return carry

    lax.fori_loop(0, (total + PAIRED - 1) // PAIRED, some, 0)


def own_kernel(
    lay, pack, orb, columns, units, points, coded, scalars, entries, sem
):
    place = Place(lay)
    block = block_of(lay, pack)
    choice = partner_choice(lay, place, block)
    coded[...] = code_batches(
        lay, place, 0, block, choice, 0, lambda window, near: window < lay.rows
    )
    copy = pltpu.make_async_copy(coded, scalars, sem)
    copy.start()
    orb[lay.blank] = jnp.zeros(orb.shape[1:], orb.dtype)
    spread_columns(lay, place, 0, pack, columns)
    points[...] = jnp.zeros_like(points)
    spread_points(lay, 0, pack, points)
    copy.wait()
    total, end = list_batches(lay, scalars, 0, entries, units, (jnp.int32(0), jnp.int32(0)))
    units[2 * lay.batches * lay.listed + 1] = end
    work_out(lay, entries, total, points, columns, orb)


def first_kernel(
    lay,
    pack_own,
    pack_pair,
    pack_far,
    density_own,
    density_pair,
    units_given,
    orb_in,
    columns_in,
    part,
    orb,
    columns,
    units,
    points,
    density,
    rho,
    units_own,
    coded,
    scalars,
    entries,
    scalar_sem,
    density_sems,
    units_sem,
):
    rows, listed = lay.rows, lay.listed
    density_copies = [
        pltpu.make_async_copy(source, density.at[pl.ds(g * rows, rows)], density_sems.at[g])
        for g, source in enumerate((density_own, density_pair))
    ]
    for copy in density_copies:
        copy.start()
    units_copy = pltpu.make_async_copy(units_given, units_own, units_sem)
    units_copy.start()
    place = Place(lay)
    blocks = [block_of(lay, pack) for pack in (pack_own, pack_pair, pack_far)]
    own_choice = partner_choice(lay, place, blocks[0])
    pair_choice = partner_choice(lay, place, blocks[1])
    of_far = code_batches(
        lay, place, 2, blocks[2], own_choice, 0, lambda window, near: near
    )
    of_own = code_batches(
        lay,
        place,
        0,
        blocks[0],
        pair_choice,
        rows,
        lambda window, near: (window >= rows) & ((window < 2 * rows) | near),
    )
    lane = lax.broadcasted_iota(jnp.int32, of_far.shape, 1)
    coded[...] = jnp.where(lane < 4 * LANES, of_far, pltpu.roll(of_own, 4 * LANES, 1))
    scalar_copy = pltpu.make_async_copy(coded, scalars, scalar_sem)
    scalar_copy.start()
    spread_columns(lay, place, 1, pack_pair, columns)
    spread_columns(lay, place, 2, pack_far, columns)
    points[...] = jnp.zeros_like(points)
    spread_points(lay, 0, pack_own, points)
    spread_points(lay, 2, pack_far, points)
    rho[...] = jnp.zeros_like(rho)
    scalar_copy.wait()
    totals = (jnp.int32(0), jnp.int32(0))
    totals = list_batches(lay, scalars, 0, entries, units, totals)
    units[4 * lay.batches * listed + 1] = totals[1]
    total, end = list_batches(lay, scalars, 4 * LANES, entries, units, totals)
    work_out(lay, entries, total, points, columns, orb)
    for copy in density_copies:
        copy.wait()
    units_copy.wait()
    shared = units_own[2 * lay.batches * listed + 1]
    end = end + shared

    def fold(step, carry):
        sums = []
        for u in range(UNROLL):
            index = step * UNROLL + u
            word = jnp.where(
                index < shared,
                units_own[jnp.minimum(index, lay.units - 1)],
                units[jnp.maximum(index - shared, 0)],
            )
            word = jnp.where(index < end, word, lay.empty)
            slot, row, (k1, o1), (k2, o2) = decode(lay, word)
            others = jnp.concatenate([orb[o1], orb[o2]], axis=0)
            stored = jnp.concatenate([density[row, k1], density[row, k2]], axis=1)
            folded = jnp.dot(stored, others, preferred_element_type=jnp.float32)
            product = orb[slot].astype(jnp.float32) * folded
            total = product[0:8]
            for begin in range(8, lay.orbitals, 8):
                total = total + product[begin : begin + 8]
            sums.append((split(slot, listed)[0], total))
        for number, total in sums:
            rho[number] = rho[number] + total
        return carry

    lax.fori_loop(0, (end + UNROLL - 1) // UNROLL, fold, 0)
    part[: lay.batches, :] = jnp.sum(rho[: lay.batches], axis=1)
    part[lay.batches :, :] = jnp.sum(rho[2 * lay.batches : 3 * lay.batches], axis=1)


def pair_kernel(
    lay,
    pack_own,
    pack_pair,
    orb_in,
    columns,
    orb,
    units,
    points,
    coded,
    scalars,
    entries,
    sem,
):
    place = Place(lay)
    choice = partner_choice(lay, place, block_of(lay, pack_own))
    block = block_of(lay, pack_pair)
    coded[...] = code_batches(lay, place, 1, block, choice, 0, lambda window, near: near)
    copy = pltpu.make_async_copy(coded, scalars, sem)
    copy.start()
    points[...] = jnp.zeros_like(points)
    spread_points(lay, 1, pack_pair, points)
    copy.wait()
    total, end = list_batches(lay, scalars, 0, entries, units, (jnp.int32(0), jnp.int32(0)))
    units[2 * lay.batches * lay.listed + 1] = end
    work_out(lay, entries, total, points, columns, orb)


def total_kernel(lay, part, arrived, units, out):
    out[...] = part[: lay.batches] + arrived[lay.batches :]


def decode(lay, word):
    slot = word >> 16
    row = (word >> 12) & 15
    base = slot & ~(lay.listed - 1)
    partners = []
    for shift in (6, 0):
        inner = (word >> shift) & 15
        partners.append(
            ((word >> (shift + 4)) & 3, jnp.where(inner == NONE, lay.blank, base + inner))
        )
    return slot, row, *partners


def cube_root(x):
    size = jnp.abs(x)
    safe = jnp.where(size > 0.0, size, 1.0)
    root = jnp.exp2(jnp.log2(safe) * (1.0 / 3.0))
    root = root - (root - safe / (root * root)) * (1.0 / 3.0)
    root = jnp.where(size > 0.0, root, 0.0)
    return jnp.where(x < 0.0, -root, root)


def second_kernel(
    lay,
    pack_own,
    pack_pair,
    pack_far,
    part,
    arrived,
    pair_rho,
    orb,
    units_given,
    out,
    potential,
    units_held,
    sems,
):
    copies = [
        pltpu.make_async_copy(source, target, sems.at[number])
        for number, (source, target) in enumerate(zip(units_given, units_held))
    ]
    for copy in copies:
        copy.start()
    packs = (pack_own, pack_pair, pack_far)
    n = lay.batches
    density_values = (part[:n] + arrived[n:], pair_rho[...], part[n:] + arrived[:n])
    potential[...] = jnp.zeros_like(potential)
    for g in range(3):
        weights = packs[g][lay.weights : lay.weights + n, :]
        potential[g * n : (g + 1) * n, :] = -exchange_coef * cube_root(density_values[g]) * weights
    out[...] = jnp.zeros_like(out)
    for copy in copies:
        copy.wait()
    units_own, units_first, units_pair = units_held
    most = 2 * n * lay.listed
    one = units_own[most + 1]
    two = one + units_first[2 * most + 1]
    total = two + units_pair[most + 1]

    def contribute(step, carry):
        for u in range(UNROLL):
            index = step * UNROLL + u
            words = [
                units[jnp.clip(index - begin, 0, lay.units - 1)]
                for units, begin in ((units_own, 0), (units_first, one), (units_pair, two))
            ]
            word = jnp.where(index < one, words[0], jnp.where(index < two, words[1], words[2]))
            word = jnp.where(index < total, word, lay.empty)
            slot, row, (k1, o1), (k2, o2) = decode(lay, word)
            others = jnp.concatenate([orb[o1], orb[o2]], axis=0)
            scale = potential[pl.ds(split(slot, lay.listed)[0], 1), :]
            weighted = (orb[slot].astype(jnp.float32) * scale).astype(jnp.bfloat16)
            contrib = lax.dot_general(
                weighted, others, (((1,), (1,)), ((), ())), preferred_element_type=jnp.float32
            )
            out[row, k1] += contrib[:, : lay.orbitals]
            out[row, k2] += contrib[:, lay.orbitals :]
        return carry

    lax.fori_loop(0, (total + UNROLL - 1) // UNROLL, contribute, 0)


def on_device(counts, points, weights, block_lists, pattern, basis_table, density):
    batches, listed = block_lists.shape
    rows, partners = pattern.shape
    orbitals = basis_table.shape[2]
    lay = Layout(batches, listed, points.shape[2], rows, partners, orbitals)
    devices = lax.axis_size("space")
    in_vmem = pl.BlockSpec(memory_space=VMEM)
    in_smem = pl.BlockSpec(memory_space=SMEM)
    in_hbm = pl.BlockSpec(memory_space=HBM)
    cost = pl.CostEstimate(flops=0, bytes_accessed=16 << 20, transcendentals=0)

    def params(limit=LIMIT):
        return pltpu.CompilerParams(vmem_limit_bytes=limit)

    pair_route = [(i, i ^ 1) for i in range(devices)]
    far_route = [
        (i, i + 1 if i % 2 else i - 1)
        for i in range(devices)
        if 0 <= (i + 1 if i % 2 else i - 1) < devices
    ]

    density_pair = lax.ppermute(density, "space", pair_route)
    inputs = (counts, points, weights, block_lists.T, pattern.T, basis_table)
    pack = pl.pallas_call(
        functools.partial(pack_kernel, lay),
        out_shape=jax.ShapeDtypeStruct((lay.height, lay.points), jnp.float32),
        in_specs=[in_hbm] * 6,
        out_specs=in_vmem,
        scratch_shapes=[
            [SMEM(counts.shape, counts.dtype)] + [VMEM(x.shape, x.dtype) for x in inputs[1:]],
            pltpu.SemaphoreType.DMA((6,)),
        ],
        compiler_params=params(WHOLE),
        name="pack",
    )(*inputs)
    pack_far = lax.ppermute(pack, "space", far_route)
    pack_pair = lax.ppermute(pack, "space", pair_route)

    orb_shape = jax.ShapeDtypeStruct((lay.slots + 2, orbitals, lay.points), jnp.bfloat16)
    columns_shape = jax.ShapeDtypeStruct((lay.columns, 4, orbitals, 128), jnp.float32)
    anywhere = pl.BlockSpec(memory_space=pl.ANY)
    most = 2 * batches * listed

    def units_shape(parts):
        return jax.ShapeDtypeStruct((parts * most + 2,), jnp.int32)

    def scratch(groups):
        return [
            VMEM((listed, 128), jnp.int32),
            SMEM((listed, 128), jnp.int32),
            SMEM((groups * batches * listed + PAIRED,), jnp.int32),
            pltpu.SemaphoreType.DMA(()),
        ]

    points_scratch = VMEM((3 * batches, 8, lay.points), jnp.float32)
    orb, columns, units_own = pl.pallas_call(
        functools.partial(own_kernel, lay),
        out_shape=(orb_shape, columns_shape, units_shape(1)),
        in_specs=[in_vmem],
        out_specs=(in_vmem, in_vmem, in_smem),
        scratch_shapes=[points_scratch, *scratch(1)],
        compiler_params=params(),
        cost_estimate=cost,
        name="first_own",
    )(pack)

    part, orb, columns, units_first = pl.pallas_call(
        functools.partial(first_kernel, lay),
        out_shape=(
            jax.ShapeDtypeStruct((2 * batches, lay.points), jnp.float32),
            orb_shape,
            columns_shape,
            units_shape(2),
        ),
        in_specs=[in_vmem] * 3 + [in_hbm, in_hbm, anywhere, in_vmem, in_vmem],
        out_specs=(in_vmem, in_vmem, in_vmem, in_smem),
        scratch_shapes=[
            points_scratch,
            VMEM((2 * rows, partners, orbitals, orbitals), jnp.bfloat16),
            VMEM((3 * batches + 1, 8, lay.points), jnp.float32),
            SMEM(units_shape(1).shape, jnp.int32),
            *scratch(2),
            pltpu.SemaphoreType.DMA((2,)),
            pltpu.SemaphoreType.DMA(()),
        ],
        input_output_aliases={6: 1, 7: 2},
        compiler_params=params(BUSY),
        cost_estimate=cost,
        name="first",
    )(pack, pack_pair, pack_far, density, density_pair, units_own, orb, columns)

    arrived = lax.ppermute(part, "space", far_route)
    orb, units_pair = pl.pallas_call(
        functools.partial(pair_kernel, lay),
        out_shape=(orb_shape, units_shape(1)),
        in_specs=[in_vmem] * 4,
        out_specs=(in_vmem, in_smem),
        scratch_shapes=[points_scratch, *scratch(1)],
        input_output_aliases={2: 0},
        compiler_params=params(),
        cost_estimate=cost,
        name="first_pair",
    )(pack, pack_pair, orb, columns)
    own_rho = pl.pallas_call(
        functools.partial(total_kernel, lay),
        out_shape=jax.ShapeDtypeStruct((batches, lay.points), jnp.float32),
        in_specs=[in_vmem, in_vmem, anywhere],
        out_specs=in_vmem,
        compiler_params=params(1 << 20),
        name="total",
    )(part, arrived, units_pair)
    pair_rho = lax.ppermute(own_rho, "space", pair_route)

    return pl.pallas_call(
        functools.partial(second_kernel, lay),
        out_shape=jax.ShapeDtypeStruct(density.shape, jnp.float32),
        in_specs=[in_vmem] * 7 + [[anywhere] * 3],
        out_specs=in_vmem,
        scratch_shapes=[
            VMEM((-(-(3 * batches + 1) // 8) * 8, lay.points), jnp.float32),
            [SMEM(units_shape(parts).shape, jnp.int32) for parts in (1, 2, 1)],
            pltpu.SemaphoreType.DMA((3,)),
        ],
        compiler_params=params(),
        name="second",
    )(
        pack,
        pack_pair,
        pack_far,
        part,
        arrived,
        pair_rho,
        orb,
        [units_own, units_first, units_pair],
    )


def solution(mesh):
    in_specs = (
        P(("parts", "space")),
        P(("parts", "space"), None, None),
        P(("parts", "space"), None),
        P(("parts", "space"), None),
        P(("parts", "space"), None),
        P(("parts", "space"), None, None),
        P(("parts", "space"), None, None, None),
    )
    out_specs = P(("parts", "space"), None, None, None)
    return jax.shard_map(
        on_device, mesh=mesh, in_specs=in_specs, out_specs=out_specs, check_vma=False
    )
```

```python
import functools
import math

import jax
import jax.numpy as jnp
from jax import lax
from jax.experimental import pallas as pl
from jax.experimental.pallas import tpu as pltpu
from jax.sharding import PartitionSpec as P

exchange_coef = (3.0 / math.pi) ** (1.0 / 3.0)
VMEM = pltpu.VMEM
SMEM = pltpu.SMEM
HBM = pltpu.HBM
LIMIT = 12 << 20
WHOLE = 63 << 20
BUSY = 12 << 20
REACH = 3
UNROLL = 16
PAIRED = 2
LANES = 16
NOWHERE, ELSEWHERE = 31, 30
NONE = 15


def split(value, size):
    if size & (size - 1):
        quotient = value // size
        return quotient, value - quotient * size
    return lax.shift_right_logical(value, size.bit_length() - 1), value & (size - 1)


class Layout:
    def __init__(self, batches, listed, points, rows, partners, orbitals):
        self.batches, self.listed, self.points = batches, listed, points
        self.rows, self.partners, self.orbitals = rows, partners, orbitals
        self.weights = -(-3 * batches // 8) * 8
        self.basis = self.weights + -(-batches // 8) * 8
        self.lists = 0
        self.pattern = -(-listed // 8) * 8
        self.meta = self.pattern + -(-partners // 8) * 8
        self.scalar_rows = -(-max(4 * rows, self.meta + 1) // 8) * 8
        self.height = self.basis + self.scalar_rows
        self.slots = 3 * batches * listed
        self.blank, self.trash = self.slots, self.slots + 1
        self.columns = 2 * rows + REACH
        self.units = 2 * batches * listed
        self.empty = (self.blank * 16) << 12 | NONE << 6 | NONE


def pack_kernel(lay, counts, points, weights, lists, pattern, basis, out, held, sems):
    copies = [
        pltpu.make_async_copy(source, target, sems.at[number])
        for number, (source, target) in enumerate(
            zip((counts, points, weights, lists, pattern, basis), held)
        )
    ]
    for copy in copies:
        copy.start()
    out[...] = jnp.zeros_like(out)
    me = lax.axis_index("space")
    for copy in copies:
        copy.wait()
    counts, points, weights, lists, pattern, basis = held
    for t in range(lay.batches):
        out[3 * t : 3 * t + 3, :] = points[t]
    out[lay.weights : lay.weights + lay.batches, :] = weights[...]
    for w in range(lay.rows):
        out[lay.basis + 4 * w : lay.basis + 4 * w + 4, :128] = basis[w].astype(jnp.float32)
    begin = lay.basis + lay.lists
    out[begin : begin + lay.listed, 128 : 128 + lay.batches] = lists[...].astype(jnp.float32)
    begin = lay.basis + lay.pattern
    out[begin : begin + lay.partners, 128 : 128 + lay.rows] = pattern[...].astype(jnp.float32)
    begin = lay.basis + lay.meta
    lane = lax.broadcasted_iota(jnp.int32, (1, 128), 1)
    meta = jnp.where(lane == 0, counts[0], jnp.where(lane == 1, me, 0))
    out[begin : begin + 1, 128:256] = meta.astype(jnp.float32)


class Place:
    def __init__(self, lay):
        self.lay = lay
        self.own = lax.axis_index("space")
        self.pair = self.own ^ 1
        even = self.own % 2 == 0
        self.even = even
        self.far = jnp.where(even, self.own - 1, self.own + 1)
        self.far_first = jnp.where(even, lay.rows - REACH, 0)

    def window(self, raw, outside):
        rows = self.lay.rows
        owner, inner = split(raw, rows)
        far = jnp.where(owner == self.far, 2 * rows + inner, outside)
        return jnp.where(owner == self.own, inner, jnp.where(owner == self.pair, rows + inner, far))


def block_of(lay, pack):
    return pack[lay.basis : lay.basis + lay.scalar_rows, 128:256]


def partner_choice(lay, place, block):
    raw = block[lay.pattern : lay.pattern + 8].astype(jnp.int32)
    turned = place.window(raw, ELSEWHERE).astype(jnp.float32).T
    lane = lax.broadcasted_iota(jnp.int32, (lay.rows, 32), 1).astype(jnp.float32)
    return jnp.concatenate(
        [
            jnp.where(turned[: lay.rows, k : k + 1] == lane, 1.0, 0.0)
            for k in range(1, lay.partners)
        ],
        axis=0,
    ).astype(jnp.bfloat16)


def code_batches(lay, place, g, block, choice, first_row, own_choice, wanted):
    listed, rows = lay.listed, lay.rows
    raw = block.astype(jnp.int32)
    lists = raw[lay.lists : lay.lists + listed]
    window = place.window(lists, NOWHERE)
    lane = lax.broadcasted_iota(jnp.int32, (listed, 128), 1)
    position = lax.broadcasted_iota(jnp.int32, (listed, 128), 0)
    base = (g * lay.batches + lane) * listed
    column = jnp.where(window < 2 * rows, window, window - place.far_first)
    entry = (base + position) * 32 + column

    line = lax.broadcasted_iota(jnp.int32, (32, 128), 0)
    held = jnp.zeros((32, 128), jnp.int32)
    for b in range(listed):
        held = jnp.where(line == window[b : b + 1], b + 1, held)
    there = jnp.where(held[:rows] > 0, 1.0, 0.0).astype(jnp.bfloat16)
    partner_of = lax.dot_general(
        own_choice,
        jnp.concatenate([there] * (lay.partners - 1), axis=0),
        (((0,), (0,)), ((), ())),
        preferred_element_type=jnp.float32,
    )
    partner = jnp.zeros((listed, 128), jnp.float32)
    for w in range(rows, 3 * rows):
        partner = jnp.where(window == w, partner_of[w : w + 1], partner)
    result = jnp.where(wanted(window, partner > 0.5), entry, -1)

    others = jnp.dot(
        choice, held.astype(jnp.float32).astype(jnp.bfloat16), preferred_element_type=jnp.float32
    ).astype(jnp.int32)
    codes = [
        (k * 16 - 1) + others[(k - 1) * rows : k * rows] for k in range(1, lay.partners)
    ]
    one, two, three = [others[(k - 1) * rows : k * rows] > 0 for k in range(1, lay.partners)]
    itself = held[first_row : first_row + rows] - 1
    item_row = first_row + lax.broadcasted_iota(jnp.int32, (rows, 128), 0)
    item_base = (g * lay.batches + lax.broadcasted_iota(jnp.int32, (rows, 128), 1)) * listed
    common = ((item_base + itself) * 16 + item_row) << 12
    first = jnp.where(one, codes[0], jnp.where(two, codes[1], jnp.where(three, codes[2], NONE)))
    more = (one & two) | ((one | two) & three)
    second = jnp.where(one & two, codes[1], codes[2])
    third = jnp.where(one & two & three, codes[2], NONE)
    exists = itself >= 0
    units = (
        jnp.where(exists, common + (itself << 6) + first, -1),
        jnp.where(exists & more, common + (second << 6) + third, -1),
    )
    for number, unit in enumerate(units):
        found = jnp.full((listed, 128), -1, jnp.int32)
        for w in range(rows):
            found = jnp.where(window == first_row + w, unit[w : w + 1], found)
        begin = LANES * (number + 1)
        result = jnp.where(lane < begin, result, pltpu.roll(found, begin, 1))
    begin = LANES * 3
    return jnp.where(lane < begin, result, pltpu.roll(raw[lay.meta : lay.meta + 8], begin, 1))


def list_batches(lay, scalars, begin, entries, units, totals):
    def visit(t, totals):
        entry_total, unit_total = totals
        for b in range(lay.listed):
            entry = scalars[b, begin + t]
            entries[entry_total] = entry
            entry_total = entry_total + jnp.where(entry >= 0, 1, 0)
            for lane in (LANES, 2 * LANES):
                unit = scalars[b, begin + lane + t]
                units[unit_total] = unit
                unit_total = unit_total + jnp.where(unit >= 0, 1, 0)
        return (entry_total, unit_total)

    live = jnp.minimum(scalars[0, begin + 3 * LANES], lay.batches)
    return lax.fori_loop(0, live, visit, totals)


def spread_columns(lay, place, g, pack, columns):
    rows = lay.rows
    table = pack[lay.basis : lay.basis + 4 * rows, :128]
    count, first, owner = rows, 0, (place.own, place.pair, place.far)[g]
    if g == 2:
        count, first = REACH, place.far_first
        table = jnp.where(place.even, table[4 * (rows - count) :], table[: 4 * count])
    table = table.T
    for w in range(count):
        for c in range(4):
            column = table[:, 4 * w + c : 4 * w + c + 1]
            if c == 0:
                column = column + (owner * rows + first + w).astype(jnp.float32)
            if c == 3:
                column = -column
            columns[g * rows + w, c] = jnp.broadcast_to(column, (lay.orbitals, 128))


def spread_points(lay, g, pack, points):
    for t in range(lay.batches):
        points[g * lay.batches + t, 0:3, :] = pack[3 * t : 3 * t + 3, :]


def work_out(lay, entries, total, points, columns, orb):
    for u in range(PAIRED - 1):
        entries[total + u] = lay.trash * 32

    def some(step, carry):
        for u in range(PAIRED):
            slot, column = split(entries[step * PAIRED + u], 32)
            batch = jnp.minimum(split(slot, lay.listed)[0], 3 * lay.batches - 1)
            at = [points[batch, c : c + 1, :] for c in range(3)]
            for begin in range(0, lay.orbitals, 16):
                lines = pl.ds(begin, 16)
                centre = [columns[column, c, lines, :] for c in range(4)]
                for half in range(0, lay.points, 128):
                    distance = (at[0][:, half : half + 128] - centre[0]) ** 2
                    distance = distance + (at[1][:, half : half + 128] - centre[1]) ** 2
                    distance = distance + (at[2][:, half : half + 128] - centre[2]) ** 2
                    result = jnp.exp(centre[3] * distance)
                    orb[slot, lines, half : half + 128] = result.astype(jnp.bfloat16)
        return carry

    lax.fori_loop(0, (total + PAIRED - 1) // PAIRED, some, 0)


def own_kernel(
    lay, pack, orb, columns, units, points, coded, scalars, entries, sem
):
    place = Place(lay)
    block = block_of(lay, pack)
    choice = partner_choice(lay, place, block)
    coded[...] = code_batches(
        lay, place, 0, block, choice, 0, choice, lambda window, partner: window < lay.rows
    )
    copy = pltpu.make_async_copy(coded, scalars, sem)
    copy.start()
    orb[lay.blank] = jnp.zeros(orb.shape[1:], orb.dtype)
    spread_columns(lay, place, 0, pack, columns)
    points[...] = jnp.zeros_like(points)
    spread_points(lay, 0, pack, points)
    copy.wait()
    total, end = list_batches(lay, scalars, 0, entries, units, (jnp.int32(0), jnp.int32(0)))
    units[2 * lay.batches * lay.listed + 1] = end
    work_out(lay, entries, total, points, columns, orb)


def first_kernel(
    lay,
    pack_own,
    pack_pair,
    pack_far,
    density_own,
    density_pair,
    units_given,
    orb_in,
    columns_in,
    part,
    orb,
    columns,
    units,
    points,
    density,
    rho,
    units_own,
    coded,
    scalars,
    entries,
    scalar_sem,
    density_sems,
    units_sem,
):
    rows, listed = lay.rows, lay.listed
    density_copies = [
        pltpu.make_async_copy(source, density.at[pl.ds(g * rows, rows)], density_sems.at[g])
        for g, source in enumerate((density_own, density_pair))
    ]
    for copy in density_copies:
        copy.start()
    units_copy = pltpu.make_async_copy(units_given, units_own, units_sem)
    units_copy.start()
    place = Place(lay)
    blocks = [block_of(lay, pack) for pack in (pack_own, pack_pair, pack_far)]
    own_choice = partner_choice(lay, place, blocks[0])
    pair_choice = partner_choice(lay, place, blocks[1])
    of_far = code_batches(
        lay,
        place,
        2,
        blocks[2],
        own_choice,
        0,
        own_choice,
        lambda window, partner: (window < rows) | partner,
    )
    of_own = code_batches(
        lay,
        place,
        0,
        blocks[0],
        pair_choice,
        rows,
        own_choice,
        lambda window, partner: (window >= rows) & ((window < 2 * rows) | partner),
    )
    lane = lax.broadcasted_iota(jnp.int32, of_far.shape, 1)
    coded[...] = jnp.where(lane < 4 * LANES, of_far, pltpu.roll(of_own, 4 * LANES, 1))
    scalar_copy = pltpu.make_async_copy(coded, scalars, scalar_sem)
    scalar_copy.start()
    spread_columns(lay, place, 1, pack_pair, columns)
    spread_columns(lay, place, 2, pack_far, columns)
    points[...] = jnp.zeros_like(points)
    spread_points(lay, 0, pack_own, points)
    spread_points(lay, 2, pack_far, points)
    rho[...] = jnp.zeros_like(rho)
    scalar_copy.wait()
    totals = (jnp.int32(0), jnp.int32(0))
    totals = list_batches(lay, scalars, 0, entries, units, totals)
    units[4 * lay.batches * listed + 1] = totals[1]
    total, end = list_batches(lay, scalars, 4 * LANES, entries, units, totals)
    work_out(lay, entries, total, points, columns, orb)
    for copy in density_copies:
        copy.wait()
    units_copy.wait()
    shared = units_own[2 * lay.batches * listed + 1]
    end = end + shared

    def fold(step, carry):
        sums = []
        for u in range(UNROLL):
            index = step * UNROLL + u
            word = jnp.where(
                index < shared,
                units_own[jnp.minimum(index, lay.units - 1)],
                units[jnp.maximum(index - shared, 0)],
            )
            word = jnp.where(index < end, word, lay.empty)
            slot, row, (k1, o1), (k2, o2) = decode(lay, word)
            others = jnp.concatenate([orb[o1], orb[o2]], axis=0)
            stored = jnp.concatenate([density[row, k1], density[row, k2]], axis=1)
            folded = jnp.dot(stored, others, preferred_element_type=jnp.float32)
            product = orb[slot].astype(jnp.float32) * folded
            total = product[0:8]
            for begin in range(8, lay.orbitals, 8):
                total = total + product[begin : begin + 8]
            sums.append((split(slot, listed)[0], total))
        for number, total in sums:
            rho[number] = rho[number] + total
        return carry

    lax.fori_loop(0, (end + UNROLL - 1) // UNROLL, fold, 0)
    part[: lay.batches, :] = jnp.sum(rho[: lay.batches], axis=1)
    part[lay.batches :, :] = jnp.sum(rho[2 * lay.batches : 3 * lay.batches], axis=1)


def pair_kernel(
    lay,
    pack_own,
    pack_pair,
    orb_in,
    columns,
    orb,
    units,
    points,
    coded,
    scalars,
    entries,
    sem,
):
    place = Place(lay)
    choice = partner_choice(lay, place, block_of(lay, pack_own))
    block = block_of(lay, pack_pair)
    coded[...] = code_batches(
        lay,
        place,
        1,
        block,
        choice,
        0,
        choice,
        lambda window, partner: (window < lay.rows) | partner,
    )
    copy = pltpu.make_async_copy(coded, scalars, sem)
    copy.start()
    points[...] = jnp.zeros_like(points)
    spread_points(lay, 1, pack_pair, points)
    copy.wait()
    total, end = list_batches(lay, scalars, 0, entries, units, (jnp.int32(0), jnp.int32(0)))
    units[2 * lay.batches * lay.listed + 1] = end
    work_out(lay, entries, total, points, columns, orb)


def total_kernel(lay, part, arrived, units, out):
    out[...] = part[: lay.batches] + arrived[lay.batches :]


def decode(lay, word):
    slot = word >> 16
    row = (word >> 12) & 15
    base = slot & ~(lay.listed - 1)
    partners = []
    for shift in (6, 0):
        inner = (word >> shift) & 15
        partners.append(
            ((word >> (shift + 4)) & 3, jnp.where(inner == NONE, lay.blank, base + inner))
        )
    return slot, row, *partners


def cube_root(x):
    size = jnp.abs(x)
    safe = jnp.where(size > 0.0, size, 1.0)
    root = jnp.exp2(jnp.log2(safe) * (1.0 / 3.0))
    root = root - (root - safe / (root * root)) * (1.0 / 3.0)
    root = jnp.where(size > 0.0, root, 0.0)
    return jnp.where(x < 0.0, -root, root)


def second_kernel(
    lay,
    pack_own,
    pack_pair,
    pack_far,
    part,
    arrived,
    pair_rho,
    orb,
    units_given,
    out,
    potential,
    units_held,
    sems,
):
    copies = [
        pltpu.make_async_copy(source, target, sems.at[number])
        for number, (source, target) in enumerate(zip(units_given, units_held))
    ]
    for copy in copies:
        copy.start()
    packs = (pack_own, pack_pair, pack_far)
    n = lay.batches
    density_values = (part[:n] + arrived[n:], pair_rho[...], part[n:] + arrived[:n])
    potential[...] = jnp.zeros_like(potential)
    for g in range(3):
        weights = packs[g][lay.weights : lay.weights + n, :]
        potential[g * n : (g + 1) * n, :] = -exchange_coef * cube_root(density_values[g]) * weights
    out[...] = jnp.zeros_like(out)
    for copy in copies:
        copy.wait()
    units_own, units_first, units_pair = units_held
    most = 2 * n * lay.listed
    one = units_own[most + 1]
    two = one + units_first[2 * most + 1]
    total = two + units_pair[most + 1]

    def contribute(step, carry):
        for u in range(UNROLL):
            index = step * UNROLL + u
            words = [
                units[jnp.clip(index - begin, 0, lay.units - 1)]
                for units, begin in ((units_own, 0), (units_first, one), (units_pair, two))
            ]
            word = jnp.where(index < one, words[0], jnp.where(index < two, words[1], words[2]))
            word = jnp.where(index < total, word, lay.empty)
            slot, row, (k1, o1), (k2, o2) = decode(lay, word)
            others = jnp.concatenate([orb[o1], orb[o2]], axis=0)
            scale = potential[pl.ds(split(slot, lay.listed)[0], 1), :]
            weighted = (orb[slot].astype(jnp.float32) * scale).astype(jnp.bfloat16)
            contrib = lax.dot_general(
                weighted, others, (((1,), (1,)), ((), ())), preferred_element_type=jnp.float32
            )
            out[row, k1] += contrib[:, : lay.orbitals]
            out[row, k2] += contrib[:, lay.orbitals :]
        return carry

    lax.fori_loop(0, (total + UNROLL - 1) // UNROLL, contribute, 0)


def on_device(counts, points, weights, block_lists, pattern, basis_table, density):
    batches, listed = block_lists.shape
    rows, partners = pattern.shape
    orbitals = basis_table.shape[2]
    lay = Layout(batches, listed, points.shape[2], rows, partners, orbitals)
    devices = lax.axis_size("space")
    in_vmem = pl.BlockSpec(memory_space=VMEM)
    in_smem = pl.BlockSpec(memory_space=SMEM)
    in_hbm = pl.BlockSpec(memory_space=HBM)
    cost = pl.CostEstimate(flops=0, bytes_accessed=16 << 20, transcendentals=0)

    def params(limit=LIMIT):
        return pltpu.CompilerParams(vmem_limit_bytes=limit)

    pair_route = [(i, i ^ 1) for i in range(devices)]
    far_route = [
        (i, i + 1 if i % 2 else i - 1)
        for i in range(devices)
        if 0 <= (i + 1 if i % 2 else i - 1) < devices
    ]

    density_pair = lax.ppermute(density, "space", pair_route)
    inputs = (counts, points, weights, block_lists.T, pattern.T, basis_table)
    pack = pl.pallas_call(
        functools.partial(pack_kernel, lay),
        out_shape=jax.ShapeDtypeStruct((lay.height, lay.points), jnp.float32),
        in_specs=[in_hbm] * 6,
        out_specs=in_vmem,
        scratch_shapes=[
            [SMEM(counts.shape, counts.dtype)] + [VMEM(x.shape, x.dtype) for x in inputs[1:]],
            pltpu.SemaphoreType.DMA((6,)),
        ],
        compiler_params=params(WHOLE),
        name="pack",
    )(*inputs)
    pack_far = lax.ppermute(pack, "space", far_route)
    pack_pair = lax.ppermute(pack, "space", pair_route)

    orb_shape = jax.ShapeDtypeStruct((lay.slots + 2, orbitals, lay.points), jnp.bfloat16)
    columns_shape = jax.ShapeDtypeStruct((lay.columns, 4, orbitals, 128), jnp.float32)
    anywhere = pl.BlockSpec(memory_space=pl.ANY)
    most = 2 * batches * listed

    def units_shape(parts):
        return jax.ShapeDtypeStruct((parts * most + 2,), jnp.int32)

    def scratch(groups):
        return [
            VMEM((listed, 128), jnp.int32),
            SMEM((listed, 128), jnp.int32),
            SMEM((groups * batches * listed + PAIRED,), jnp.int32),
            pltpu.SemaphoreType.DMA(()),
        ]

    points_scratch = VMEM((3 * batches, 8, lay.points), jnp.float32)
    orb, columns, units_own = pl.pallas_call(
        functools.partial(own_kernel, lay),
        out_shape=(orb_shape, columns_shape, units_shape(1)),
        in_specs=[in_vmem],
        out_specs=(in_vmem, in_vmem, in_smem),
        scratch_shapes=[points_scratch, *scratch(1)],
        compiler_params=params(),
        cost_estimate=cost,
        name="first_own",
    )(pack)

    part, orb, columns, units_first = pl.pallas_call(
        functools.partial(first_kernel, lay),
        out_shape=(
            jax.ShapeDtypeStruct((2 * batches, lay.points), jnp.float32),
            orb_shape,
            columns_shape,
            units_shape(2),
        ),
        in_specs=[in_vmem] * 3 + [in_hbm, in_hbm, anywhere, in_vmem, in_vmem],
        out_specs=(in_vmem, in_vmem, in_vmem, in_smem),
        scratch_shapes=[
            points_scratch,
            VMEM((2 * rows, partners, orbitals, orbitals), jnp.bfloat16),
            VMEM((3 * batches + 1, 8, lay.points), jnp.float32),
            SMEM(units_shape(1).shape, jnp.int32),
            *scratch(2),
            pltpu.SemaphoreType.DMA((2,)),
            pltpu.SemaphoreType.DMA(()),
        ],
        input_output_aliases={6: 1, 7: 2},
        compiler_params=params(BUSY),
        cost_estimate=cost,
        name="first",
    )(pack, pack_pair, pack_far, density, density_pair, units_own, orb, columns)

    arrived = lax.ppermute(part, "space", far_route)
    orb, units_pair = pl.pallas_call(
        functools.partial(pair_kernel, lay),
        out_shape=(orb_shape, units_shape(1)),
        in_specs=[in_vmem] * 4,
        out_specs=(in_vmem, in_smem),
        scratch_shapes=[points_scratch, *scratch(1)],
        input_output_aliases={2: 0},
        compiler_params=params(),
        cost_estimate=cost,
        name="first_pair",
    )(pack, pack_pair, orb, columns)
    own_rho = pl.pallas_call(
        functools.partial(total_kernel, lay),
        out_shape=jax.ShapeDtypeStruct((batches, lay.points), jnp.float32),
        in_specs=[in_vmem, in_vmem, anywhere],
        out_specs=in_vmem,
        compiler_params=params(1 << 20),
        name="total",
    )(part, arrived, units_pair)
    pair_rho = lax.ppermute(own_rho, "space", pair_route)

    return pl.pallas_call(
        functools.partial(second_kernel, lay),
        out_shape=jax.ShapeDtypeStruct(density.shape, jnp.float32),
        in_specs=[in_vmem] * 7 + [[anywhere] * 3],
        out_specs=in_vmem,
        scratch_shapes=[
            VMEM((-(-(3 * batches + 1) // 8) * 8, lay.points), jnp.float32),
            [SMEM(units_shape(parts).shape, jnp.int32) for parts in (1, 2, 1)],
            pltpu.SemaphoreType.DMA((3,)),
        ],
        compiler_params=params(),
        name="second",
    )(
        pack,
        pack_pair,
        pack_far,
        part,
        arrived,
        pair_rho,
        orb,
        [units_own, units_first, units_pair],
    )


def solution(mesh):
    in_specs = (
        P(("parts", "space")),
        P(("parts", "space"), None, None),
        P(("parts", "space"), None),
        P(("parts", "space"), None),
        P(("parts", "space"), None),
        P(("parts", "space"), None, None),
        P(("parts", "space"), None, None, None),
    )
    out_specs = P(("parts", "space"), None, None, None)
    return jax.shard_map(
        on_device, mesh=mesh, in_specs=in_specs, out_specs=out_specs, check_vma=False
    )
```

```python
import functools
import math

import jax
import jax.numpy as jnp
from jax import lax
from jax.experimental import pallas as pl
from jax.experimental.pallas import tpu as pltpu
from jax.sharding import PartitionSpec as P

exchange_coef = (3.0 / math.pi) ** (1.0 / 3.0)
VMEM = pltpu.VMEM
SMEM = pltpu.SMEM
HBM = pltpu.HBM
LIMIT = 12 << 20
WHOLE = 63 << 20
BUSY = 12 << 20
REACH = 3
UNROLL = 16
PAIRED = 2
LANES = 16
NOWHERE, ELSEWHERE = 31, 30
NONE = 15


def split(value, size):
    if size & (size - 1):
        quotient = value // size
        return quotient, value - quotient * size
    return lax.shift_right_logical(value, size.bit_length() - 1), value & (size - 1)


class Layout:
    def __init__(self, batches, listed, points, rows, partners, orbitals):
        self.batches, self.listed, self.points = batches, listed, points
        self.rows, self.partners, self.orbitals = rows, partners, orbitals
        self.weights = -(-3 * batches // 8) * 8
        self.basis = self.weights + -(-batches // 8) * 8
        self.lists = 0
        self.pattern = -(-listed // 8) * 8
        self.meta = self.pattern + -(-partners // 8) * 8
        self.scalar_rows = -(-max(4 * rows, self.meta + 1) // 8) * 8
        self.height = self.basis + self.scalar_rows
        self.slots = 3 * batches * listed
        self.blank, self.trash = self.slots, self.slots + 1
        self.columns = 2 * rows + REACH
        self.units = 2 * batches * listed
        self.empty = (self.blank * 16) << 12 | NONE << 6 | NONE


def pack_kernel(lay, counts, points, weights, lists, pattern, basis, out, held, sems):
    copies = [
        pltpu.make_async_copy(source, target, sems.at[number])
        for number, (source, target) in enumerate(
            zip((counts, points, weights, lists, pattern, basis), held)
        )
    ]
    for copy in copies:
        copy.start()
    out[...] = jnp.zeros_like(out)
    me = lax.axis_index("space")
    for copy in copies:
        copy.wait()
    counts, points, weights, lists, pattern, basis = held
    for t in range(lay.batches):
        out[3 * t : 3 * t + 3, :] = points[t]
    out[lay.weights : lay.weights + lay.batches, :] = weights[...]
    for w in range(lay.rows):
        out[lay.basis + 4 * w : lay.basis + 4 * w + 4, :128] = basis[w].astype(jnp.float32)
    begin = lay.basis + lay.lists
    out[begin : begin + lay.listed, 128 : 128 + lay.batches] = lists[...].astype(jnp.float32)
    begin = lay.basis + lay.pattern
    out[begin : begin + lay.partners, 128 : 128 + lay.rows] = pattern[...].astype(jnp.float32)
    begin = lay.basis + lay.meta
    lane = lax.broadcasted_iota(jnp.int32, (1, 128), 1)
    meta = jnp.where(lane == 0, counts[0], jnp.where(lane == 1, me, 0))
    out[begin : begin + 1, 128:256] = meta.astype(jnp.float32)


class Place:
    def __init__(self, lay):
        self.lay = lay
        self.own = lax.axis_index("space")
        self.pair = self.own ^ 1
        even = self.own % 2 == 0
        self.even = even
        self.far = jnp.where(even, self.own - 1, self.own + 1)
        self.far_first = jnp.where(even, lay.rows - REACH, 0)

    def window(self, raw, outside):
        rows = self.lay.rows
        owner, inner = split(raw, rows)
        far = jnp.where(owner == self.far, 2 * rows + inner, outside)
        return jnp.where(owner == self.own, inner, jnp.where(owner == self.pair, rows + inner, far))


def block_of(lay, pack):
    return pack[lay.basis : lay.basis + lay.scalar_rows, 128:256]


def partner_choice(lay, place, block):
    raw = block[lay.pattern : lay.pattern + 8].astype(jnp.int32)
    turned = place.window(raw, ELSEWHERE).astype(jnp.float32).T
    lane = lax.broadcasted_iota(jnp.int32, (lay.rows, 32), 1).astype(jnp.float32)
    return jnp.concatenate(
        [
            jnp.where(turned[: lay.rows, k : k + 1] == lane, 1.0, 0.0)
            for k in range(1, lay.partners)
        ],
        axis=0,
    ).astype(jnp.bfloat16)


def code_batches(lay, place, g, block, choice, first_row, own_choice, wanted):
    listed, rows = lay.listed, lay.rows
    raw = block.astype(jnp.int32)
    lists = raw[lay.lists : lay.lists + listed]
    window = place.window(lists, NOWHERE)
    lane = lax.broadcasted_iota(jnp.int32, (listed, 128), 1)
    position = lax.broadcasted_iota(jnp.int32, (listed, 128), 0)
    base = (g * lay.batches + lane) * listed
    column = jnp.where(window < 2 * rows, window, window - place.far_first)
    entry = (base + position) * 32 + column

    line = lax.broadcasted_iota(jnp.int32, (32, 128), 0)
    held = jnp.zeros((32, 128), jnp.int32)
    for b in range(listed):
        held = jnp.where(line == window[b : b + 1], b + 1, held)
    there = jnp.where(held[:rows] > 0, 1.0, 0.0).astype(jnp.bfloat16)
    partner_of = lax.dot_general(
        own_choice,
        jnp.concatenate([there] * (lay.partners - 1), axis=0),
        (((0,), (0,)), ((), ())),
        preferred_element_type=jnp.float32,
    )
    partner = jnp.zeros((listed, 128), jnp.float32)
    for w in range(rows, 3 * rows):
        partner = jnp.where(window == w, partner_of[w : w + 1], partner)
    result = jnp.where(wanted(window, partner > 0.5), entry, -1)

    others = jnp.dot(
        choice, held.astype(jnp.float32).astype(jnp.bfloat16), preferred_element_type=jnp.float32
    ).astype(jnp.int32)
    codes = [
        (k * 16 - 1) + others[(k - 1) * rows : k * rows] for k in range(1, lay.partners)
    ]
    one, two, three = [others[(k - 1) * rows : k * rows] > 0 for k in range(1, lay.partners)]
    itself = held[first_row : first_row + rows] - 1
    item_row = first_row + lax.broadcasted_iota(jnp.int32, (rows, 128), 0)
    item_base = (g * lay.batches + lax.broadcasted_iota(jnp.int32, (rows, 128), 1)) * listed
    common = ((item_base + itself) * 16 + item_row) << 12
    first = jnp.where(one, codes[0], jnp.where(two, codes[1], jnp.where(three, codes[2], NONE)))
    more = (one & two) | ((one | two) & three)
    second = jnp.where(one & two, codes[1], codes[2])
    third = jnp.where(one & two & three, codes[2], NONE)
    exists = itself >= 0
    units = (
        jnp.where(exists, common + (itself << 6) + first, -1),
        jnp.where(exists & more, common + (second << 6) + third, -1),
    )
    for number, unit in enumerate(units):
        found = jnp.full((listed, 128), -1, jnp.int32)
        for w in range(rows):
            found = jnp.where(window == first_row + w, unit[w : w + 1], found)
        begin = LANES * (number + 1)
        result = jnp.where(lane < begin, result, pltpu.roll(found, begin, 1))
    begin = LANES * 3
    return jnp.where(lane < begin, result, pltpu.roll(raw[lay.meta : lay.meta + 8], begin, 1))


def live_batches(lay, scalars, begin):
    return jnp.minimum(scalars[0, begin + 3 * LANES], lay.batches)


def list_entries(lay, scalars, begin, entries, total):
    def visit(t, total):
        for b in range(lay.listed):
            entry = scalars[b, begin + t]
            entries[total] = entry
            total = total + jnp.where(entry >= 0, 1, 0)
        return total

    return lax.fori_loop(0, live_batches(lay, scalars, begin), visit, total)


def list_units(lay, scalars, begin, t, units, total):
    live = t < live_batches(lay, scalars, begin)
    t = jnp.minimum(t, lay.batches - 1)
    for b in range(lay.listed):
        for lane in (LANES, 2 * LANES):
            unit = scalars[b, begin + lane + t]
            units[total] = unit
            total = total + jnp.where(live & (unit >= 0), 1, 0)
    return total


def spread_columns(lay, place, g, pack, columns):
    rows = lay.rows
    table = pack[lay.basis : lay.basis + 4 * rows, :128]
    count, first, owner = rows, 0, (place.own, place.pair, place.far)[g]
    if g == 2:
        count, first = REACH, place.far_first
        table = jnp.where(place.even, table[4 * (rows - count) :], table[: 4 * count])
    table = table.T
    for w in range(count):
        for c in range(4):
            column = table[:, 4 * w + c : 4 * w + c + 1]
            if c == 0:
                column = column + (owner * rows + first + w).astype(jnp.float32)
            if c == 3:
                column = -column
            columns[g * rows + w, c] = jnp.broadcast_to(column, (lay.orbitals, 128))


def spread_points(lay, g, pack, points):
    for t in range(lay.batches):
        points[g * lay.batches + t, 0:3, :] = pack[3 * t : 3 * t + 3, :]


def work_out(lay, entries, total, points, columns, orb, scalars, groups, units):
    for u in range(PAIRED):
        entries[total + u] = lay.trash * 32
    steps = (total + PAIRED - 1) // PAIRED
    for begin in groups:
        steps = jnp.maximum(steps, live_batches(lay, scalars, begin))

    def some(step, ends):
        for u in range(PAIRED):
            index = jnp.minimum(step * PAIRED + u, total)
            slot, column = split(entries[index], 32)
            batch = jnp.minimum(split(slot, lay.listed)[0], 3 * lay.batches - 1)
            at = [points[batch, c : c + 1, :] for c in range(3)]
            for begin in range(0, lay.orbitals, 16):
                lines = pl.ds(begin, 16)
                centre = [columns[column, c, lines, :] for c in range(4)]
                for half in range(0, lay.points, 128):
                    distance = (at[0][:, half : half + 128] - centre[0]) ** 2
                    distance = distance + (at[1][:, half : half + 128] - centre[1]) ** 2
                    distance = distance + (at[2][:, half : half + 128] - centre[2]) ** 2
                    result = jnp.exp(centre[3] * distance)
                    orb[slot, lines, half : half + 128] = result.astype(jnp.bfloat16)
        return [
            list_units(lay, scalars, begin, step, target, end)
            for begin, target, end in zip(groups, units, ends)
        ]

    return lax.fori_loop(0, steps, some, [jnp.int32(0)] * len(groups))


def own_kernel(
    lay, pack, orb, columns, units, points, coded, scalars, entries, sem
):
    place = Place(lay)
    block = block_of(lay, pack)
    choice = partner_choice(lay, place, block)
    coded[...] = code_batches(
        lay, place, 0, block, choice, 0, choice, lambda window, partner: window < lay.rows
    )
    copy = pltpu.make_async_copy(coded, scalars, sem)
    copy.start()
    orb[lay.blank] = jnp.zeros(orb.shape[1:], orb.dtype)
    spread_columns(lay, place, 0, pack, columns)
    points[...] = jnp.zeros_like(points)
    spread_points(lay, 0, pack, points)
    copy.wait()
    total = list_entries(lay, scalars, 0, entries, jnp.int32(0))
    (end,) = work_out(lay, entries, total, points, columns, orb, scalars, (0,), (units,))
    units[lay.units + 1] = end


def first_kernel(
    lay,
    pack_own,
    pack_pair,
    pack_far,
    density_own,
    density_pair,
    units_given,
    orb_in,
    columns_in,
    part,
    orb,
    columns,
    units,
    points,
    density,
    rho,
    units_own,
    units_rest,
    coded,
    scalars,
    entries,
    scalar_sem,
    density_sems,
    units_sem,
):
    rows, listed = lay.rows, lay.listed
    density_copies = [
        pltpu.make_async_copy(source, density.at[pl.ds(g * rows, rows)], density_sems.at[g])
        for g, source in enumerate((density_own, density_pair))
    ]
    for copy in density_copies:
        copy.start()
    units_copy = pltpu.make_async_copy(units_given, units_own, units_sem)
    units_copy.start()
    place = Place(lay)
    blocks = [block_of(lay, pack) for pack in (pack_own, pack_pair, pack_far)]
    own_choice = partner_choice(lay, place, blocks[0])
    pair_choice = partner_choice(lay, place, blocks[1])
    of_far = code_batches(
        lay,
        place,
        2,
        blocks[2],
        own_choice,
        0,
        own_choice,
        lambda window, partner: (window < rows) | partner,
    )
    of_own = code_batches(
        lay,
        place,
        0,
        blocks[0],
        pair_choice,
        rows,
        own_choice,
        lambda window, partner: (window >= rows) & ((window < 2 * rows) | partner),
    )
    lane = lax.broadcasted_iota(jnp.int32, of_far.shape, 1)
    coded[...] = jnp.where(lane < 4 * LANES, of_far, pltpu.roll(of_own, 4 * LANES, 1))
    scalar_copy = pltpu.make_async_copy(coded, scalars, scalar_sem)
    scalar_copy.start()
    spread_columns(lay, place, 1, pack_pair, columns)
    spread_columns(lay, place, 2, pack_far, columns)
    points[...] = jnp.zeros_like(points)
    spread_points(lay, 0, pack_own, points)
    spread_points(lay, 2, pack_far, points)
    rho[...] = jnp.zeros_like(rho)
    scalar_copy.wait()
    total = list_entries(lay, scalars, 0, entries, jnp.int32(0))
    total = list_entries(lay, scalars, 4 * LANES, entries, total)
    ends = work_out(
        lay, entries, total, points, columns, orb, scalars, (0, 4 * LANES), (units, units_rest)
    )
    units[lay.units + 1] = ends[0]
    for copy in density_copies:
        copy.wait()
    units_copy.wait()
    one = units_own[lay.units + 1]
    two = one + ends[0]
    end = two + ends[1]

    def fold(step, carry):
        sums = []
        for u in range(UNROLL):
            index = step * UNROLL + u
            word = pick(
                lay, index, ((units_own, 0), (units, one), (units_rest, two)), end
            )
            slot, row, (k1, o1), (k2, o2) = decode(lay, word)
            others = jnp.concatenate([orb[o1], orb[o2]], axis=0)
            stored = jnp.concatenate([density[row, k1], density[row, k2]], axis=1)
            folded = jnp.dot(stored, others, preferred_element_type=jnp.float32)
            product = orb[slot].astype(jnp.float32) * folded
            total = product[0:8]
            for begin in range(8, lay.orbitals, 8):
                total = total + product[begin : begin + 8]
            sums.append((split(slot, listed)[0], total))
        for number, total in sums:
            rho[number] = rho[number] + total
        return carry

    lax.fori_loop(0, (end + UNROLL - 1) // UNROLL, fold, 0)
    part[: lay.batches, :] = jnp.sum(rho[: lay.batches], axis=1)
    part[lay.batches :, :] = jnp.sum(rho[2 * lay.batches : 3 * lay.batches], axis=1)


def pair_kernel(
    lay,
    pack_own,
    pack_pair,
    orb_in,
    columns,
    orb,
    units,
    points,
    coded,
    scalars,
    entries,
    sem,
):
    place = Place(lay)
    choice = partner_choice(lay, place, block_of(lay, pack_own))
    block = block_of(lay, pack_pair)
    coded[...] = code_batches(
        lay,
        place,
        1,
        block,
        choice,
        0,
        choice,
        lambda window, partner: (window < lay.rows) | partner,
    )
    copy = pltpu.make_async_copy(coded, scalars, sem)
    copy.start()
    points[...] = jnp.zeros_like(points)
    spread_points(lay, 1, pack_pair, points)
    copy.wait()
    total = list_entries(lay, scalars, 0, entries, jnp.int32(0))
    (end,) = work_out(lay, entries, total, points, columns, orb, scalars, (0,), (units,))
    units[lay.units + 1] = end


def total_kernel(lay, part, arrived, units, out):
    out[...] = part[: lay.batches] + arrived[lay.batches :]


def pick(lay, index, lists, total):
    word, end = jnp.int32(lay.empty), total
    for units, begin in reversed(lists):
        word = jnp.where(index < end, units[jnp.clip(index - begin, 0, lay.units - 1)], word)
        end = begin
    return word


def decode(lay, word):
    slot = word >> 16
    row = (word >> 12) & 15
    base = slot & ~(lay.listed - 1)
    partners = []
    for shift in (6, 0):
        inner = (word >> shift) & 15
        partners.append(
            ((word >> (shift + 4)) & 3, jnp.where(inner == NONE, lay.blank, base + inner))
        )
    return slot, row, *partners


def cube_root(x):
    size = jnp.abs(x)
    safe = jnp.where(size > 0.0, size, 1.0)
    root = jnp.exp2(jnp.log2(safe) * (1.0 / 3.0))
    root = root - (root - safe / (root * root)) * (1.0 / 3.0)
    root = jnp.where(size > 0.0, root, 0.0)
    return jnp.where(x < 0.0, -root, root)


def second_kernel(
    lay,
    pack_own,
    pack_pair,
    pack_far,
    part,
    arrived,
    pair_rho,
    orb,
    units_given,
    out,
    potential,
    units_held,
    sems,
):
    copies = [
        pltpu.make_async_copy(source, target, sems.at[number])
        for number, (source, target) in enumerate(zip(units_given, units_held))
    ]
    for copy in copies:
        copy.start()
    packs = (pack_own, pack_pair, pack_far)
    n = lay.batches
    density_values = (part[:n] + arrived[n:], pair_rho[...], part[n:] + arrived[:n])
    potential[...] = jnp.zeros_like(potential)
    for g in range(3):
        weights = packs[g][lay.weights : lay.weights + n, :]
        potential[g * n : (g + 1) * n, :] = -exchange_coef * cube_root(density_values[g]) * weights
    out[...] = jnp.zeros_like(out)
    for copy in copies:
        copy.wait()
    units_own, units_first, units_pair = units_held
    one = units_own[lay.units + 1]
    two = one + units_first[lay.units + 1]
    total = two + units_pair[lay.units + 1]

    def contribute(step, carry):
        for u in range(UNROLL):
            index = step * UNROLL + u
            word = pick(
                lay, index, ((units_own, 0), (units_first, one), (units_pair, two)), total
            )
            slot, row, (k1, o1), (k2, o2) = decode(lay, word)
            others = jnp.concatenate([orb[o1], orb[o2]], axis=0)
            scale = potential[pl.ds(split(slot, lay.listed)[0], 1), :]
            weighted = (orb[slot].astype(jnp.float32) * scale).astype(jnp.bfloat16)
            contrib = lax.dot_general(
                weighted, others, (((1,), (1,)), ((), ())), preferred_element_type=jnp.float32
            )
            out[row, k1] += contrib[:, : lay.orbitals]
            out[row, k2] += contrib[:, lay.orbitals :]
        return carry

    lax.fori_loop(0, (total + UNROLL - 1) // UNROLL, contribute, 0)


def on_device(counts, points, weights, block_lists, pattern, basis_table, density):
    batches, listed = block_lists.shape
    rows, partners = pattern.shape
    orbitals = basis_table.shape[2]
    lay = Layout(batches, listed, points.shape[2], rows, partners, orbitals)
    devices = lax.axis_size("space")
    in_vmem = pl.BlockSpec(memory_space=VMEM)
    in_smem = pl.BlockSpec(memory_space=SMEM)
    in_hbm = pl.BlockSpec(memory_space=HBM)
    cost = pl.CostEstimate(flops=0, bytes_accessed=16 << 20, transcendentals=0)

    def params(limit=LIMIT):
        return pltpu.CompilerParams(vmem_limit_bytes=limit)

    pair_route = [(i, i ^ 1) for i in range(devices)]
    far_route = [
        (i, i + 1 if i % 2 else i - 1)
        for i in range(devices)
        if 0 <= (i + 1 if i % 2 else i - 1) < devices
    ]

    inputs = (counts, points, weights, block_lists.T, pattern.T, basis_table)
    pack = pl.pallas_call(
        functools.partial(pack_kernel, lay),
        out_shape=jax.ShapeDtypeStruct((lay.height, lay.points), jnp.float32),
        in_specs=[in_hbm] * 6,
        out_specs=in_vmem,
        scratch_shapes=[
            [SMEM(counts.shape, counts.dtype)] + [VMEM(x.shape, x.dtype) for x in inputs[1:]],
            pltpu.SemaphoreType.DMA((6,)),
        ],
        compiler_params=params(WHOLE),
        name="pack",
    )(*inputs)
    pack_far = lax.ppermute(pack, "space", far_route)
    pack_pair = lax.ppermute(pack, "space", pair_route)
    pack, density = lax.optimization_barrier((pack, density))
    density_pair = lax.ppermute(density, "space", pair_route)

    orb_shape = jax.ShapeDtypeStruct((lay.slots + 2, orbitals, lay.points), jnp.bfloat16)
    columns_shape = jax.ShapeDtypeStruct((lay.columns, 4, orbitals, 128), jnp.float32)
    anywhere = pl.BlockSpec(memory_space=pl.ANY)
    units_shape = jax.ShapeDtypeStruct((lay.units + 2,), jnp.int32)

    def scratch(groups):
        return [
            VMEM((listed, 128), jnp.int32),
            SMEM((listed, 128), jnp.int32),
            SMEM((groups * batches * listed + PAIRED,), jnp.int32),
            pltpu.SemaphoreType.DMA(()),
        ]

    points_scratch = VMEM((3 * batches, 8, lay.points), jnp.float32)
    orb, columns, units_own = pl.pallas_call(
        functools.partial(own_kernel, lay),
        out_shape=(orb_shape, columns_shape, units_shape),
        in_specs=[in_vmem],
        out_specs=(in_vmem, in_vmem, in_smem),
        scratch_shapes=[points_scratch, *scratch(1)],
        compiler_params=params(),
        cost_estimate=cost,
        name="first_own",
    )(pack)

    part, orb, columns, units_first = pl.pallas_call(
        functools.partial(first_kernel, lay),
        out_shape=(
            jax.ShapeDtypeStruct((2 * batches, lay.points), jnp.float32),
            orb_shape,
            columns_shape,
            units_shape,
        ),
        in_specs=[in_vmem] * 3 + [in_hbm, in_hbm, anywhere, in_vmem, in_vmem],
        out_specs=(in_vmem, in_vmem, in_vmem, in_smem),
        scratch_shapes=[
            points_scratch,
            VMEM((2 * rows, partners, orbitals, orbitals), jnp.bfloat16),
            VMEM((3 * batches + 1, 8, lay.points), jnp.float32),
            SMEM(units_shape.shape, jnp.int32),
            SMEM(units_shape.shape, jnp.int32),
            *scratch(2),
            pltpu.SemaphoreType.DMA((2,)),
            pltpu.SemaphoreType.DMA(()),
        ],
        input_output_aliases={6: 1, 7: 2},
        compiler_params=params(BUSY),
        cost_estimate=cost,
        name="first",
    )(pack, pack_pair, pack_far, density, density_pair, units_own, orb, columns)

    arrived = lax.ppermute(part, "space", far_route)
    orb, units_pair = pl.pallas_call(
        functools.partial(pair_kernel, lay),
        out_shape=(orb_shape, units_shape),
        in_specs=[in_vmem] * 4,
        out_specs=(in_vmem, in_smem),
        scratch_shapes=[points_scratch, *scratch(1)],
        input_output_aliases={2: 0},
        compiler_params=params(),
        cost_estimate=cost,
        name="first_pair",
    )(pack, pack_pair, orb, columns)
    own_rho = pl.pallas_call(
        functools.partial(total_kernel, lay),
        out_shape=jax.ShapeDtypeStruct((batches, lay.points), jnp.float32),
        in_specs=[in_vmem, in_vmem, anywhere],
        out_specs=in_vmem,
        compiler_params=params(1 << 20),
        name="total",
    )(part, arrived, units_pair)
    pair_rho = lax.ppermute(own_rho, "space", pair_route)

    return pl.pallas_call(
        functools.partial(second_kernel, lay),
        out_shape=jax.ShapeDtypeStruct(density.shape, jnp.float32),
        in_specs=[in_vmem] * 7 + [[anywhere] * 3],
        out_specs=in_vmem,
        scratch_shapes=[
            VMEM((-(-(3 * batches + 1) // 8) * 8, lay.points), jnp.float32),
            [SMEM(units_shape.shape, jnp.int32)] * 3,
            pltpu.SemaphoreType.DMA((3,)),
        ],
        compiler_params=params(),
        name="second",
    )(
        pack,
        pack_pair,
        pack_far,
        part,
        arrived,
        pair_rho,
        orb,
        [units_own, units_first, units_pair],
    )


def solution(mesh):
    in_specs = (
        P(("parts", "space")),
        P(("parts", "space"), None, None),
        P(("parts", "space"), None),
        P(("parts", "space"), None),
        P(("parts", "space"), None),
        P(("parts", "space"), None, None),
        P(("parts", "space"), None, None, None),
    )
    out_specs = P(("parts", "space"), None, None, None)
    return jax.shard_map(
        on_device, mesh=mesh, in_specs=in_specs, out_specs=out_specs, check_vma=False
    )
```

```python
import functools
import math

import jax
import jax.numpy as jnp
from jax import lax
from jax.experimental import pallas as pl
from jax.experimental.pallas import tpu as pltpu
from jax.sharding import PartitionSpec as P

exchange_coef = (3.0 / math.pi) ** (1.0 / 3.0)
VMEM = pltpu.VMEM
SMEM = pltpu.SMEM
HBM = pltpu.HBM
LIMIT = 12 << 20
WHOLE = 63 << 20
BUSY = 12 << 20
REACH = 3
UNROLL = 16
PAIRED = 2
LANES = 16
NOWHERE, ELSEWHERE = 31, 30
NONE = 15


def split(value, size):
    if size & (size - 1):
        quotient = value // size
        return quotient, value - quotient * size
    return lax.shift_right_logical(value, size.bit_length() - 1), value & (size - 1)


class Layout:
    def __init__(self, batches, listed, points, rows, partners, orbitals):
        self.batches, self.listed, self.points = batches, listed, points
        self.rows, self.partners, self.orbitals = rows, partners, orbitals
        self.weights = -(-3 * batches // 8) * 8
        self.basis = self.weights + -(-batches // 8) * 8
        self.lists = 0
        self.pattern = -(-listed // 8) * 8
        self.meta = self.pattern + -(-partners // 8) * 8
        self.scalar_rows = -(-max(4 * rows, self.meta + 1) // 8) * 8
        self.height = self.basis + self.scalar_rows
        self.slots = 3 * batches * listed
        self.blank, self.trash = self.slots, self.slots + 1
        self.columns = 2 * rows + REACH
        self.units = 2 * batches * listed
        self.empty = (self.blank * 16) << 12 | NONE << 6 | NONE


def pack_kernel(lay, counts, points, weights, lists, pattern, basis, out, held, sems):
    copies = [
        pltpu.make_async_copy(source, target, sems.at[number])
        for number, (source, target) in enumerate(
            zip((counts, points, weights, lists, pattern, basis), held)
        )
    ]
    for copy in copies:
        copy.start()
    out[...] = jnp.zeros_like(out)
    me = lax.axis_index("space")
    for copy in copies:
        copy.wait()
    counts, points, weights, lists, pattern, basis = held
    for t in range(lay.batches):
        out[3 * t : 3 * t + 3, :] = points[t]
    out[lay.weights : lay.weights + lay.batches, :] = weights[...]
    for w in range(lay.rows):
        out[lay.basis + 4 * w : lay.basis + 4 * w + 4, :128] = basis[w].astype(jnp.float32)
    begin = lay.basis + lay.lists
    out[begin : begin + lay.listed, 128 : 128 + lay.batches] = lists[...].astype(jnp.float32)
    begin = lay.basis + lay.pattern
    out[begin : begin + lay.partners, 128 : 128 + lay.rows] = pattern[...].astype(jnp.float32)
    begin = lay.basis + lay.meta
    lane = lax.broadcasted_iota(jnp.int32, (1, 128), 1)
    meta = jnp.where(lane == 0, counts[0], jnp.where(lane == 1, me, 0))
    out[begin : begin + 1, 128:256] = meta.astype(jnp.float32)


class Place:
    def __init__(self, lay):
        self.lay = lay
        self.own = lax.axis_index("space")
        self.pair = self.own ^ 1
        even = self.own % 2 == 0
        self.even = even
        self.far = jnp.where(even, self.own - 1, self.own + 1)
        self.far_first = jnp.where(even, lay.rows - REACH, 0)

    def window(self, raw, outside):
        rows = self.lay.rows
        owner, inner = split(raw, rows)
        far = jnp.where(owner == self.far, 2 * rows + inner, outside)
        return jnp.where(owner == self.own, inner, jnp.where(owner == self.pair, rows + inner, far))


def block_of(lay, pack):
    return pack[lay.basis : lay.basis + lay.scalar_rows, 128:256]


def partner_choice(lay, place, block):
    raw = block[lay.pattern : lay.pattern + 8].astype(jnp.int32)
    turned = place.window(raw, ELSEWHERE).astype(jnp.float32).T
    lane = lax.broadcasted_iota(jnp.int32, (lay.rows, 32), 1).astype(jnp.float32)
    return jnp.concatenate(
        [
            jnp.where(turned[: lay.rows, k : k + 1] == lane, 1.0, 0.0)
            for k in range(1, lay.partners)
        ],
        axis=0,
    ).astype(jnp.bfloat16)


def code_batches(lay, place, g, block, choice, first_row, own_choice, wanted):
    listed, rows = lay.listed, lay.rows
    raw = block.astype(jnp.int32)
    lists = raw[lay.lists : lay.lists + listed]
    window = place.window(lists, NOWHERE)
    lane = lax.broadcasted_iota(jnp.int32, (listed, 128), 1)
    position = lax.broadcasted_iota(jnp.int32, (listed, 128), 0)
    base = (g * lay.batches + lane) * listed
    column = jnp.where(window < 2 * rows, window, window - place.far_first)
    entry = (base + position) * 32 + column

    line = lax.broadcasted_iota(jnp.int32, (32, 128), 0)
    held = jnp.zeros((32, 128), jnp.int32)
    for b in range(listed):
        held = jnp.where(line == window[b : b + 1], b + 1, held)
    there = jnp.where(held[:rows] > 0, 1.0, 0.0).astype(jnp.bfloat16)
    partner_of = lax.dot_general(
        own_choice,
        jnp.concatenate([there] * (lay.partners - 1), axis=0),
        (((0,), (0,)), ((), ())),
        preferred_element_type=jnp.float32,
    )
    partner = jnp.zeros((listed, 128), jnp.float32)
    for w in range(rows, 3 * rows):
        partner = jnp.where(window == w, partner_of[w : w + 1], partner)
    result = jnp.where(wanted(window, partner > 0.5), entry, -1)

    others = jnp.dot(
        choice, held.astype(jnp.float32).astype(jnp.bfloat16), preferred_element_type=jnp.float32
    ).astype(jnp.int32)
    codes = [
        (k * 16 - 1) + others[(k - 1) * rows : k * rows] for k in range(1, lay.partners)
    ]
    one, two, three = [others[(k - 1) * rows : k * rows] > 0 for k in range(1, lay.partners)]
    itself = held[first_row : first_row + rows] - 1
    item_row = first_row + lax.broadcasted_iota(jnp.int32, (rows, 128), 0)
    item_base = (g * lay.batches + lax.broadcasted_iota(jnp.int32, (rows, 128), 1)) * listed
    common = ((item_base + itself) * 16 + item_row) << 12
    first = jnp.where(one, codes[0], jnp.where(two, codes[1], jnp.where(three, codes[2], NONE)))
    more = (one & two) | ((one | two) & three)
    second = jnp.where(one & two, codes[1], codes[2])
    third = jnp.where(one & two & three, codes[2], NONE)
    exists = itself >= 0
    units = (
        jnp.where(exists, common + (itself << 6) + first, -1),
        jnp.where(exists & more, common + (second << 6) + third, -1),
    )
    for number, unit in enumerate(units):
        found = jnp.full((listed, 128), -1, jnp.int32)
        for w in range(rows):
            found = jnp.where(window == first_row + w, unit[w : w + 1], found)
        begin = LANES * (number + 1)
        result = jnp.where(lane < begin, result, pltpu.roll(found, begin, 1))
    begin = LANES * 3
    return jnp.where(lane < begin, result, pltpu.roll(raw[lay.meta : lay.meta + 8], begin, 1))


def live_batches(lay, scalars, begin):
    return jnp.minimum(scalars[0, begin + 3 * LANES], lay.batches)


def list_entries(lay, scalars, begin, entries, total):
    def visit(t, total):
        for entry in [scalars[b, begin + t] for b in range(lay.listed)]:
            entries[total] = entry
            total = total + jnp.where(entry >= 0, 1, 0)
        return total

    return lax.fori_loop(0, live_batches(lay, scalars, begin), visit, total)


def list_units(lay, scalars, begin, t, units, total):
    live = t < live_batches(lay, scalars, begin)
    t = jnp.minimum(t, lay.batches - 1)
    found = [
        scalars[b, begin + lane + t] for b in range(lay.listed) for lane in (LANES, 2 * LANES)
    ]
    for unit in found:
        units[total] = unit
        total = total + jnp.where(live & (unit >= 0), 1, 0)
    return total


def spread_columns(lay, place, g, pack, columns):
    rows = lay.rows
    table = pack[lay.basis : lay.basis + 4 * rows, :128]
    count, first, owner = rows, 0, (place.own, place.pair, place.far)[g]
    if g == 2:
        count, first = REACH, place.far_first
        table = jnp.where(place.even, table[4 * (rows - count) :], table[: 4 * count])
    table = table.T
    for w in range(count):
        for c in range(4):
            column = table[:, 4 * w + c : 4 * w + c + 1]
            if c == 0:
                column = column + (owner * rows + first + w).astype(jnp.float32)
            if c == 3:
                column = -column
            columns[g * rows + w, c] = jnp.broadcast_to(column, (lay.orbitals, 128))


def spread_points(lay, g, pack, points):
    for t in range(lay.batches):
        points[g * lay.batches + t, 0:3, :] = pack[3 * t : 3 * t + 3, :]


def work_out(lay, entries, total, points, columns, orb, scalars, groups, units):
    for u in range(PAIRED):
        entries[total + u] = lay.trash * 32
    steps = (total + PAIRED - 1) // PAIRED
    for begin in groups:
        steps = jnp.maximum(steps, live_batches(lay, scalars, begin))

    def some(step, ends):
        for u in range(PAIRED):
            index = jnp.minimum(step * PAIRED + u, total)
            slot, column = split(entries[index], 32)
            batch = jnp.minimum(split(slot, lay.listed)[0], 3 * lay.batches - 1)
            at = [points[batch, c : c + 1, :] for c in range(3)]
            for begin in range(0, lay.orbitals, 16):
                lines = pl.ds(begin, 16)
                centre = [columns[column, c, lines, :] for c in range(4)]
                for half in range(0, lay.points, 128):
                    distance = (at[0][:, half : half + 128] - centre[0]) ** 2
                    distance = distance + (at[1][:, half : half + 128] - centre[1]) ** 2
                    distance = distance + (at[2][:, half : half + 128] - centre[2]) ** 2
                    result = jnp.exp(centre[3] * distance)
                    orb[slot, lines, half : half + 128] = result.astype(jnp.bfloat16)
        return [
            list_units(lay, scalars, begin, step, target, end)
            for begin, target, end in zip(groups, units, ends)
        ]

    return lax.fori_loop(0, steps, some, [jnp.int32(0)] * len(groups))


def own_kernel(
    lay, pack, orb, columns, units, points, coded, scalars, entries, sem
):
    place = Place(lay)
    block = block_of(lay, pack)
    choice = partner_choice(lay, place, block)
    coded[...] = code_batches(
        lay, place, 0, block, choice, 0, choice, lambda window, partner: window < lay.rows
    )
    copy = pltpu.make_async_copy(coded, scalars, sem)
    copy.start()
    orb[lay.blank] = jnp.zeros(orb.shape[1:], orb.dtype)
    spread_columns(lay, place, 0, pack, columns)
    spread_points(lay, 0, pack, points)
    copy.wait()
    total = list_entries(lay, scalars, 0, entries, jnp.int32(0))
    (end,) = work_out(lay, entries, total, points, columns, orb, scalars, (0,), (units,))
    units[lay.units + 1] = end


def first_kernel(
    lay,
    pack_own,
    pack_pair,
    pack_far,
    density_own,
    density_pair,
    units_given,
    orb_in,
    columns_in,
    part,
    orb,
    columns,
    units,
    points,
    density,
    rho,
    units_own,
    units_rest,
    coded,
    scalars,
    entries,
    scalar_sem,
    density_sems,
    units_sem,
):
    rows, listed = lay.rows, lay.listed
    density_copies = [
        pltpu.make_async_copy(source, density.at[pl.ds(g * rows, rows)], density_sems.at[g])
        for g, source in enumerate((density_own, density_pair))
    ]
    for copy in density_copies:
        copy.start()
    units_copy = pltpu.make_async_copy(units_given, units_own, units_sem)
    units_copy.start()
    place = Place(lay)
    blocks = [block_of(lay, pack) for pack in (pack_own, pack_pair, pack_far)]
    own_choice = partner_choice(lay, place, blocks[0])
    pair_choice = partner_choice(lay, place, blocks[1])
    of_far = code_batches(
        lay,
        place,
        2,
        blocks[2],
        own_choice,
        0,
        own_choice,
        lambda window, partner: (window < rows) | partner,
    )
    of_own = code_batches(
        lay,
        place,
        0,
        blocks[0],
        pair_choice,
        rows,
        own_choice,
        lambda window, partner: (window >= rows) & ((window < 2 * rows) | partner),
    )
    lane = lax.broadcasted_iota(jnp.int32, of_far.shape, 1)
    coded[...] = jnp.where(lane < 4 * LANES, of_far, pltpu.roll(of_own, 4 * LANES, 1))
    scalar_copy = pltpu.make_async_copy(coded, scalars, scalar_sem)
    scalar_copy.start()
    spread_columns(lay, place, 1, pack_pair, columns)
    spread_columns(lay, place, 2, pack_far, columns)
    spread_points(lay, 0, pack_own, points)
    spread_points(lay, 2, pack_far, points)
    rho[...] = jnp.zeros_like(rho)
    scalar_copy.wait()
    total = list_entries(lay, scalars, 0, entries, jnp.int32(0))
    total = list_entries(lay, scalars, 4 * LANES, entries, total)
    ends = work_out(
        lay, entries, total, points, columns, orb, scalars, (0, 4 * LANES), (units, units_rest)
    )
    units[lay.units + 1] = ends[0]
    for copy in density_copies:
        copy.wait()
    units_copy.wait()
    one = units_own[lay.units + 1]
    two = one + ends[0]
    end = two + ends[1]

    def fold(step, carry):
        sums = []
        for u in range(UNROLL):
            index = step * UNROLL + u
            word = pick(
                lay, index, ((units_own, 0), (units, one), (units_rest, two)), end
            )
            slot, row, (k1, o1), (k2, o2) = decode(lay, word)
            others = jnp.concatenate([orb[o1], orb[o2]], axis=0)
            stored = jnp.concatenate([density[row, k1], density[row, k2]], axis=1)
            folded = jnp.dot(stored, others, preferred_element_type=jnp.float32)
            product = orb[slot].astype(jnp.float32) * folded
            total = product[0:8]
            for begin in range(8, lay.orbitals, 8):
                total = total + product[begin : begin + 8]
            sums.append((split(slot, listed)[0], total))
        for number, total in sums:
            rho[number] = rho[number] + total
        return carry

    lax.fori_loop(0, (end + UNROLL - 1) // UNROLL, fold, 0)
    part[: lay.batches, :] = jnp.sum(rho[: lay.batches], axis=1)
    part[lay.batches :, :] = jnp.sum(rho[2 * lay.batches : 3 * lay.batches], axis=1)


def pair_kernel(
    lay,
    pack_own,
    pack_pair,
    orb_in,
    columns,
    orb,
    units,
    points,
    coded,
    scalars,
    entries,
    sem,
):
    place = Place(lay)
    choice = partner_choice(lay, place, block_of(lay, pack_own))
    block = block_of(lay, pack_pair)
    coded[...] = code_batches(
        lay,
        place,
        1,
        block,
        choice,
        0,
        choice,
        lambda window, partner: (window < lay.rows) | partner,
    )
    copy = pltpu.make_async_copy(coded, scalars, sem)
    copy.start()
    spread_points(lay, 1, pack_pair, points)
    copy.wait()
    total = list_entries(lay, scalars, 0, entries, jnp.int32(0))
    (end,) = work_out(lay, entries, total, points, columns, orb, scalars, (0,), (units,))
    units[lay.units + 1] = end


def total_kernel(lay, part, arrived, units, out):
    out[...] = part[: lay.batches] + arrived[lay.batches :]


def pick(lay, index, lists, total):
    word, end = jnp.int32(lay.empty), total
    for units, begin in reversed(lists):
        word = jnp.where(index < end, units[jnp.clip(index - begin, 0, lay.units - 1)], word)
        end = begin
    return word


def decode(lay, word):
    slot = word >> 16
    row = (word >> 12) & 15
    base = slot & ~(lay.listed - 1)
    partners = []
    for shift in (6, 0):
        inner = (word >> shift) & 15
        partners.append(
            ((word >> (shift + 4)) & 3, jnp.where(inner == NONE, lay.blank, base + inner))
        )
    return slot, row, *partners


def cube_root(x):
    size = jnp.abs(x)
    safe = jnp.where(size > 0.0, size, 1.0)
    root = jnp.exp2(jnp.log2(safe) * (1.0 / 3.0))
    root = root - (root - safe / (root * root)) * (1.0 / 3.0)
    root = jnp.where(size > 0.0, root, 0.0)
    return jnp.where(x < 0.0, -root, root)


def second_kernel(
    lay,
    pack_own,
    pack_pair,
    pack_far,
    part,
    arrived,
    pair_rho,
    orb,
    units_given,
    out,
    potential,
    units_held,
    sems,
):
    copies = [
        pltpu.make_async_copy(source, target, sems.at[number])
        for number, (source, target) in enumerate(zip(units_given, units_held))
    ]
    for copy in copies:
        copy.start()
    packs = (pack_own, pack_pair, pack_far)
    n = lay.batches
    density_values = (part[:n] + arrived[n:], pair_rho[...], part[n:] + arrived[:n])
    potential[...] = jnp.zeros_like(potential)
    for g in range(3):
        weights = packs[g][lay.weights : lay.weights + n, :]
        potential[g * n : (g + 1) * n, :] = -exchange_coef * cube_root(density_values[g]) * weights
    out[...] = jnp.zeros_like(out)
    for copy in copies:
        copy.wait()
    units_own, units_first, units_pair = units_held
    one = units_own[lay.units + 1]
    two = one + units_first[lay.units + 1]
    total = two + units_pair[lay.units + 1]

    def contribute(step, carry):
        for u in range(UNROLL):
            index = step * UNROLL + u
            word = pick(
                lay, index, ((units_own, 0), (units_first, one), (units_pair, two)), total
            )
            slot, row, (k1, o1), (k2, o2) = decode(lay, word)
            others = jnp.concatenate([orb[o1], orb[o2]], axis=0)
            scale = potential[pl.ds(split(slot, lay.listed)[0], 1), :]
            weighted = (orb[slot].astype(jnp.float32) * scale).astype(jnp.bfloat16)
            contrib = lax.dot_general(
                weighted, others, (((1,), (1,)), ((), ())), preferred_element_type=jnp.float32
            )
            out[row, k1] += contrib[:, : lay.orbitals]
            out[row, k2] += contrib[:, lay.orbitals :]
        return carry

    lax.fori_loop(0, (total + UNROLL - 1) // UNROLL, contribute, 0)


def on_device(counts, points, weights, block_lists, pattern, basis_table, density):
    batches, listed = block_lists.shape
    rows, partners = pattern.shape
    orbitals = basis_table.shape[2]
    lay = Layout(batches, listed, points.shape[2], rows, partners, orbitals)
    devices = lax.axis_size("space")
    in_vmem = pl.BlockSpec(memory_space=VMEM)
    in_smem = pl.BlockSpec(memory_space=SMEM)
    in_hbm = pl.BlockSpec(memory_space=HBM)
    cost = pl.CostEstimate(flops=10**10, bytes_accessed=0, transcendentals=0)

    def params(limit=LIMIT):
        return pltpu.CompilerParams(vmem_limit_bytes=limit)

    pair_route = [(i, i ^ 1) for i in range(devices)]
    far_route = [
        (i, i + 1 if i % 2 else i - 1)
        for i in range(devices)
        if 0 <= (i + 1 if i % 2 else i - 1) < devices
    ]

    inputs = (counts, points, weights, block_lists.T, pattern.T, basis_table)
    pack = pl.pallas_call(
        functools.partial(pack_kernel, lay),
        out_shape=jax.ShapeDtypeStruct((lay.height, lay.points), jnp.float32),
        in_specs=[in_hbm] * 6,
        out_specs=in_vmem,
        scratch_shapes=[
            [SMEM(counts.shape, counts.dtype)] + [VMEM(x.shape, x.dtype) for x in inputs[1:]],
            pltpu.SemaphoreType.DMA((6,)),
        ],
        compiler_params=params(WHOLE),
        name="pack",
    )(*inputs)
    pack_far = lax.ppermute(pack, "space", far_route)
    pack_pair = lax.ppermute(pack, "space", pair_route)
    pack, density = lax.optimization_barrier((pack, density))
    density_pair = lax.ppermute(density, "space", pair_route)

    orb_shape = jax.ShapeDtypeStruct((lay.slots + 2, orbitals, lay.points), jnp.bfloat16)
    columns_shape = jax.ShapeDtypeStruct((lay.columns, 4, orbitals, 128), jnp.float32)
    anywhere = pl.BlockSpec(memory_space=pl.ANY)
    units_shape = jax.ShapeDtypeStruct((lay.units + 2,), jnp.int32)

    def scratch(groups):
        return [
            VMEM((listed, 128), jnp.int32),
            SMEM((listed, 128), jnp.int32),
            SMEM((groups * batches * listed + PAIRED,), jnp.int32),
            pltpu.SemaphoreType.DMA(()),
        ]

    points_scratch = VMEM((3 * batches, 8, lay.points), jnp.float32)
    orb, columns, units_own = pl.pallas_call(
        functools.partial(own_kernel, lay),
        out_shape=(orb_shape, columns_shape, units_shape),
        in_specs=[in_vmem],
        out_specs=(in_vmem, in_vmem, in_smem),
        scratch_shapes=[points_scratch, *scratch(1)],
        compiler_params=params(),
        cost_estimate=cost,
        name="first_own",
    )(pack)

    part, orb, columns, units_first = pl.pallas_call(
        functools.partial(first_kernel, lay),
        out_shape=(
            jax.ShapeDtypeStruct((2 * batches, lay.points), jnp.float32),
            orb_shape,
            columns_shape,
            units_shape,
        ),
        in_specs=[in_vmem] * 3 + [in_hbm, in_hbm, anywhere, in_vmem, in_vmem],
        out_specs=(in_vmem, in_vmem, in_vmem, in_smem),
        scratch_shapes=[
            points_scratch,
            VMEM((2 * rows, partners, orbitals, orbitals), jnp.bfloat16),
            VMEM((3 * batches + 1, 8, lay.points), jnp.float32),
            SMEM(units_shape.shape, jnp.int32),
            SMEM(units_shape.shape, jnp.int32),
            *scratch(2),
            pltpu.SemaphoreType.DMA((2,)),
            pltpu.SemaphoreType.DMA(()),
        ],
        input_output_aliases={6: 1, 7: 2},
        compiler_params=params(BUSY),
        cost_estimate=cost,
        name="first",
    )(pack, pack_pair, pack_far, density, density_pair, units_own, orb, columns)

    arrived = lax.ppermute(part, "space", far_route)
    orb, units_pair = pl.pallas_call(
        functools.partial(pair_kernel, lay),
        out_shape=(orb_shape, units_shape),
        in_specs=[in_vmem] * 4,
        out_specs=(in_vmem, in_smem),
        scratch_shapes=[points_scratch, *scratch(1)],
        input_output_aliases={2: 0},
        compiler_params=params(),
        cost_estimate=cost,
        name="first_pair",
    )(pack, pack_pair, orb, columns)
    own_rho = pl.pallas_call(
        functools.partial(total_kernel, lay),
        out_shape=jax.ShapeDtypeStruct((batches, lay.points), jnp.float32),
        in_specs=[in_vmem, in_vmem, anywhere],
        out_specs=in_vmem,
        compiler_params=params(1 << 20),
        name="total",
    )(part, arrived, units_pair)
    pair_rho = lax.ppermute(own_rho, "space", pair_route)

    return pl.pallas_call(
        functools.partial(second_kernel, lay),
        out_shape=jax.ShapeDtypeStruct(density.shape, jnp.float32),
        in_specs=[in_vmem] * 7 + [[anywhere] * 3],
        out_specs=in_vmem,
        scratch_shapes=[
            VMEM((-(-(3 * batches + 1) // 8) * 8, lay.points), jnp.float32),
            [SMEM(units_shape.shape, jnp.int32)] * 3,
            pltpu.SemaphoreType.DMA((3,)),
        ],
        compiler_params=params(),
        name="second",
    )(
        pack,
        pack_pair,
        pack_far,
        part,
        arrived,
        pair_rho,
        orb,
        [units_own, units_first, units_pair],
    )


def solution(mesh):
    in_specs = (
        P(("parts", "space")),
        P(("parts", "space"), None, None),
        P(("parts", "space"), None),
        P(("parts", "space"), None),
        P(("parts", "space"), None),
        P(("parts", "space"), None, None),
        P(("parts", "space"), None, None, None),
    )
    out_specs = P(("parts", "space"), None, None, None)
    return jax.shard_map(
        on_device, mesh=mesh, in_specs=in_specs, out_specs=out_specs, check_vma=False
    )
```

```python
import functools
import math

import jax
import jax.numpy as jnp
from jax import lax
from jax.experimental import pallas as pl
from jax.experimental.pallas import tpu as pltpu
from jax.sharding import PartitionSpec as P

exchange_coef = (3.0 / math.pi) ** (1.0 / 3.0)
VMEM = pltpu.VMEM
SMEM = pltpu.SMEM
HBM = pltpu.HBM
LIMIT = 12 << 20
WHOLE = 63 << 20
BUSY = 12 << 20
REACH = 3
UNROLL = 16
PAIRED = 2
LANES = 16
NOWHERE, ELSEWHERE = 31, 30
NONE = 15


def split(value, size):
    if size & (size - 1):
        quotient = value // size
        return quotient, value - quotient * size
    return lax.shift_right_logical(value, size.bit_length() - 1), value & (size - 1)


class Layout:
    def __init__(self, batches, listed, points, rows, partners, orbitals):
        self.batches, self.listed, self.points = batches, listed, points
        self.rows, self.partners, self.orbitals = rows, partners, orbitals
        self.weights = -(-3 * batches // 8) * 8
        self.basis = self.weights + -(-batches // 8) * 8
        self.lists = 0
        self.pattern = -(-listed // 8) * 8
        self.meta = self.pattern + -(-partners // 8) * 8
        self.scalar_rows = -(-max(4 * rows, self.meta + 1) // 8) * 8
        self.height = self.basis + self.scalar_rows
        self.slots = 3 * batches * listed
        self.blank, self.trash = self.slots, self.slots + 1
        self.columns = 2 * rows + REACH
        self.units = 2 * batches * listed
        self.empty = (self.blank * 16) << 12 | NONE << 6 | NONE


def pack_kernel(lay, counts, points, weights, lists, pattern, basis, out, held, sems):
    copies = [
        pltpu.make_async_copy(source, target, sems.at[number])
        for number, (source, target) in enumerate(
            zip((counts, points, weights, lists, pattern, basis), held)
        )
    ]
    for copy in copies:
        copy.start()
    out[...] = jnp.zeros_like(out)
    me = lax.axis_index("space")
    for copy in copies:
        copy.wait()
    counts, points, weights, lists, pattern, basis = held
    for t in range(lay.batches):
        out[3 * t : 3 * t + 3, :] = points[t]
    out[lay.weights : lay.weights + lay.batches, :] = weights[...]
    for w in range(lay.rows):
        out[lay.basis + 4 * w : lay.basis + 4 * w + 4, :128] = basis[w].astype(jnp.float32)
    begin = lay.basis + lay.lists
    out[begin : begin + lay.listed, 128 : 128 + lay.batches] = lists[...].astype(jnp.float32)
    begin = lay.basis + lay.pattern
    out[begin : begin + lay.partners, 128 : 128 + lay.rows] = pattern[...].astype(jnp.float32)
    begin = lay.basis + lay.meta
    lane = lax.broadcasted_iota(jnp.int32, (1, 128), 1)
    meta = jnp.where(lane == 0, counts[0], jnp.where(lane == 1, me, 0))
    out[begin : begin + 1, 128:256] = meta.astype(jnp.float32)


class Place:
    def __init__(self, lay):
        self.lay = lay
        self.own = lax.axis_index("space")
        self.pair = self.own ^ 1
        even = self.own % 2 == 0
        self.even = even
        self.far = jnp.where(even, self.own - 1, self.own + 1)
        self.far_first = jnp.where(even, lay.rows - REACH, 0)

    def window(self, raw, outside):
        rows = self.lay.rows
        owner, inner = split(raw, rows)
        far = jnp.where(owner == self.far, 2 * rows + inner, outside)
        return jnp.where(owner == self.own, inner, jnp.where(owner == self.pair, rows + inner, far))


def block_of(lay, pack):
    return pack[lay.basis : lay.basis + lay.scalar_rows, 128:256]


def partner_choice(lay, place, block):
    raw = block[lay.pattern : lay.pattern + 8].astype(jnp.int32)
    turned = place.window(raw, ELSEWHERE).astype(jnp.float32).T
    lane = lax.broadcasted_iota(jnp.int32, (lay.rows, 32), 1).astype(jnp.float32)
    return jnp.concatenate(
        [
            jnp.where(turned[: lay.rows, k : k + 1] == lane, 1.0, 0.0)
            for k in range(1, lay.partners)
        ],
        axis=0,
    ).astype(jnp.bfloat16)


def code_entries(lay, place, g, block, own_choice, wanted):
    listed, rows = lay.listed, lay.rows
    raw = block.astype(jnp.int32)
    window = place.window(raw[lay.lists : lay.lists + listed], NOWHERE)
    lane = lax.broadcasted_iota(jnp.int32, (listed, 128), 1)
    position = lax.broadcasted_iota(jnp.int32, (listed, 128), 0)
    column = jnp.where(window < 2 * rows, window, window - place.far_first)
    entry = ((g * lay.batches + lane) * listed + position) * 32 + column
    if own_choice is None:
        result = jnp.where(wanted(window, None), entry, -1)
        held = None
    else:
        line = lax.broadcasted_iota(jnp.int32, (32, 128), 0)
        held = jnp.zeros((32, 128), jnp.int32)
        for b in range(listed):
            held = jnp.where(line == window[b : b + 1], b + 1, held)
        there = jnp.where(held[:rows] > 0, 1.0, 0.0).astype(jnp.bfloat16)
        partner_of = lax.dot_general(
            own_choice,
            jnp.concatenate([there] * (lay.partners - 1), axis=0),
            (((0,), (0,)), ((), ())),
            preferred_element_type=jnp.float32,
        )
        partner = jnp.zeros((listed, 128), jnp.float32)
        for w in range(rows, 3 * rows):
            partner = jnp.where(window == w, partner_of[w : w + 1], partner)
        result = jnp.where(wanted(window, partner > 0.5), entry, -1)
    live = lane < raw[lay.meta : lay.meta + 1, 0:1]
    return jnp.where(live, result, -1), window, held


def code_units(lay, g, block, window, held, choice, first_row):
    listed, rows = lay.listed, lay.rows
    lane = lax.broadcasted_iota(jnp.int32, (listed, 128), 1)
    others = jnp.dot(
        choice, held.astype(jnp.float32).astype(jnp.bfloat16), preferred_element_type=jnp.float32
    ).astype(jnp.int32)
    codes = [
        (k * 16 - 1) + others[(k - 1) * rows : k * rows] for k in range(1, lay.partners)
    ]
    one, two, three = [others[(k - 1) * rows : k * rows] > 0 for k in range(1, lay.partners)]
    itself = held[first_row : first_row + rows] - 1
    item_row = first_row + lax.broadcasted_iota(jnp.int32, (rows, 128), 0)
    item_base = (g * lay.batches + lax.broadcasted_iota(jnp.int32, (rows, 128), 1)) * listed
    common = ((item_base + itself) * 16 + item_row) << 12
    first = jnp.where(one, codes[0], jnp.where(two, codes[1], jnp.where(three, codes[2], NONE)))
    more = (one & two) | ((one | two) & three)
    second = jnp.where(one & two, codes[1], codes[2])
    third = jnp.where(one & two & three, codes[2], NONE)
    exists = itself >= 0
    units = (
        jnp.where(exists, common + (itself << 6) + first, -1),
        jnp.where(exists & more, common + (second << 6) + third, -1),
    )
    live = lane < block[lay.meta : lay.meta + 1, 0:1].astype(jnp.int32)
    result = jnp.full((listed, 128), -1, jnp.int32)
    for number, unit in enumerate(units):
        found = jnp.full((listed, 128), -1, jnp.int32)
        for w in range(rows):
            found = jnp.where(window == first_row + w, unit[w : w + 1], found)
        found = jnp.where(live, found, -1)
        begin = LANES * number
        result = jnp.where(lane < begin, result, pltpu.roll(found, begin, 1))
    return result


def list_entries(lay, coded, begin, entries, total):
    for t in range(lay.batches):
        for b in range(lay.listed):
            entry = coded[b, begin + t]
            entries[total] = entry
            total = total + 1 + (entry >> 31)
    return total


def live_batches(lay, pack):
    return jnp.minimum(pack[lay.basis + lay.meta, 128].astype(jnp.int32), lay.batches)


def list_scalars(lay, scalars, begin, live, entries, total):
    def visit(t, total):
        for entry in [scalars[b, begin + t] for b in range(lay.listed)]:
            entries[total] = entry
            total = total + 1 + (entry >> 31)
        return total

    return lax.fori_loop(0, live, visit, total)


def list_units(lay, scalars, begin, t, units, total):
    t = jnp.minimum(t, LANES - 1)
    found = [
        scalars[b, begin + lane + t] for b in range(lay.listed) for lane in (0, LANES)
    ]
    for unit in found:
        units[total] = unit
        total = total + 1 + (unit >> 31)
    return total


def spread_columns(lay, place, g, pack, columns):
    rows = lay.rows
    table = pack[lay.basis : lay.basis + 4 * rows, :128]
    count, first, owner = rows, 0, (place.own, place.pair, place.far)[g]
    if g == 2:
        count, first = REACH, place.far_first
        table = jnp.where(place.even, table[4 * (rows - count) :], table[: 4 * count])
    table = table.T
    for w in range(count):
        for c in range(4):
            column = table[:, 4 * w + c : 4 * w + c + 1]
            if c == 0:
                column = column + (owner * rows + first + w).astype(jnp.float32)
            if c == 3:
                column = -column
            columns[g * rows + w, c] = jnp.broadcast_to(column, (lay.orbitals, 128))


def spread_points(lay, g, pack, points):
    for t in range(lay.batches):
        points[g * lay.batches + t, 0:3, :] = pack[3 * t : 3 * t + 3, :]


def work_out(lay, entries, total, points, columns, orb, scalars, groups, units, live):
    for u in range(PAIRED):
        entries[total + u] = lay.trash * 32
    steps = (total + PAIRED - 1) // PAIRED
    steps = jnp.maximum(steps, live)

    def some(step, ends):
        for u in range(PAIRED):
            index = jnp.minimum(step * PAIRED + u, total)
            slot, column = split(entries[index], 32)
            batch = jnp.minimum(split(slot, lay.listed)[0], 3 * lay.batches - 1)
            at = [points[batch, c : c + 1, :] for c in range(3)]
            for begin in range(0, lay.orbitals, 16):
                lines = pl.ds(begin, 16)
                centre = [columns[column, c, lines, :] for c in range(4)]
                for half in range(0, lay.points, 128):
                    distance = (at[0][:, half : half + 128] - centre[0]) ** 2
                    distance = distance + (at[1][:, half : half + 128] - centre[1]) ** 2
                    distance = distance + (at[2][:, half : half + 128] - centre[2]) ** 2
                    result = jnp.exp(centre[3] * distance)
                    orb[slot, lines, half : half + 128] = result.astype(jnp.bfloat16)
        return [
            list_units(lay, scalars, begin, step, target, end)
            for begin, target, end in zip(groups, units, ends)
        ]

    return lax.fori_loop(0, steps, some, [jnp.int32(0)] * len(groups))


def own_kernel(lay, pack, orb, columns, points, coded, entries):
    place = Place(lay)
    coded[...] = code_entries(
        lay, place, 0, block_of(lay, pack), None, lambda window, partner: window < lay.rows
    )[0]
    orb[lay.blank] = jnp.zeros(orb.shape[1:], orb.dtype)
    spread_columns(lay, place, 0, pack, columns)
    spread_points(lay, 0, pack, points)
    total = list_entries(lay, coded, 0, entries, jnp.int32(0))
    work_out(lay, entries, total, points, columns, orb, None, (), (), 0)


def first_kernel(
    lay,
    pack_own,
    pack_pair,
    pack_far,
    density_own,
    density_pair,
    orb_in,
    columns_in,
    part,
    orb,
    columns,
    units_own_out,
    units_far_out,
    points,
    density,
    rho,
    units_own,
    units_far,
    units_rest,
    coded,
    scalars,
    entries,
    scalar_sem,
    density_sems,
    units_sems,
):
    rows, listed = lay.rows, lay.listed
    density_copies = [
        pltpu.make_async_copy(source, density.at[pl.ds(g * rows, rows)], density_sems.at[g])
        for g, source in enumerate((density_own, density_pair))
    ]
    for copy in density_copies:
        copy.start()
    place = Place(lay)
    blocks = [block_of(lay, pack) for pack in (pack_own, pack_pair, pack_far)]
    own_choice = partner_choice(lay, place, blocks[0])
    pair_choice = partner_choice(lay, place, blocks[1])
    of_far, window, held = code_entries(
        lay, place, 2, blocks[2], own_choice, lambda window, partner: (window < rows) | partner
    )
    entries_far = of_far
    of_far = code_units(lay, 2, blocks[2], window, held, own_choice, 0)
    entries_rest, window, held = code_entries(
        lay,
        place,
        0,
        blocks[0],
        own_choice,
        lambda window, partner: (window >= rows) & ((window < 2 * rows) | partner),
    )
    of_own = code_units(lay, 0, blocks[0], window, held, own_choice, 0)
    of_rest = code_units(lay, 0, blocks[0], window, held, pair_choice, rows)
    lane = lax.broadcasted_iota(jnp.int32, of_far.shape, 1)
    coded[...] = jnp.where(
        lane < 2 * LANES,
        of_own,
        jnp.where(
            lane < 4 * LANES,
            pltpu.roll(of_far, 2 * LANES, 1),
            jnp.where(
                lane < 6 * LANES,
                pltpu.roll(of_rest, 4 * LANES, 1),
                jnp.where(
                    lane < 7 * LANES,
                    pltpu.roll(entries_far, 6 * LANES, 1),
                    pltpu.roll(entries_rest, 7 * LANES, 1),
                ),
            ),
        ),
    )
    scalar_copy = pltpu.make_async_copy(coded, scalars, scalar_sem)
    scalar_copy.start()
    spread_columns(lay, place, 1, pack_pair, columns)
    spread_columns(lay, place, 2, pack_far, columns)
    spread_points(lay, 0, pack_own, points)
    spread_points(lay, 2, pack_far, points)
    rho[...] = jnp.zeros_like(rho)
    far_live, own_live = live_batches(lay, pack_far), live_batches(lay, pack_own)
    scalar_copy.wait()
    total = list_scalars(lay, scalars, 6 * LANES, far_live, entries, jnp.int32(0))
    total = list_scalars(lay, scalars, 7 * LANES, own_live, entries, total)
    lists = (units_own, units_far, units_rest)
    ends = work_out(
        lay,
        entries,
        total,
        points,
        columns,
        orb,
        scalars,
        (0, 2 * LANES, 4 * LANES),
        lists,
        jnp.maximum(far_live, own_live),
    )
    units_own[lay.units + 1] = ends[0]
    units_far[lay.units + 1] = ends[1]
    units_copies = [
        pltpu.make_async_copy(source, target, units_sems.at[number])
        for number, (source, target) in enumerate(
            ((units_own, units_own_out), (units_far, units_far_out))
        )
    ]
    for copy in units_copies:
        copy.start()
    for copy in density_copies:
        copy.wait()
    one = ends[0]
    two = one + ends[1]
    end = two + ends[2]

    def fold(step, carry):
        sums = []
        for u in range(UNROLL):
            index = step * UNROLL + u
            word = pick(
                lay, index, ((units_own, 0), (units_far, one), (units_rest, two)), end
            )
            slot, row, (k1, o1), (k2, o2) = decode(lay, word)
            others = jnp.concatenate([orb[o1], orb[o2]], axis=0)
            stored = jnp.concatenate([density[row, k1], density[row, k2]], axis=1)
            folded = jnp.dot(stored, others, preferred_element_type=jnp.float32)
            product = orb[slot].astype(jnp.float32) * folded
            total = product[0:8]
            for begin in range(8, lay.orbitals, 8):
                total = total + product[begin : begin + 8]
            sums.append((split(slot, listed)[0], total))
        for number, total in sums:
            rho[number] = rho[number] + total
        return carry

    lax.fori_loop(0, (end + UNROLL - 1) // UNROLL, fold, 0)
    part[: lay.batches, :] = jnp.sum(rho[: lay.batches], axis=1)
    part[lay.batches :, :] = jnp.sum(rho[2 * lay.batches : 3 * lay.batches], axis=1)
    for copy in units_copies:
        copy.wait()


def pair_kernel(
    lay,
    pack_own,
    pack_pair,
    orb_in,
    columns,
    orb,
    units,
    points,
    coded,
    scalars,
    entries,
    sem,
):
    place = Place(lay)
    choice = partner_choice(lay, place, block_of(lay, pack_own))
    block = block_of(lay, pack_pair)
    result, window, held = code_entries(
        lay, place, 1, block, choice, lambda window, partner: (window < lay.rows) | partner
    )
    units_found = code_units(lay, 1, block, window, held, choice, 0)
    lane = lax.broadcasted_iota(jnp.int32, result.shape, 1)
    coded[...] = jnp.where(lane < 2 * LANES, units_found, pltpu.roll(result, 2 * LANES, 1))
    copy = pltpu.make_async_copy(coded, scalars, sem)
    copy.start()
    spread_points(lay, 1, pack_pair, points)
    live = live_batches(lay, pack_pair)
    copy.wait()
    total = list_scalars(lay, scalars, 2 * LANES, live, entries, jnp.int32(0))
    (end,) = work_out(lay, entries, total, points, columns, orb, scalars, (0,), (units,), live)
    units[lay.units + 1] = end


def total_kernel(lay, part, arrived, units, out):
    out[...] = part[: lay.batches] + arrived[lay.batches :]


def pick(lay, index, lists, total):
    word, end = jnp.int32(lay.empty), total
    for units, begin in reversed(lists):
        word = jnp.where(index < end, units[jnp.clip(index - begin, 0, lay.units - 1)], word)
        end = begin
    return word


def decode(lay, word):
    slot = word >> 16
    row = (word >> 12) & 15
    base = slot & ~(lay.listed - 1)
    partners = []
    for shift in (6, 0):
        inner = (word >> shift) & 15
        partners.append(
            ((word >> (shift + 4)) & 3, jnp.where(inner == NONE, lay.blank, base + inner))
        )
    return slot, row, *partners


def cube_root(x):
    size = jnp.abs(x)
    safe = jnp.where(size > 0.0, size, 1.0)
    root = jnp.exp2(jnp.log2(safe) * (1.0 / 3.0))
    root = root - (root - safe / (root * root)) * (1.0 / 3.0)
    root = jnp.where(size > 0.0, root, 0.0)
    return jnp.where(x < 0.0, -root, root)


def second_kernel(
    lay,
    pack_own,
    pack_pair,
    pack_far,
    part,
    arrived,
    pair_rho,
    orb,
    units_given,
    out,
    potential,
    units_held,
    sems,
):
    copies = [
        pltpu.make_async_copy(source, target, sems.at[number])
        for number, (source, target) in enumerate(zip(units_given, units_held))
    ]
    for copy in copies:
        copy.start()
    packs = (pack_own, pack_pair, pack_far)
    n = lay.batches
    density_values = (part[:n] + arrived[n:], pair_rho[...], part[n:] + arrived[:n])
    potential[...] = jnp.zeros_like(potential)
    for g in range(3):
        weights = packs[g][lay.weights : lay.weights + n, :]
        potential[g * n : (g + 1) * n, :] = -exchange_coef * cube_root(density_values[g]) * weights
    out[...] = jnp.zeros_like(out)
    for copy in copies:
        copy.wait()
    units_own, units_first, units_pair = units_held
    one = units_own[lay.units + 1]
    two = one + units_first[lay.units + 1]
    total = two + units_pair[lay.units + 1]

    def contribute(step, carry):
        for u in range(UNROLL):
            index = step * UNROLL + u
            word = pick(
                lay, index, ((units_own, 0), (units_first, one), (units_pair, two)), total
            )
            slot, row, (k1, o1), (k2, o2) = decode(lay, word)
            others = jnp.concatenate([orb[o1], orb[o2]], axis=0)
            scale = potential[pl.ds(split(slot, lay.listed)[0], 1), :]
            weighted = (orb[slot].astype(jnp.float32) * scale).astype(jnp.bfloat16)
            contrib = lax.dot_general(
                weighted, others, (((1,), (1,)), ((), ())), preferred_element_type=jnp.float32
            )
            out[row, k1] += contrib[:, : lay.orbitals]
            out[row, k2] += contrib[:, lay.orbitals :]
        return carry

    lax.fori_loop(0, (total + UNROLL - 1) // UNROLL, contribute, 0)


def on_device(counts, points, weights, block_lists, pattern, basis_table, density):
    batches, listed = block_lists.shape
    rows, partners = pattern.shape
    orbitals = basis_table.shape[2]
    lay = Layout(batches, listed, points.shape[2], rows, partners, orbitals)
    devices = lax.axis_size("space")
    in_vmem = pl.BlockSpec(memory_space=VMEM)
    in_smem = pl.BlockSpec(memory_space=SMEM)
    in_hbm = pl.BlockSpec(memory_space=HBM)
    cost = pl.CostEstimate(flops=10**10, bytes_accessed=0, transcendentals=0)

    def params(limit=LIMIT):
        return pltpu.CompilerParams(vmem_limit_bytes=limit)

    pair_route = [(i, i ^ 1) for i in range(devices)]
    far_route = [
        (i, i + 1 if i % 2 else i - 1)
        for i in range(devices)
        if 0 <= (i + 1 if i % 2 else i - 1) < devices
    ]

    inputs = (counts, points, weights, block_lists.T, pattern.T, basis_table)
    pack = pl.pallas_call(
        functools.partial(pack_kernel, lay),
        out_shape=jax.ShapeDtypeStruct((lay.height, lay.points), jnp.float32),
        in_specs=[in_hbm] * 6,
        out_specs=in_vmem,
        scratch_shapes=[
            [SMEM(counts.shape, counts.dtype)] + [VMEM(x.shape, x.dtype) for x in inputs[1:]],
            pltpu.SemaphoreType.DMA((6,)),
        ],
        compiler_params=params(WHOLE),
        name="pack",
    )(*inputs)
    pack_far = lax.ppermute(pack, "space", far_route)
    pack_pair = lax.ppermute(pack, "space", pair_route)
    pack, density = lax.optimization_barrier((pack, density))
    density_pair = lax.ppermute(density, "space", pair_route)

    orb_shape = jax.ShapeDtypeStruct((lay.slots + 2, orbitals, lay.points), jnp.bfloat16)
    columns_shape = jax.ShapeDtypeStruct((lay.columns, 4, orbitals, 128), jnp.float32)
    anywhere = pl.BlockSpec(memory_space=pl.ANY)
    units_shape = jax.ShapeDtypeStruct((lay.units + 2,), jnp.int32)

    def scratch(groups):
        return [
            VMEM((listed, 128), jnp.int32),
            SMEM((listed, 128), jnp.int32),
            SMEM((groups * batches * listed + PAIRED,), jnp.int32),
            pltpu.SemaphoreType.DMA(()),
        ]

    points_scratch = VMEM((3 * batches, 8, lay.points), jnp.float32)
    orb, columns = pl.pallas_call(
        functools.partial(own_kernel, lay),
        out_shape=(orb_shape, columns_shape),
        in_specs=[in_vmem],
        out_specs=(in_vmem, in_vmem),
        scratch_shapes=[
            points_scratch,
            VMEM((listed, 128), jnp.int32),
            SMEM((batches * listed + PAIRED,), jnp.int32),
        ],
        compiler_params=params(),
        cost_estimate=cost,
        name="first_own",
    )(pack)

    part, orb, columns, units_own, units_first = pl.pallas_call(
        functools.partial(first_kernel, lay),
        out_shape=(
            jax.ShapeDtypeStruct((2 * batches, lay.points), jnp.float32),
            orb_shape,
            columns_shape,
            units_shape,
            units_shape,
        ),
        in_specs=[in_vmem] * 3 + [in_hbm, in_hbm, in_vmem, in_vmem],
        out_specs=(in_vmem, in_vmem, in_vmem, anywhere, anywhere),
        scratch_shapes=[
            points_scratch,
            VMEM((2 * rows, partners, orbitals, orbitals), jnp.bfloat16),
            VMEM((3 * batches + 1, 8, lay.points), jnp.float32),
            *[SMEM(units_shape.shape, jnp.int32)] * 3,
            *scratch(2),
            pltpu.SemaphoreType.DMA((2,)),
            pltpu.SemaphoreType.DMA((2,)),
        ],
        input_output_aliases={5: 1, 6: 2},
        compiler_params=params(BUSY),
        cost_estimate=cost,
        name="first",
    )(pack, pack_pair, pack_far, density, density_pair, orb, columns)

    arrived = lax.ppermute(part, "space", far_route)
    orb, units_pair = pl.pallas_call(
        functools.partial(pair_kernel, lay),
        out_shape=(orb_shape, units_shape),
        in_specs=[in_vmem] * 4,
        out_specs=(in_vmem, in_smem),
        scratch_shapes=[points_scratch, *scratch(1)],
        input_output_aliases={2: 0},
        compiler_params=params(),
        cost_estimate=cost,
        name="first_pair",
    )(pack, pack_pair, orb, columns)
    own_rho = pl.pallas_call(
        functools.partial(total_kernel, lay),
        out_shape=jax.ShapeDtypeStruct((batches, lay.points), jnp.float32),
        in_specs=[in_vmem, in_vmem, anywhere],
        out_specs=in_vmem,
        compiler_params=params(1 << 20),
        name="total",
    )(part, arrived, units_pair)
    pair_rho = lax.ppermute(own_rho, "space", pair_route)

    return pl.pallas_call(
        functools.partial(second_kernel, lay),
        out_shape=jax.ShapeDtypeStruct(density.shape, jnp.float32),
        in_specs=[in_vmem] * 7 + [[anywhere] * 3],
        out_specs=in_vmem,
        scratch_shapes=[
            VMEM((-(-(3 * batches + 1) // 8) * 8, lay.points), jnp.float32),
            [SMEM(units_shape.shape, jnp.int32)] * 3,
            pltpu.SemaphoreType.DMA((3,)),
        ],
        compiler_params=params(),
        name="second",
    )(
        pack,
        pack_pair,
        pack_far,
        part,
        arrived,
        pair_rho,
        orb,
        [units_own, units_first, units_pair],
    )


def solution(mesh):
    in_specs = (
        P(("parts", "space")),
        P(("parts", "space"), None, None),
        P(("parts", "space"), None),
        P(("parts", "space"), None),
        P(("parts", "space"), None),
        P(("parts", "space"), None, None),
        P(("parts", "space"), None, None, None),
    )
    out_specs = P(("parts", "space"), None, None, None)
    return jax.shard_map(
        on_device, mesh=mesh, in_specs=in_specs, out_specs=out_specs, check_vma=False
    )
```

```python
import functools
import math

import jax
import jax.numpy as jnp
from jax import lax
from jax.experimental import pallas as pl
from jax.experimental.pallas import tpu as pltpu
from jax.sharding import PartitionSpec as P

exchange_coef = (3.0 / math.pi) ** (1.0 / 3.0)
VMEM = pltpu.VMEM
SMEM = pltpu.SMEM
HBM = pltpu.HBM
LIMIT = 12 << 20
WHOLE = 63 << 20
BUSY = 12 << 20
REACH = 3
UNROLL = 16
PAIRED = 3
LANES = 16
NOWHERE, ELSEWHERE = 31, 30
NONE = 15


def split(value, size):
    if size & (size - 1):
        quotient = value // size
        return quotient, value - quotient * size
    return lax.shift_right_logical(value, size.bit_length() - 1), value & (size - 1)


class Layout:
    def __init__(self, batches, listed, points, rows, partners, orbitals):
        self.batches, self.listed, self.points = batches, listed, points
        self.rows, self.partners, self.orbitals = rows, partners, orbitals
        self.weights = -(-3 * batches // 8) * 8
        self.basis = self.weights + -(-batches // 8) * 8
        self.lists = 0
        self.pattern = -(-listed // 8) * 8
        self.meta = self.pattern + -(-partners // 8) * 8
        self.scalar_rows = -(-max(4 * rows, self.meta + 1) // 8) * 8
        self.height = self.basis + self.scalar_rows
        self.slots = 3 * batches * listed
        self.blank, self.trash = self.slots, self.slots + 1
        self.columns = 2 * rows + REACH
        self.units = 2 * batches * listed
        self.empty = (self.blank * 16) << 12 | NONE << 6 | NONE


def pack_kernel(lay, counts, points, weights, lists, pattern, basis, out, held, sems):
    copies = [
        pltpu.make_async_copy(source, target, sems.at[number])
        for number, (source, target) in enumerate(
            zip((counts, points, weights, lists, pattern, basis), held)
        )
    ]
    for copy in copies:
        copy.start()
    out[...] = jnp.zeros_like(out)
    me = lax.axis_index("space")
    for copy in copies:
        copy.wait()
    counts, points, weights, lists, pattern, basis = held
    for t in range(lay.batches):
        out[3 * t : 3 * t + 3, :] = points[t]
    out[lay.weights : lay.weights + lay.batches, :] = weights[...]
    for w in range(lay.rows):
        out[lay.basis + 4 * w : lay.basis + 4 * w + 4, :128] = basis[w].astype(jnp.float32)
    begin = lay.basis + lay.lists
    out[begin : begin + lay.listed, 128 : 128 + lay.batches] = lists[...].astype(jnp.float32)
    begin = lay.basis + lay.pattern
    out[begin : begin + lay.partners, 128 : 128 + lay.rows] = pattern[...].astype(jnp.float32)
    begin = lay.basis + lay.meta
    lane = lax.broadcasted_iota(jnp.int32, (1, 128), 1)
    meta = jnp.where(lane == 0, counts[0], jnp.where(lane == 1, me, 0))
    out[begin : begin + 1, 128:256] = meta.astype(jnp.float32)


class Place:
    def __init__(self, lay):
        self.lay = lay
        self.own = lax.axis_index("space")
        self.pair = self.own ^ 1
        even = self.own % 2 == 0
        self.even = even
        self.far = jnp.where(even, self.own - 1, self.own + 1)
        self.far_first = jnp.where(even, lay.rows - REACH, 0)

    def window(self, raw, outside):
        rows = self.lay.rows
        owner, inner = split(raw, rows)
        far = jnp.where(owner == self.far, 2 * rows + inner, outside)
        return jnp.where(owner == self.own, inner, jnp.where(owner == self.pair, rows + inner, far))


def block_of(lay, pack):
    return pack[lay.basis : lay.basis + lay.scalar_rows, 128:256]


def partner_choice(lay, place, block):
    raw = block[lay.pattern : lay.pattern + 8].astype(jnp.int32)
    turned = place.window(raw, ELSEWHERE).astype(jnp.float32).T
    lane = lax.broadcasted_iota(jnp.int32, (lay.rows, 32), 1).astype(jnp.float32)
    return jnp.concatenate(
        [
            jnp.where(turned[: lay.rows, k : k + 1] == lane, 1.0, 0.0)
            for k in range(1, lay.partners)
        ],
        axis=0,
    ).astype(jnp.bfloat16)


def code_entries(lay, place, g, block, own_choice, wanted):
    listed, rows = lay.listed, lay.rows
    raw = block.astype(jnp.int32)
    window = place.window(raw[lay.lists : lay.lists + listed], NOWHERE)
    lane = lax.broadcasted_iota(jnp.int32, (listed, 128), 1)
    position = lax.broadcasted_iota(jnp.int32, (listed, 128), 0)
    column = jnp.where(window < 2 * rows, window, window - place.far_first)
    entry = ((g * lay.batches + lane) * listed + position) * 32 + column
    if own_choice is None:
        result = jnp.where(wanted(window, None), entry, -1)
        held = None
    else:
        line = lax.broadcasted_iota(jnp.int32, (32, 128), 0)
        held = jnp.zeros((32, 128), jnp.int32)
        for b in range(listed):
            held = jnp.where(line == window[b : b + 1], b + 1, held)
        there = jnp.where(held[:rows] > 0, 1.0, 0.0).astype(jnp.bfloat16)
        partner_of = lax.dot_general(
            own_choice,
            jnp.concatenate([there] * (lay.partners - 1), axis=0),
            (((0,), (0,)), ((), ())),
            preferred_element_type=jnp.float32,
        )
        partner = jnp.zeros((listed, 128), jnp.float32)
        for w in range(rows, 3 * rows):
            partner = jnp.where(window == w, partner_of[w : w + 1], partner)
        result = jnp.where(wanted(window, partner > 0.5), entry, -1)
    live = lane < raw[lay.meta : lay.meta + 1, 0:1]
    return jnp.where(live, result, -1), window, held


def code_units(lay, g, block, window, held, choice, first_row):
    listed, rows = lay.listed, lay.rows
    lane = lax.broadcasted_iota(jnp.int32, (listed, 128), 1)
    others = jnp.dot(
        choice, held.astype(jnp.float32).astype(jnp.bfloat16), preferred_element_type=jnp.float32
    ).astype(jnp.int32)
    codes = [
        (k * 16 - 1) + others[(k - 1) * rows : k * rows] for k in range(1, lay.partners)
    ]
    one, two, three = [others[(k - 1) * rows : k * rows] > 0 for k in range(1, lay.partners)]
    itself = held[first_row : first_row + rows] - 1
    item_row = first_row + lax.broadcasted_iota(jnp.int32, (rows, 128), 0)
    item_base = (g * lay.batches + lax.broadcasted_iota(jnp.int32, (rows, 128), 1)) * listed
    common = ((item_base + itself) * 16 + item_row) << 12
    first = jnp.where(one, codes[0], jnp.where(two, codes[1], jnp.where(three, codes[2], NONE)))
    more = (one & two) | ((one | two) & three)
    second = jnp.where(one & two, codes[1], codes[2])
    third = jnp.where(one & two & three, codes[2], NONE)
    exists = itself >= 0
    units = (
        jnp.where(exists, common + (itself << 6) + first, -1),
        jnp.where(exists & more, common + (second << 6) + third, -1),
    )
    live = lane < block[lay.meta : lay.meta + 1, 0:1].astype(jnp.int32)
    result = jnp.full((listed, 128), -1, jnp.int32)
    for number, unit in enumerate(units):
        found = jnp.full((listed, 128), -1, jnp.int32)
        for w in range(rows):
            found = jnp.where(window == first_row + w, unit[w : w + 1], found)
        found = jnp.where(live, found, -1)
        begin = LANES * number
        result = jnp.where(lane < begin, result, pltpu.roll(found, begin, 1))
    return result


def list_entries(lay, coded, begin, entries, total):
    for t in range(lay.batches):
        for b in range(lay.listed):
            entry = coded[b, begin + t]
            entries[total] = entry
            total = total + 1 + (entry >> 31)
    return total


def live_batches(lay, pack):
    return jnp.minimum(pack[lay.basis + lay.meta, 128].astype(jnp.int32), lay.batches)


def list_scalars(lay, scalars, begin, live, entries, total):
    def visit(t, total):
        for entry in [scalars[b, begin + t] for b in range(lay.listed)]:
            entries[total] = entry
            total = total + 1 + (entry >> 31)
        return total

    return lax.fori_loop(0, live, visit, total)


def list_units(lay, scalars, begin, t, units, total):
    t = jnp.minimum(t, LANES - 1)
    found = [
        scalars[b, begin + lane + t] for b in range(lay.listed) for lane in (0, LANES)
    ]
    for unit in found:
        units[total] = unit
        total = total + 1 + (unit >> 31)
    return total


def spread_columns(lay, place, g, pack, columns):
    rows = lay.rows
    table = pack[lay.basis : lay.basis + 4 * rows, :128]
    count, first, owner = rows, 0, (place.own, place.pair, place.far)[g]
    if g == 2:
        count, first = REACH, place.far_first
        table = jnp.where(place.even, table[4 * (rows - count) :], table[: 4 * count])
    table = table.T
    for w in range(count):
        for c in range(4):
            column = table[:, 4 * w + c : 4 * w + c + 1]
            if c == 0:
                column = column + (owner * rows + first + w).astype(jnp.float32)
            if c == 3:
                column = -column
            columns[g * rows + w, c] = jnp.broadcast_to(column, (lay.orbitals, 128))


def spread_points(lay, g, pack, points):
    for t in range(lay.batches):
        points[g * lay.batches + t, 0:3, :] = pack[3 * t : 3 * t + 3, :]


def work_out(lay, entries, total, points, columns, orb, scalars, groups, units, live):
    for u in range(PAIRED):
        entries[total + u] = lay.trash * 32
    steps = (total + PAIRED - 1) // PAIRED
    steps = jnp.maximum(steps, live)

    def some(step, ends):
        for u in range(PAIRED):
            index = jnp.minimum(step * PAIRED + u, total)
            slot, column = split(entries[index], 32)
            batch = jnp.minimum(split(slot, lay.listed)[0], 3 * lay.batches - 1)
            at = [points[batch, c : c + 1, :] for c in range(3)]
            for begin in range(0, lay.orbitals, 16):
                lines = pl.ds(begin, 16)
                centre = [columns[column, c, lines, :] for c in range(4)]
                for half in range(0, lay.points, 128):
                    distance = (at[0][:, half : half + 128] - centre[0]) ** 2
                    distance = distance + (at[1][:, half : half + 128] - centre[1]) ** 2
                    distance = distance + (at[2][:, half : half + 128] - centre[2]) ** 2
                    result = jnp.exp(centre[3] * distance)
                    orb[slot, lines, half : half + 128] = result.astype(jnp.bfloat16)
        return [
            list_units(lay, scalars, begin, step, target, end)
            for begin, target, end in zip(groups, units, ends)
        ]

    return lax.fori_loop(0, steps, some, [jnp.int32(0)] * len(groups))


def own_kernel(lay, pack, orb, columns, points, coded, entries):
    place = Place(lay)
    coded[...] = code_entries(
        lay, place, 0, block_of(lay, pack), None, lambda window, partner: window < lay.rows
    )[0]
    orb[lay.blank] = jnp.zeros(orb.shape[1:], orb.dtype)
    spread_columns(lay, place, 0, pack, columns)
    spread_points(lay, 0, pack, points)
    total = list_entries(lay, coded, 0, entries, jnp.int32(0))
    work_out(lay, entries, total, points, columns, orb, None, (), (), 0)


def first_kernel(
    lay,
    pack_own,
    pack_pair,
    pack_far,
    density_own,
    density_pair,
    orb_in,
    columns_in,
    part,
    orb,
    columns,
    units_own_out,
    units_far_out,
    points,
    density,
    rho,
    units_own,
    units_far,
    units_rest,
    coded,
    scalars,
    entries,
    scalar_sem,
    density_sems,
    units_sems,
):
    rows, listed = lay.rows, lay.listed
    density_copies = [
        pltpu.make_async_copy(source, density.at[pl.ds(g * rows, rows)], density_sems.at[g])
        for g, source in enumerate((density_own, density_pair))
    ]
    for copy in density_copies:
        copy.start()
    place = Place(lay)
    blocks = [block_of(lay, pack) for pack in (pack_own, pack_pair, pack_far)]
    own_choice = partner_choice(lay, place, blocks[0])
    pair_choice = partner_choice(lay, place, blocks[1])
    of_far, window, held = code_entries(
        lay, place, 2, blocks[2], own_choice, lambda window, partner: (window < rows) | partner
    )
    entries_far = of_far
    of_far = code_units(lay, 2, blocks[2], window, held, own_choice, 0)
    entries_rest, window, held = code_entries(
        lay,
        place,
        0,
        blocks[0],
        own_choice,
        lambda window, partner: (window >= rows) & ((window < 2 * rows) | partner),
    )
    of_own = code_units(lay, 0, blocks[0], window, held, own_choice, 0)
    of_rest = code_units(lay, 0, blocks[0], window, held, pair_choice, rows)
    lane = lax.broadcasted_iota(jnp.int32, of_far.shape, 1)
    coded[...] = jnp.where(
        lane < 2 * LANES,
        of_own,
        jnp.where(
            lane < 4 * LANES,
            pltpu.roll(of_far, 2 * LANES, 1),
            jnp.where(
                lane < 6 * LANES,
                pltpu.roll(of_rest, 4 * LANES, 1),
                jnp.where(
                    lane < 7 * LANES,
                    pltpu.roll(entries_far, 6 * LANES, 1),
                    pltpu.roll(entries_rest, 7 * LANES, 1),
                ),
            ),
        ),
    )
    scalar_copy = pltpu.make_async_copy(coded, scalars, scalar_sem)
    scalar_copy.start()
    spread_columns(lay, place, 1, pack_pair, columns)
    spread_columns(lay, place, 2, pack_far, columns)
    spread_points(lay, 0, pack_own, points)
    spread_points(lay, 2, pack_far, points)
    rho[...] = jnp.zeros_like(rho)
    far_live, own_live = live_batches(lay, pack_far), live_batches(lay, pack_own)
    scalar_copy.wait()
    total = list_scalars(lay, scalars, 6 * LANES, far_live, entries, jnp.int32(0))
    total = list_scalars(lay, scalars, 7 * LANES, own_live, entries, total)
    lists = (units_own, units_far, units_rest)
    ends = work_out(
        lay,
        entries,
        total,
        points,
        columns,
        orb,
        scalars,
        (0, 2 * LANES, 4 * LANES),
        lists,
        jnp.maximum(far_live, own_live),
    )
    units_own[lay.units + 1] = ends[0]
    units_far[lay.units + 1] = ends[1]
    units_copies = [
        pltpu.make_async_copy(source, target, units_sems.at[number])
        for number, (source, target) in enumerate(
            ((units_own, units_own_out), (units_far, units_far_out))
        )
    ]
    for copy in units_copies:
        copy.start()
    for copy in density_copies:
        copy.wait()
    one = ends[0]
    two = one + ends[1]
    end = two + ends[2]

    def fold(step, carry):
        sums = []
        for u in range(UNROLL):
            index = step * UNROLL + u
            word = pick(
                lay, index, ((units_own, 0), (units_far, one), (units_rest, two)), end
            )
            slot, row, (k1, o1), (k2, o2) = decode(lay, word)
            others = jnp.concatenate([orb[o1], orb[o2]], axis=0)
            stored = jnp.concatenate([density[row, k1], density[row, k2]], axis=1)
            folded = jnp.dot(stored, others, preferred_element_type=jnp.float32)
            product = orb[slot].astype(jnp.float32) * folded
            total = product[0:8]
            for begin in range(8, lay.orbitals, 8):
                total = total + product[begin : begin + 8]
            sums.append((split(slot, listed)[0], total))
        for number, total in sums:
            rho[number] = rho[number] + total
        return carry

    lax.fori_loop(0, (end + UNROLL - 1) // UNROLL, fold, 0)
    part[: lay.batches, :] = jnp.sum(rho[: lay.batches], axis=1)
    part[lay.batches :, :] = jnp.sum(rho[2 * lay.batches : 3 * lay.batches], axis=1)
    for copy in units_copies:
        copy.wait()


def pair_kernel(
    lay,
    pack_own,
    pack_pair,
    orb_in,
    columns,
    orb,
    units,
    points,
    coded,
    scalars,
    entries,
    sem,
):
    place = Place(lay)
    choice = partner_choice(lay, place, block_of(lay, pack_own))
    block = block_of(lay, pack_pair)
    result, window, held = code_entries(
        lay, place, 1, block, choice, lambda window, partner: (window < lay.rows) | partner
    )
    units_found = code_units(lay, 1, block, window, held, choice, 0)
    lane = lax.broadcasted_iota(jnp.int32, result.shape, 1)
    coded[...] = jnp.where(lane < 2 * LANES, units_found, pltpu.roll(result, 2 * LANES, 1))
    copy = pltpu.make_async_copy(coded, scalars, sem)
    copy.start()
    spread_points(lay, 1, pack_pair, points)
    live = live_batches(lay, pack_pair)
    copy.wait()
    total = list_scalars(lay, scalars, 2 * LANES, live, entries, jnp.int32(0))
    (end,) = work_out(lay, entries, total, points, columns, orb, scalars, (0,), (units,), live)
    units[lay.units + 1] = end


def total_kernel(lay, part, arrived, units, out):
    out[...] = part[: lay.batches] + arrived[lay.batches :]


def pick(lay, index, lists, total):
    word, end = jnp.int32(lay.empty), total
    for units, begin in reversed(lists):
        word = jnp.where(index < end, units[jnp.clip(index - begin, 0, lay.units - 1)], word)
        end = begin
    return word


def decode(lay, word):
    slot = word >> 16
    row = (word >> 12) & 15
    base = slot & ~(lay.listed - 1)
    partners = []
    for shift in (6, 0):
        inner = (word >> shift) & 15
        partners.append(
            ((word >> (shift + 4)) & 3, jnp.where(inner == NONE, lay.blank, base + inner))
        )
    return slot, row, *partners


def cube_root(x):
    size = jnp.abs(x)
    safe = jnp.where(size > 0.0, size, 1.0)
    root = jnp.exp2(jnp.log2(safe) * (1.0 / 3.0))
    root = root - (root - safe / (root * root)) * (1.0 / 3.0)
    root = jnp.where(size > 0.0, root, 0.0)
    return jnp.where(x < 0.0, -root, root)


def second_kernel(
    lay,
    pack_own,
    pack_pair,
    pack_far,
    part,
    arrived,
    pair_rho,
    orb,
    units_given,
    out,
    potential,
    units_held,
    sems,
):
    copies = [
        pltpu.make_async_copy(source, target, sems.at[number])
        for number, (source, target) in enumerate(zip(units_given, units_held))
    ]
    for copy in copies:
        copy.start()
    packs = (pack_own, pack_pair, pack_far)
    n = lay.batches
    density_values = (part[:n] + arrived[n:], pair_rho[...], part[n:] + arrived[:n])
    potential[...] = jnp.zeros_like(potential)
    for g in range(3):
        weights = packs[g][lay.weights : lay.weights + n, :]
        potential[g * n : (g + 1) * n, :] = -exchange_coef * cube_root(density_values[g]) * weights
    out[...] = jnp.zeros_like(out)
    for copy in copies:
        copy.wait()
    units_own, units_first, units_pair = units_held
    one = units_own[lay.units + 1]
    two = one + units_first[lay.units + 1]
    total = two + units_pair[lay.units + 1]

    def contribute(step, carry):
        for u in range(UNROLL):
            index = step * UNROLL + u
            word = pick(
                lay, index, ((units_own, 0), (units_first, one), (units_pair, two)), total
            )
            slot, row, (k1, o1), (k2, o2) = decode(lay, word)
            others = jnp.concatenate([orb[o1], orb[o2]], axis=0)
            scale = potential[pl.ds(split(slot, lay.listed)[0], 1), :]
            weighted = (orb[slot].astype(jnp.float32) * scale).astype(jnp.bfloat16)
            contrib = lax.dot_general(
                weighted, others, (((1,), (1,)), ((), ())), preferred_element_type=jnp.float32
            )
            out[row, k1] += contrib[:, : lay.orbitals]
            out[row, k2] += contrib[:, lay.orbitals :]
        return carry

    lax.fori_loop(0, (total + UNROLL - 1) // UNROLL, contribute, 0)


def on_device(counts, points, weights, block_lists, pattern, basis_table, density):
    batches, listed = block_lists.shape
    rows, partners = pattern.shape
    orbitals = basis_table.shape[2]
    lay = Layout(batches, listed, points.shape[2], rows, partners, orbitals)
    devices = lax.axis_size("space")
    in_vmem = pl.BlockSpec(memory_space=VMEM)
    in_smem = pl.BlockSpec(memory_space=SMEM)
    in_hbm = pl.BlockSpec(memory_space=HBM)
    cost = pl.CostEstimate(flops=10**10, bytes_accessed=0, transcendentals=0)

    def params(limit=LIMIT):
        return pltpu.CompilerParams(vmem_limit_bytes=limit)

    pair_route = [(i, i ^ 1) for i in range(devices)]
    far_route = [
        (i, i + 1 if i % 2 else i - 1)
        for i in range(devices)
        if 0 <= (i + 1 if i % 2 else i - 1) < devices
    ]

    inputs = (counts, points, weights, block_lists.T, pattern.T, basis_table)
    pack = pl.pallas_call(
        functools.partial(pack_kernel, lay),
        out_shape=jax.ShapeDtypeStruct((lay.height, lay.points), jnp.float32),
        in_specs=[in_hbm] * 6,
        out_specs=in_vmem,
        scratch_shapes=[
            [SMEM(counts.shape, counts.dtype)] + [VMEM(x.shape, x.dtype) for x in inputs[1:]],
            pltpu.SemaphoreType.DMA((6,)),
        ],
        compiler_params=params(WHOLE),
        name="pack",
    )(*inputs)
    pack_far = lax.ppermute(pack, "space", far_route)
    pack_pair = lax.ppermute(pack, "space", pair_route)
    pack, density = lax.optimization_barrier((pack, density))
    density_pair = lax.ppermute(density, "space", pair_route)

    orb_shape = jax.ShapeDtypeStruct((lay.slots + 2, orbitals, lay.points), jnp.bfloat16)
    columns_shape = jax.ShapeDtypeStruct((lay.columns, 4, orbitals, 128), jnp.float32)
    anywhere = pl.BlockSpec(memory_space=pl.ANY)
    units_shape = jax.ShapeDtypeStruct((lay.units + 2,), jnp.int32)

    def scratch(groups):
        return [
            VMEM((listed, 128), jnp.int32),
            SMEM((listed, 128), jnp.int32),
            SMEM((groups * batches * listed + PAIRED,), jnp.int32),
            pltpu.SemaphoreType.DMA(()),
        ]

    points_scratch = VMEM((3 * batches, 8, lay.points), jnp.float32)
    orb, columns = pl.pallas_call(
        functools.partial(own_kernel, lay),
        out_shape=(orb_shape, columns_shape),
        in_specs=[in_vmem],
        out_specs=(in_vmem, in_vmem),
        scratch_shapes=[
            points_scratch,
            VMEM((listed, 128), jnp.int32),
            SMEM((batches * listed + PAIRED,), jnp.int32),
        ],
        compiler_params=params(),
        cost_estimate=cost,
        name="first_own",
    )(pack)

    part, orb, columns, units_own, units_first = pl.pallas_call(
        functools.partial(first_kernel, lay),
        out_shape=(
            jax.ShapeDtypeStruct((2 * batches, lay.points), jnp.float32),
            orb_shape,
            columns_shape,
            units_shape,
            units_shape,
        ),
        in_specs=[in_vmem] * 3 + [in_hbm, in_hbm, in_vmem, in_vmem],
        out_specs=(in_vmem, in_vmem, in_vmem, anywhere, anywhere),
        scratch_shapes=[
            points_scratch,
            VMEM((2 * rows, partners, orbitals, orbitals), jnp.bfloat16),
            VMEM((3 * batches + 1, 8, lay.points), jnp.float32),
            *[SMEM(units_shape.shape, jnp.int32)] * 3,
            *scratch(2),
            pltpu.SemaphoreType.DMA((2,)),
            pltpu.SemaphoreType.DMA((2,)),
        ],
        input_output_aliases={5: 1, 6: 2},
        compiler_params=params(BUSY),
        cost_estimate=cost,
        name="first",
    )(pack, pack_pair, pack_far, density, density_pair, orb, columns)

    arrived = lax.ppermute(part, "space", far_route)
    orb, units_pair = pl.pallas_call(
        functools.partial(pair_kernel, lay),
        out_shape=(orb_shape, units_shape),
        in_specs=[in_vmem] * 4,
        out_specs=(in_vmem, in_smem),
        scratch_shapes=[points_scratch, *scratch(1)],
        input_output_aliases={2: 0},
        compiler_params=params(),
        cost_estimate=cost,
        name="first_pair",
    )(pack, pack_pair, orb, columns)
    own_rho = pl.pallas_call(
        functools.partial(total_kernel, lay),
        out_shape=jax.ShapeDtypeStruct((batches, lay.points), jnp.float32),
        in_specs=[in_vmem, in_vmem, anywhere],
        out_specs=in_vmem,
        compiler_params=params(1 << 20),
        name="total",
    )(part, arrived, units_pair)
    pair_rho = lax.ppermute(own_rho, "space", pair_route)

    return pl.pallas_call(
        functools.partial(second_kernel, lay),
        out_shape=jax.ShapeDtypeStruct(density.shape, jnp.float32),
        in_specs=[in_vmem] * 7 + [[anywhere] * 3],
        out_specs=in_vmem,
        scratch_shapes=[
            VMEM((-(-(3 * batches + 1) // 8) * 8, lay.points), jnp.float32),
            [SMEM(units_shape.shape, jnp.int32)] * 3,
            pltpu.SemaphoreType.DMA((3,)),
        ],
        compiler_params=params(),
        name="second",
    )(
        pack,
        pack_pair,
        pack_far,
        part,
        arrived,
        pair_rho,
        orb,
        [units_own, units_first, units_pair],
    )


def solution(mesh):
    in_specs = (
        P(("parts", "space")),
        P(("parts", "space"), None, None),
        P(("parts", "space"), None),
        P(("parts", "space"), None),
        P(("parts", "space"), None),
        P(("parts", "space"), None, None),
        P(("parts", "space"), None, None, None),
    )
    out_specs = P(("parts", "space"), None, None, None)
    return jax.shard_map(
        on_device, mesh=mesh, in_specs=in_specs, out_specs=out_specs, check_vma=False
    )
```

```python
import functools
import math

import jax
import jax.numpy as jnp
from jax import lax
from jax.experimental import pallas as pl
from jax.experimental.pallas import tpu as pltpu
from jax.sharding import PartitionSpec as P

exchange_coef = (3.0 / math.pi) ** (1.0 / 3.0)
VMEM = pltpu.VMEM
SMEM = pltpu.SMEM
HBM = pltpu.HBM
LIMIT = 12 << 20
WHOLE = 63 << 20
BUSY = 12 << 20
REACH = 3
UNROLL = 16
PAIRED = 3
LANES = 16
NOWHERE, ELSEWHERE = 31, 30
NONE = 15


def split(value, size):
    if size & (size - 1):
        quotient = value // size
        return quotient, value - quotient * size
    return lax.shift_right_logical(value, size.bit_length() - 1), value & (size - 1)


class Layout:
    def __init__(self, batches, listed, points, rows, partners, orbitals):
        self.batches, self.listed, self.points = batches, listed, points
        self.rows, self.partners, self.orbitals = rows, partners, orbitals
        self.weights = -(-3 * batches // 8) * 8
        self.basis = self.weights + -(-batches // 8) * 8
        self.lists = 0
        self.pattern = -(-listed // 8) * 8
        self.meta = self.pattern + -(-partners // 8) * 8
        self.scalar_rows = -(-max(4 * rows, self.meta + 1) // 8) * 8
        self.height = self.basis + self.scalar_rows
        self.slots = 3 * batches * listed
        self.blank, self.trash = self.slots, self.slots + 1
        self.columns = 2 * rows + REACH
        self.units = 2 * batches * listed
        self.empty = (self.blank * 16) << 12 | NONE << 6 | NONE


def pack_kernel(lay, counts, points, weights, lists, pattern, basis, out, held, sems):
    copies = [
        pltpu.make_async_copy(source, target, sems.at[number])
        for number, (source, target) in enumerate(
            zip((counts, points, weights, lists, pattern, basis), held)
        )
    ]
    for copy in copies:
        copy.start()
    out[...] = jnp.zeros_like(out)
    me = lax.axis_index("space")
    for copy in copies:
        copy.wait()
    counts, points, weights, lists, pattern, basis = held
    for t in range(lay.batches):
        out[3 * t : 3 * t + 3, :] = points[t]
    out[lay.weights : lay.weights + lay.batches, :] = weights[...]
    for w in range(lay.rows):
        out[lay.basis + 4 * w : lay.basis + 4 * w + 4, :128] = basis[w].astype(jnp.float32)
    begin = lay.basis + lay.lists
    out[begin : begin + lay.listed, 128 : 128 + lay.batches] = lists[...].astype(jnp.float32)
    begin = lay.basis + lay.pattern
    out[begin : begin + lay.partners, 128 : 128 + lay.rows] = pattern[...].astype(jnp.float32)
    begin = lay.basis + lay.meta
    lane = lax.broadcasted_iota(jnp.int32, (1, 128), 1)
    meta = jnp.where(lane == 0, counts[0], jnp.where(lane == 1, me, 0))
    out[begin : begin + 1, 128:256] = meta.astype(jnp.float32)


class Place:
    def __init__(self, lay):
        self.lay = lay
        self.own = lax.axis_index("space")
        self.pair = self.own ^ 1
        even = self.own % 2 == 0
        self.even = even
        self.far = jnp.where(even, self.own - 1, self.own + 1)
        self.far_first = jnp.where(even, lay.rows - REACH, 0)

    def window(self, raw, outside):
        rows = self.lay.rows
        owner, inner = split(raw, rows)
        far = jnp.where(owner == self.far, 2 * rows + inner, outside)
        return jnp.where(owner == self.own, inner, jnp.where(owner == self.pair, rows + inner, far))


def block_of(lay, pack):
    return pack[lay.basis : lay.basis + lay.scalar_rows, 128:256]


def partner_choice(lay, place, block):
    raw = block[lay.pattern : lay.pattern + 8].astype(jnp.int32)
    turned = place.window(raw, ELSEWHERE).astype(jnp.float32).T
    lane = lax.broadcasted_iota(jnp.int32, (lay.rows, 32), 1).astype(jnp.float32)
    return jnp.concatenate(
        [
            jnp.where(turned[: lay.rows, k : k + 1] == lane, 1.0, 0.0)
            for k in range(1, lay.partners)
        ],
        axis=0,
    ).astype(jnp.bfloat16)


def code_entries(lay, place, g, block, own_choice, wanted):
    listed, rows = lay.listed, lay.rows
    raw = block.astype(jnp.int32)
    window = place.window(raw[lay.lists : lay.lists + listed], NOWHERE)
    lane = lax.broadcasted_iota(jnp.int32, (listed, 128), 1)
    position = lax.broadcasted_iota(jnp.int32, (listed, 128), 0)
    column = jnp.where(window < 2 * rows, window, window - place.far_first)
    entry = ((g * lay.batches + lane) * listed + position) * 32 + column
    if own_choice is None:
        result = jnp.where(wanted(window, None), entry, -1)
        held = None
    else:
        line = lax.broadcasted_iota(jnp.int32, (32, 128), 0)
        held = jnp.zeros((32, 128), jnp.int32)
        for b in range(listed):
            held = jnp.where(line == window[b : b + 1], b + 1, held)
        there = jnp.where(held[:rows] > 0, 1.0, 0.0).astype(jnp.bfloat16)
        partner_of = lax.dot_general(
            own_choice,
            jnp.concatenate([there] * (lay.partners - 1), axis=0),
            (((0,), (0,)), ((), ())),
            preferred_element_type=jnp.float32,
        )
        partner = jnp.zeros((listed, 128), jnp.float32)
        for w in range(rows, 3 * rows):
            partner = jnp.where(window == w, partner_of[w : w + 1], partner)
        result = jnp.where(wanted(window, partner > 0.5), entry, -1)
    live = lane < raw[lay.meta : lay.meta + 1, 0:1]
    return jnp.where(live, result, -1), window, held


def code_units(lay, g, block, window, held, choice, first_row):
    listed, rows = lay.listed, lay.rows
    lane = lax.broadcasted_iota(jnp.int32, (listed, 128), 1)
    others = jnp.dot(
        choice, held.astype(jnp.float32).astype(jnp.bfloat16), preferred_element_type=jnp.float32
    ).astype(jnp.int32)
    codes = [
        (k * 16 - 1) + others[(k - 1) * rows : k * rows] for k in range(1, lay.partners)
    ]
    one, two, three = [others[(k - 1) * rows : k * rows] > 0 for k in range(1, lay.partners)]
    itself = held[first_row : first_row + rows] - 1
    item_row = first_row + lax.broadcasted_iota(jnp.int32, (rows, 128), 0)
    item_base = (g * lay.batches + lax.broadcasted_iota(jnp.int32, (rows, 128), 1)) * listed
    common = ((item_base + itself) * 16 + item_row) << 12
    first = jnp.where(one, codes[0], jnp.where(two, codes[1], jnp.where(three, codes[2], NONE)))
    more = (one & two) | ((one | two) & three)
    second = jnp.where(one & two, codes[1], codes[2])
    third = jnp.where(one & two & three, codes[2], NONE)
    exists = itself >= 0
    units = (
        jnp.where(exists, common + (itself << 6) + first, -1),
        jnp.where(exists & more, common + (second << 6) + third, -1),
    )
    live = lane < block[lay.meta : lay.meta + 1, 0:1].astype(jnp.int32)
    result = jnp.full((listed, 128), -1, jnp.int32)
    for number, unit in enumerate(units):
        found = jnp.full((listed, 128), -1, jnp.int32)
        for w in range(rows):
            found = jnp.where(window == first_row + w, unit[w : w + 1], found)
        found = jnp.where(live, found, -1)
        begin = LANES * number
        result = jnp.where(lane < begin, result, pltpu.roll(found, begin, 1))
    return result


def list_entries(lay, coded, begin, entries, total):
    for t in range(lay.batches):
        for b in range(lay.listed):
            entry = coded[b, begin + t]
            entries[total] = entry
            total = total + 1 + (entry >> 31)
    return total


def live_batches(lay, pack):
    return jnp.minimum(pack[lay.basis + lay.meta, 128].astype(jnp.int32), lay.batches)


def list_scalars(lay, scalars, begin, live, entries, total):
    def visit(t, total):
        for entry in [scalars[b, begin + t] for b in range(lay.listed)]:
            entries[total] = entry
            total = total + 1 + (entry >> 31)
        return total

    return lax.fori_loop(0, live, visit, total)


def list_units(lay, scalars, begin, t, units, total):
    t = jnp.minimum(t, LANES - 1)
    found = [
        scalars[b, begin + lane + t] for b in range(lay.listed) for lane in (0, LANES)
    ]
    for unit in found:
        units[total] = unit
        total = total + 1 + (unit >> 31)
    return total


def spread_columns(lay, place, g, pack, columns):
    rows = lay.rows
    table = pack[lay.basis : lay.basis + 4 * rows, :128]
    count, first, owner = rows, 0, (place.own, place.pair, place.far)[g]
    if g == 2:
        count, first = REACH, place.far_first
        table = jnp.where(place.even, table[4 * (rows - count) :], table[: 4 * count])
    table = table.T
    for w in range(count):
        for c in range(4):
            column = table[:, 4 * w + c : 4 * w + c + 1]
            if c == 0:
                column = column + (owner * rows + first + w).astype(jnp.float32)
            if c == 3:
                column = -column
            columns[g * rows + w, c] = jnp.broadcast_to(column, (lay.orbitals, 128))


def spread_points(lay, g, pack, points):
    for t in range(lay.batches):
        points[g * lay.batches + t, 0:3, :] = pack[3 * t : 3 * t + 3, :]


def work_out(lay, entries, total, points, columns, orb, scalars, groups, units, live):
    for u in range(PAIRED):
        entries[total + u] = lay.trash * 32
    steps = (total + PAIRED - 1) // PAIRED
    steps = jnp.maximum(steps, live)

    def some(step, ends):
        for u in range(PAIRED):
            index = jnp.minimum(step * PAIRED + u, total)
            slot, column = split(entries[index], 32)
            batch = jnp.minimum(split(slot, lay.listed)[0], 3 * lay.batches - 1)
            at = [points[batch, c : c + 1, :] for c in range(3)]
            for begin in range(0, lay.orbitals, 16):
                lines = pl.ds(begin, 16)
                centre = [columns[column, c, lines, :] for c in range(4)]
                for half in range(0, lay.points, 128):
                    distance = (at[0][:, half : half + 128] - centre[0]) ** 2
                    distance = distance + (at[1][:, half : half + 128] - centre[1]) ** 2
                    distance = distance + (at[2][:, half : half + 128] - centre[2]) ** 2
                    result = jnp.exp(centre[3] * distance)
                    orb[slot, lines, half : half + 128] = result.astype(jnp.bfloat16)
        return [
            list_units(lay, scalars, begin, step, target, end)
            for begin, target, end in zip(groups, units, ends)
        ]

    return lax.fori_loop(0, steps, some, [jnp.int32(0)] * len(groups))


def own_kernel(lay, pack, orb, columns, points, coded, entries):
    place = Place(lay)
    coded[...] = code_entries(
        lay, place, 0, block_of(lay, pack), None, lambda window, partner: window < lay.rows
    )[0]
    orb[lay.blank] = jnp.zeros(orb.shape[1:], orb.dtype)
    spread_columns(lay, place, 0, pack, columns)
    spread_points(lay, 0, pack, points)
    total = list_entries(lay, coded, 0, entries, jnp.int32(0))
    work_out(lay, entries, total, points, columns, orb, None, (), (), 0)


def first_kernel(
    lay,
    pack_own,
    pack_pair,
    pack_far,
    density_own,
    density_pair,
    orb_in,
    columns_in,
    part,
    orb,
    columns,
    units_own_out,
    units_far_out,
    points,
    density,
    rho,
    units_own,
    units_far,
    units_rest,
    coded,
    scalars,
    entries,
    scalar_sem,
    density_sems,
    units_sems,
):
    rows, listed = lay.rows, lay.listed
    density_copies = [
        pltpu.make_async_copy(source, density.at[pl.ds(g * rows, rows)], density_sems.at[g])
        for g, source in enumerate((density_own, density_pair))
    ]
    for copy in density_copies:
        copy.start()
    place = Place(lay)
    blocks = [block_of(lay, pack) for pack in (pack_own, pack_pair, pack_far)]
    own_choice = partner_choice(lay, place, blocks[0])
    pair_choice = partner_choice(lay, place, blocks[1])
    of_far, window, held = code_entries(
        lay, place, 2, blocks[2], own_choice, lambda window, partner: (window < rows) | partner
    )
    entries_far = of_far
    of_far = code_units(lay, 2, blocks[2], window, held, own_choice, 0)
    entries_rest, window, held = code_entries(
        lay,
        place,
        0,
        blocks[0],
        own_choice,
        lambda window, partner: (window >= rows) & ((window < 2 * rows) | partner),
    )
    of_own = code_units(lay, 0, blocks[0], window, held, own_choice, 0)
    of_rest = code_units(lay, 0, blocks[0], window, held, pair_choice, rows)
    lane = lax.broadcasted_iota(jnp.int32, of_far.shape, 1)
    coded[...] = jnp.where(
        lane < 2 * LANES,
        of_own,
        jnp.where(
            lane < 4 * LANES,
            pltpu.roll(of_far, 2 * LANES, 1),
            jnp.where(
                lane < 6 * LANES,
                pltpu.roll(of_rest, 4 * LANES, 1),
                jnp.where(
                    lane < 7 * LANES,
                    pltpu.roll(entries_far, 6 * LANES, 1),
                    pltpu.roll(entries_rest, 7 * LANES, 1),
                ),
            ),
        ),
    )
    scalar_copy = pltpu.make_async_copy(coded, scalars, scalar_sem)
    scalar_copy.start()
    spread_columns(lay, place, 1, pack_pair, columns)
    spread_columns(lay, place, 2, pack_far, columns)
    spread_points(lay, 0, pack_own, points)
    spread_points(lay, 2, pack_far, points)
    rho[...] = jnp.zeros_like(rho)
    far_live, own_live = live_batches(lay, pack_far), live_batches(lay, pack_own)
    scalar_copy.wait()
    total = list_scalars(lay, scalars, 6 * LANES, far_live, entries, jnp.int32(0))
    total = list_scalars(lay, scalars, 7 * LANES, own_live, entries, total)
    lists = (units_own, units_far, units_rest)
    ends = work_out(
        lay,
        entries,
        total,
        points,
        columns,
        orb,
        scalars,
        (0, 2 * LANES, 4 * LANES),
        lists,
        jnp.maximum(far_live, own_live),
    )
    units_own[lay.units + 1] = ends[0]
    units_far[lay.units + 1] = ends[1]
    units_copies = [
        pltpu.make_async_copy(source, target, units_sems.at[number])
        for number, (source, target) in enumerate(
            ((units_own, units_own_out), (units_far, units_far_out))
        )
    ]
    for copy in units_copies:
        copy.start()
    for copy in density_copies:
        copy.wait()
    one = ends[0]
    two = one + ends[1]
    end = two + ends[2]

    def fold(start, count):
        sums = []
        for u in range(count):
            index = start + u
            word = pick(
                lay, index, ((units_own, 0), (units_far, one), (units_rest, two)), end
            )
            slot, row, (k1, o1), (k2, o2) = decode(lay, word)
            others = jnp.concatenate([orb[o1], orb[o2]], axis=0)
            stored = jnp.concatenate([density[row, k1], density[row, k2]], axis=1)
            folded = jnp.dot(stored, others, preferred_element_type=jnp.float32)
            product = orb[slot].astype(jnp.float32) * folded
            total = product[0:8]
            for begin in range(8, lay.orbitals, 8):
                total = total + product[begin : begin + 8]
            sums.append((split(slot, listed)[0], total))
        for number, total in sums:
            rho[number] = rho[number] + total

    over_units(end, fold)
    part[: lay.batches, :] = jnp.sum(rho[: lay.batches], axis=1)
    part[lay.batches :, :] = jnp.sum(rho[2 * lay.batches : 3 * lay.batches], axis=1)
    for copy in units_copies:
        copy.wait()


def pair_kernel(
    lay,
    pack_own,
    pack_pair,
    orb_in,
    columns,
    orb,
    units,
    points,
    coded,
    scalars,
    entries,
    sem,
):
    place = Place(lay)
    choice = partner_choice(lay, place, block_of(lay, pack_own))
    block = block_of(lay, pack_pair)
    result, window, held = code_entries(
        lay, place, 1, block, choice, lambda window, partner: (window < lay.rows) | partner
    )
    units_found = code_units(lay, 1, block, window, held, choice, 0)
    lane = lax.broadcasted_iota(jnp.int32, result.shape, 1)
    coded[...] = jnp.where(lane < 2 * LANES, units_found, pltpu.roll(result, 2 * LANES, 1))
    copy = pltpu.make_async_copy(coded, scalars, sem)
    copy.start()
    spread_points(lay, 1, pack_pair, points)
    live = live_batches(lay, pack_pair)
    copy.wait()
    total = list_scalars(lay, scalars, 2 * LANES, live, entries, jnp.int32(0))
    (end,) = work_out(lay, entries, total, points, columns, orb, scalars, (0,), (units,), live)
    units[lay.units + 1] = end


def total_kernel(lay, part, arrived, units, out):
    out[...] = part[: lay.batches] + arrived[lay.batches :]


def over_units(total, body):
    def some(start, count, step, carry):
        body(start + step * count, count)
        return carry

    whole, rest = split(total, UNROLL)
    steps = whole + jnp.where(rest > UNROLL // 2, 1, 0)
    short = jnp.where((rest > 0) & (rest <= UNROLL // 2), 1, 0)
    lax.fori_loop(0, steps, functools.partial(some, 0, UNROLL), 0)
    lax.fori_loop(0, short, functools.partial(some, steps * UNROLL, UNROLL // 2), 0)


def pick(lay, index, lists, total):
    word, end = jnp.int32(lay.empty), total
    for units, begin in reversed(lists):
        word = jnp.where(index < end, units[jnp.clip(index - begin, 0, lay.units - 1)], word)
        end = begin
    return word


def decode(lay, word):
    slot = word >> 16
    row = (word >> 12) & 15
    base = slot & ~(lay.listed - 1)
    partners = []
    for shift in (6, 0):
        inner = (word >> shift) & 15
        partners.append(
            ((word >> (shift + 4)) & 3, jnp.where(inner == NONE, lay.blank, base + inner))
        )
    return slot, row, *partners


def cube_root(x):
    size = jnp.abs(x)
    safe = jnp.where(size > 0.0, size, 1.0)
    root = jnp.exp2(jnp.log2(safe) * (1.0 / 3.0))
    root = root - (root - safe / (root * root)) * (1.0 / 3.0)
    root = jnp.where(size > 0.0, root, 0.0)
    return jnp.where(x < 0.0, -root, root)


def second_kernel(
    lay,
    pack_own,
    pack_pair,
    pack_far,
    part,
    arrived,
    pair_rho,
    orb,
    units_given,
    out,
    potential,
    units_held,
    sems,
):
    copies = [
        pltpu.make_async_copy(source, target, sems.at[number])
        for number, (source, target) in enumerate(zip(units_given, units_held))
    ]
    for copy in copies:
        copy.start()
    packs = (pack_own, pack_pair, pack_far)
    n = lay.batches
    density_values = (part[:n] + arrived[n:], pair_rho[...], part[n:] + arrived[:n])
    potential[...] = jnp.zeros_like(potential)
    for g in range(3):
        weights = packs[g][lay.weights : lay.weights + n, :]
        potential[g * n : (g + 1) * n, :] = -exchange_coef * cube_root(density_values[g]) * weights
    out[...] = jnp.zeros_like(out)
    for copy in copies:
        copy.wait()
    units_own, units_first, units_pair = units_held
    one = units_own[lay.units + 1]
    two = one + units_first[lay.units + 1]
    total = two + units_pair[lay.units + 1]

    def contribute(start, count):
        for u in range(count):
            index = start + u
            word = pick(
                lay, index, ((units_own, 0), (units_first, one), (units_pair, two)), total
            )
            slot, row, (k1, o1), (k2, o2) = decode(lay, word)
            others = jnp.concatenate([orb[o1], orb[o2]], axis=0)
            scale = potential[pl.ds(split(slot, lay.listed)[0], 1), :]
            weighted = (orb[slot].astype(jnp.float32) * scale).astype(jnp.bfloat16)
            contrib = lax.dot_general(
                weighted, others, (((1,), (1,)), ((), ())), preferred_element_type=jnp.float32
            )
            out[row, k1] += contrib[:, : lay.orbitals]
            out[row, k2] += contrib[:, lay.orbitals :]

    over_units(total, contribute)


def on_device(counts, points, weights, block_lists, pattern, basis_table, density):
    batches, listed = block_lists.shape
    rows, partners = pattern.shape
    orbitals = basis_table.shape[2]
    lay = Layout(batches, listed, points.shape[2], rows, partners, orbitals)
    devices = lax.axis_size("space")
    in_vmem = pl.BlockSpec(memory_space=VMEM)
    in_smem = pl.BlockSpec(memory_space=SMEM)
    in_hbm = pl.BlockSpec(memory_space=HBM)
    cost = pl.CostEstimate(flops=10**10, bytes_accessed=0, transcendentals=0)

    def params(limit=LIMIT):
        return pltpu.CompilerParams(vmem_limit_bytes=limit)

    pair_route = [(i, i ^ 1) for i in range(devices)]
    far_route = [
        (i, i + 1 if i % 2 else i - 1)
        for i in range(devices)
        if 0 <= (i + 1 if i % 2 else i - 1) < devices
    ]

    inputs = (counts, points, weights, block_lists.T, pattern.T, basis_table)
    pack = pl.pallas_call(
        functools.partial(pack_kernel, lay),
        out_shape=jax.ShapeDtypeStruct((lay.height, lay.points), jnp.float32),
        in_specs=[in_hbm] * 6,
        out_specs=in_vmem,
        scratch_shapes=[
            [SMEM(counts.shape, counts.dtype)] + [VMEM(x.shape, x.dtype) for x in inputs[1:]],
            pltpu.SemaphoreType.DMA((6,)),
        ],
        compiler_params=params(WHOLE),
        name="pack",
    )(*inputs)
    pack_far = lax.ppermute(pack, "space", far_route)
    pack_pair = lax.ppermute(pack, "space", pair_route)
    pack, density = lax.optimization_barrier((pack, density))
    density_pair = lax.ppermute(density, "space", pair_route)

    orb_shape = jax.ShapeDtypeStruct((lay.slots + 2, orbitals, lay.points), jnp.bfloat16)
    columns_shape = jax.ShapeDtypeStruct((lay.columns, 4, orbitals, 128), jnp.float32)
    anywhere = pl.BlockSpec(memory_space=pl.ANY)
    units_shape = jax.ShapeDtypeStruct((lay.units + 2,), jnp.int32)

    def scratch(groups):
        return [
            VMEM((listed, 128), jnp.int32),
            SMEM((listed, 128), jnp.int32),
            SMEM((groups * batches * listed + PAIRED,), jnp.int32),
            pltpu.SemaphoreType.DMA(()),
        ]

    points_scratch = VMEM((3 * batches, 8, lay.points), jnp.float32)
    orb, columns = pl.pallas_call(
        functools.partial(own_kernel, lay),
        out_shape=(orb_shape, columns_shape),
        in_specs=[in_vmem],
        out_specs=(in_vmem, in_vmem),
        scratch_shapes=[
            points_scratch,
            VMEM((listed, 128), jnp.int32),
            SMEM((batches * listed + PAIRED,), jnp.int32),
        ],
        compiler_params=params(),
        cost_estimate=cost,
        name="first_own",
    )(pack)

    part, orb, columns, units_own, units_first = pl.pallas_call(
        functools.partial(first_kernel, lay),
        out_shape=(
            jax.ShapeDtypeStruct((2 * batches, lay.points), jnp.float32),
            orb_shape,
            columns_shape,
            units_shape,
            units_shape,
        ),
        in_specs=[in_vmem] * 3 + [in_hbm, in_hbm, in_vmem, in_vmem],
        out_specs=(in_vmem, in_vmem, in_vmem, anywhere, anywhere),
        scratch_shapes=[
            points_scratch,
            VMEM((2 * rows, partners, orbitals, orbitals), jnp.bfloat16),
            VMEM((3 * batches + 1, 8, lay.points), jnp.float32),
            *[SMEM(units_shape.shape, jnp.int32)] * 3,
            *scratch(2),
            pltpu.SemaphoreType.DMA((2,)),
            pltpu.SemaphoreType.DMA((2,)),
        ],
        input_output_aliases={5: 1, 6: 2},
        compiler_params=params(BUSY),
        cost_estimate=cost,
        name="first",
    )(pack, pack_pair, pack_far, density, density_pair, orb, columns)

    arrived = lax.ppermute(part, "space", far_route)
    orb, units_pair = pl.pallas_call(
        functools.partial(pair_kernel, lay),
        out_shape=(orb_shape, units_shape),
        in_specs=[in_vmem] * 4,
        out_specs=(in_vmem, in_smem),
        scratch_shapes=[points_scratch, *scratch(1)],
        input_output_aliases={2: 0},
        compiler_params=params(),
        cost_estimate=cost,
        name="first_pair",
    )(pack, pack_pair, orb, columns)
    own_rho = pl.pallas_call(
        functools.partial(total_kernel, lay),
        out_shape=jax.ShapeDtypeStruct((batches, lay.points), jnp.float32),
        in_specs=[in_vmem, in_vmem, anywhere],
        out_specs=in_vmem,
        compiler_params=params(1 << 20),
        name="total",
    )(part, arrived, units_pair)
    pair_rho = lax.ppermute(own_rho, "space", pair_route)

    return pl.pallas_call(
        functools.partial(second_kernel, lay),
        out_shape=jax.ShapeDtypeStruct(density.shape, jnp.float32),
        in_specs=[in_vmem] * 7 + [[anywhere] * 3],
        out_specs=in_vmem,
        scratch_shapes=[
            VMEM((-(-(3 * batches + 1) // 8) * 8, lay.points), jnp.float32),
            [SMEM(units_shape.shape, jnp.int32)] * 3,
            pltpu.SemaphoreType.DMA((3,)),
        ],
        compiler_params=params(),
        name="second",
    )(
        pack,
        pack_pair,
        pack_far,
        part,
        arrived,
        pair_rho,
        orb,
        [units_own, units_first, units_pair],
    )


def solution(mesh):
    in_specs = (
        P(("parts", "space")),
        P(("parts", "space"), None, None),
        P(("parts", "space"), None),
        P(("parts", "space"), None),
        P(("parts", "space"), None),
        P(("parts", "space"), None, None),
        P(("parts", "space"), None, None, None),
    )
    out_specs = P(("parts", "space"), None, None, None)
    return jax.shard_map(
        on_device, mesh=mesh, in_specs=in_specs, out_specs=out_specs, check_vma=False
    )
```
